32 devices in a mesh: wide: 8 (over z, x), narrow: 4 (over y, core).
Axes of the slice: x: 2, y: 2, z: 4, core: 2. Of those that a mesh axis runs over, the one named last changes fastest.
Arguments:
- target_ids: int32 [32, 192], P(('wide', 'narrow')), may hold values from 0 to 250111, as said below
- target_lengths: int32 [32], P(('wide', 'narrow')), may hold values from 1 to 192, 4608 in all
- bucket_table: int32 [192], replicated, may hold values from 0 to 31, as said below
- memory: bfloat16 [32, 1536, 768], P(('wide', 'narrow')), may hold values from -6 to 6
- table: bfloat16 [250112, 768], P(('wide', 'narrow')), may hold values from -6 to 6
- self_qkv: bfloat16 [1769472], P(('wide', 'narrow')), may hold values from -0.21875 to 0.21875
- self_out: bfloat16 [589824], P(('wide', 'narrow')), may hold values from -1.75 to 1.75
- cross_q: bfloat16 [589824], P(('wide', 'narrow')), may hold values from -0.21875 to 0.21875
- cross_kv: bfloat16 [1179648], P(('wide', 'narrow')), may hold values from -0.21875 to 0.21875
- cross_out: bfloat16 [589824], P(('wide', 'narrow')), may hold values from -3.5 to 3.5
- ffn_in: bfloat16 [3145728], P(('wide', 'narrow')), may hold values from -0.21875 to 0.21875
- ffn_out: bfloat16 [1572864], P(('wide', 'narrow')), may hold values from -0.125 to 0.125
- gains: float32 [3, 768], replicated, may hold values from 0.5 to 1.5
- relative_bias: float32 [32, 12], replicated, may hold values from -4 to 4
- cotangent: float32 [32, 192, 768], P(('wide', 'narrow')), may hold values from -6 to 6
Outputs:
- hidden: float32 [32, 192, 768], P(('wide', 'narrow'))
- memory_grad: bfloat16 [32, 1536, 768], P(('wide', 'narrow'))
- table_grad: float32 [250112, 768], P(('wide', 'narrow'))
- self_qkv_grad: float32 [1769472], P(('wide', 'narrow'))
- self_out_grad: float32 [589824], P(('wide', 'narrow'))
- cross_q_grad: float32 [589824], P(('wide', 'narrow'))
- cross_kv_grad: float32 [1179648], P(('wide', 'narrow'))
- cross_out_grad: float32 [589824], P(('wide', 'narrow'))
- ffn_in_grad: float32 [3145728], P(('wide', 'narrow'))
- ffn_out_grad: float32 [1572864], P(('wide', 'narrow'))
- gains_grad: float32 [3, 768], replicated
- bias_grad: float32 [32, 12], replicated
The draws below stay inside these ranges and needn't reach their ends.
Inputs may be any that keep to these rules, and one draw needn't show every extreme that they name: `target_ids`: of the 192 ids of one device's 1 pairs, at most 12 lie in any one block of 7816 table rows (rows c * 7816 to (c + 1) * 7816 - 1); in every draw one such block holds exactly 12 of every device's ids. `target_lengths`: positions at or beyond a pair's length are padding; the lengths of all pairs sum to 4608 and some pair has length 192. `bucket_table`: nondecreasing in the distance, 0 at distance 0 and 31 at distance 192 - 1.
All inputs are finite; a program needn't handle non-finite values. No bound on the sum of `target_lengths` on one device may be relied on, other than what follows from the above.
Results may differ from the reference program's by a relative error of at most 0.02.
Values may be sent and summed in bfloat16 or wider, within the bound.
A program may use at most 256 MiB of HBM per device.

```python
import math
import jax
import jax.numpy as jnp
import numpy as np
from jax import lax

D = 768
H = 12
DH = 64
FF = 2048
VOCAB = 250112
BUCKETS = 32
TLEN = 192
MLEN = 1536
PAIRS_DEV = 1
TOK_DEV = 192
OWNERS = 32
PAIRS = 32
VDEV = 7816
CAP = 12
SLOTS = 384


def draw_target_ids(key, part):
    block_count = PAIRS // PAIRS_DEV
    full_owner = jax.random.randint(jax.random.fold_in(key, 7), (), 0, OWNERS)

    def one_block(index):
        block_key = jax.random.fold_in(key, index + 11)
        key_slots, key_order, key_spread, key_within = jax.random.split(block_key, 4)
        slot_range = jnp.arange(SLOTS, dtype=jnp.int32)
        noise = jax.random.randint(key_slots, (SLOTS,), 0, (1 << 30) // SLOTS)
        ranking = jnp.where(slot_range // CAP == full_owner, slot_range, noise * SLOTS + slot_range + SLOTS)
        chosen = jnp.argsort(ranking)[:TOK_DEV].astype(jnp.int32)
        chosen = jax.random.permutation(key_order, chosen)
        owner_index = chosen // CAP
        spread = jax.random.randint(key_spread, (TOK_DEV,), 1, VDEV + 1)
        raw_value = jax.random.randint(key_within, (TOK_DEV,), 0, 1 << 20)
        return owner_index * VDEV + raw_value % spread
    identity = jax.vmap(one_block)(jnp.arange(block_count, dtype=jnp.int32))
    return identity.reshape(PAIRS, TLEN).astype(jnp.int32)


def draw_bucket_table(key, part):
    raw_value = jax.random.randint(jax.random.fold_in(key, 3), (TLEN,), 0, BUCKETS)
    ordered = jnp.sort(raw_value)
    return ordered.at[0].set(0).at[TLEN - 1].set(BUCKETS - 1).astype(jnp.int32)


def level_of(stream_key, shape, cuts, least, largest):
    def one(dim, blocks):
        draws = jax.random.uniform(jax.random.fold_in(jax.random.fold_in(stream_key, 6), dim), (blocks,), jnp.float32, least / len(cuts), largest / len(cuts))
        return jnp.repeat(jnp.exp(draws), shape[dim] // blocks).reshape((-1,) + (1,) * (len(shape) - dim - 1))

    factor_of = one(*cuts[0])
    for cut in cuts[1:]:
        factor_of = factor_of * one(*cut)
    return factor_of


def split_up(number_of, total, bound, lean):
    weights = [(1 << 20) // math.isqrt(standing ** lean) + 1 for standing in range(2, number_of + 1)]
    spare, given = total - bound - (number_of - 1), [1] * (number_of - 1)
    while spare > 0:
        free = [i for i in range(number_of - 1) if given[i] < bound]
        pool, remaining = sum([weights[i] for i in free]), spare
        for i in free:
            extra = min(bound - given[i], max(1, remaining * weights[i] // pool), spare)
            given[i] = given[i] + extra
            spare = spare - extra
    return np.array([bound] + given)


def ragged(rng, number_of, total, bound, slope):
    if number_of == 2:
        one = jax.random.randint(rng, (), max(1, total - bound), min(bound, total - 1) + 1)
        return jnp.stack([one, total - one])
    lengths = jnp.asarray(split_up(number_of, total, bound, slope), jnp.int32)
    twos = (number_of - 1) // 2
    source_of, sink = lengths[1:1 + 2 * twos:2], lengths[2:2 + 2 * twos:2]
    room = jnp.minimum(source_of - 1, bound - sink)
    passed = jax.random.randint(jax.random.fold_in(rng, 1), (twos,), 0, 1 << 20) % (room + 1)
    lengths = lengths.at[1:1 + 2 * twos:2].set(source_of - passed).at[2:2 + 2 * twos:2].set(sink + passed)
    return lengths[jax.random.permutation(jax.random.fold_in(rng, 2), number_of)]


def normal_values(own_key, dims, width, reach, pieces=(), kind=jnp.bfloat16):
    factor_of = level_of(own_key, dims, pieces, -0.22, 0.18) if pieces else 1.0
    drawn = jax.random.normal(own_key, dims, jnp.float32) * width * factor_of
    return jnp.minimum(jnp.maximum(drawn, -reach), reach).astype(kind)


def setup_inputs(seed: int = 0) -> dict:
    seeds = jax.random.split(jax.random.key(seed), 16)
    target_ids = draw_target_ids(jax.random.fold_in(seeds[15], 71), 0)
    target_lengths = ragged(seeds[1], PAIRS, PAIRS * TLEN * 3 // 4, TLEN, 2).astype(jnp.int32)
    bucket_table = draw_bucket_table(jax.random.fold_in(seeds[15], 71), 0)
    memory = normal_values(seeds[3], (PAIRS, MLEN, D), 1.0, 6.0, ((0, 32),))
    table = normal_values(seeds[4], (VOCAB, D), 1.0, 6.0, ((0, 32),))
    self_qkv = normal_values(seeds[5], (3 * D * D,), D ** -0.5, 0.21875, ((0, 32),))
    self_out = normal_values(seeds[6], (D * D,), (max(1, D // 64)) ** -0.5, 1.75, ((0, 32),))
    cross_q = normal_values(seeds[7], (D * D,), D ** -0.5, 0.21875, ((0, 32),))
    cross_kv = normal_values(seeds[8], (2 * D * D,), D ** -0.5, 0.21875, ((0, 32),))
    cross_out = normal_values(seeds[9], (D * D,), (max(1, D // 256)) ** -0.5, 3.5, ((0, 32),))
    ffn_in = normal_values(seeds[10], (2 * D * FF,), D ** -0.5, 0.21875, ((0, 32),))
    ffn_out = normal_values(seeds[11], (FF * D,), FF ** -0.5, 0.125, ((0, 32),))
    gains = jnp.clip(1.0 + 0.1 * jax.random.normal(seeds[12], (3, D), jnp.float32), 0.5, 1.5)
    relative_bias = normal_values(seeds[13], (BUCKETS, H), 1.0, 4.0, (), jnp.float32)
    cotangent = normal_values(seeds[14], (PAIRS, TLEN, D), 1.0, 6.0, ((0, 32),), jnp.float32)
    return {"target_ids": target_ids, "target_lengths": target_lengths, "bucket_table": bucket_table, "memory": memory, "table": table, "self_qkv": self_qkv, "self_out": self_out, "cross_q": cross_q, "cross_kv": cross_kv, "cross_out": cross_out, "ffn_in": ffn_in, "ffn_out": ffn_out, "gains": gains, "relative_bias": relative_bias, "cotangent": cotangent}


@jax.custom_vjp
def low(v):
    return lax.optimization_barrier(v.astype(jnp.bfloat16)).astype(jnp.float32)

@jax.custom_vjp
def low_back(v):
    return v

def low_keep(v):
    return (low(v), None)

def low_pass(kept, grad):
    return (grad,)

def back_keep(v):
    return (v, None)

def back_low(kept, grad):
    return (low(grad),)
low.defvjp(low_keep, low_pass)
low_back.defvjp(back_keep, back_low)
epsilon = 1e-06
blocked = -1e+30
top_precision = lax.Precision.HIGHEST

def lowboth(value):
    return low_back(low(value))

def product(left, right):
    return jnp.dot(left, right, precision=top_precision)

def rms_scaled(inputs, gain):
    return inputs * lax.rsqrt(lax.optimization_barrier(jnp.mean(inputs * inputs, axis=-1, keepdims=True)) + epsilon) * gain

def reference(target_ids, target_lengths, bucket_table, memory, table, self_qkv, self_out, cross_q, cross_kv, cross_out, ffn_in, ffn_out, gains, relative_bias, cotangent):
    score_scale = DH ** (-0.5)
    positions = jnp.arange(TLEN, dtype=jnp.int32)
    valid_rows = (positions[None, :] < target_lengths[:, None]).astype(jnp.float32)
    distance = jnp.clip(positions[:, None] - positions[None, :], 0, TLEN - 1).astype(jnp.int32)
    bucket_ids = bucket_table[distance]
    allowed = (positions[None, :] <= positions[:, None])[None, :, :] & (valid_rows[:, None, :] > 0.0)
    primals = (table.astype(jnp.float32), memory.astype(jnp.float32), self_qkv.astype(jnp.float32), self_out.astype(jnp.float32), cross_q.astype(jnp.float32), cross_kv.astype(jnp.float32), cross_out.astype(jnp.float32), ffn_in.astype(jnp.float32), ffn_out.astype(jnp.float32), gains, relative_bias)

    def forward(table_full, memory_full, w_qkv, w_out1, w_q2, w_kv2, second_output_weight, w_in, w_out3, gain_rows, bias_table):
        pair_count = target_ids.shape[0]
        embedded = table_full[target_ids] * valid_rows[:, :, None]
        self_normalized = low(rms_scaled(embedded, gain_rows[0]))
        merged_heads = lowboth(product(self_normalized, w_qkv.reshape(D, 3 * D))).reshape(pair_count, TLEN, 3, H, DH)
        expanded_bias = jnp.transpose(bias_table[bucket_ids], (2, 0, 1))

        def self_pair(pair_items):
            queries, keys_all, values_all, key_mask = pair_items
            scores = jnp.einsum('qhd,khd->hqk', queries, keys_all, precision=top_precision)
            scores = low_back(scores * score_scale + expanded_bias)
            scores = jnp.where(key_mask[None], scores, blocked)
            weights = low(jax.nn.softmax(scores, axis=-1))
            blended = jnp.einsum('hqk,khd->qhd', weights, values_all, precision=top_precision)
            return lowboth(blended).reshape(TLEN, D)
        attended = lax.map(jax.checkpoint(self_pair), (merged_heads[:, :, 0], merged_heads[:, :, 1], merged_heads[:, :, 2], allowed))
        after_self = embedded + low_back(product(attended, w_out1.reshape(D, D)))
        normed_cross = low(rms_scaled(after_self, gain_rows[1]))
        cross_queries = lowboth(product(normed_cross, w_q2.reshape(D, D))).reshape(pair_count, TLEN, H, DH)
        kv_matrix = w_kv2.reshape(D, 2 * D)

        def cross_pair(pair_items):
            queries, memory_rows = pair_items
            key_values = lowboth(product(memory_rows, kv_matrix)).reshape(MLEN, 2, H, DH)
            scores = low_back(jnp.einsum('qhd,khd->hqk', queries, key_values[:, 0], precision=top_precision) * score_scale)
            weights = low(jax.nn.softmax(scores, axis=-1))
            blended = jnp.einsum('hqk,khd->qhd', weights, key_values[:, 1], precision=top_precision)
            return lowboth(blended).reshape(TLEN, D)
        cross_mixed = lax.map(jax.checkpoint(cross_pair), (cross_queries, memory_full))
        after_cross = after_self + low_back(product(cross_mixed, second_output_weight.reshape(D, D)))
        normed_ffn = low(rms_scaled(after_cross, gain_rows[2]))
        gate_up = low_back(product(normed_ffn, w_in.reshape(D, 2 * FF)))
        activated = low(jax.nn.gelu(gate_up[..., :FF], approximate=True) * gate_up[..., FF:])
        residual_out = after_cross + low_back(product(activated, w_out3.reshape(FF, D)))
        return residual_out * valid_rows[:, :, None]
    hidden, pullback = jax.vjp(forward, *primals)
    gradients = pullback(cotangent)
    return (hidden, gradients[1].astype(jnp.bfloat16), gradients[0], gradients[2], gradients[3], gradients[4], gradients[5], gradients[6], gradients[7], gradients[8], gradients[9], gradients[10])
```

```python
import functools

import jax
import jax.numpy as jnp
from jax import lax
from jax.experimental import pallas as pl
from jax.experimental.pallas import tpu as pltpu
from jax.sharding import PartitionSpec as P

epsilon = 1e-06
blocked = -1e30
top_precision = lax.Precision.HIGHEST
axes = ("wide", "narrow")
bf16 = jnp.bfloat16
f32 = jnp.float32


def rms_scaled(inputs, gain):
    return inputs * lax.rsqrt(jnp.mean(inputs * inputs, axis=-1, keepdims=True) + epsilon) * gain


def norm_backward(inputs, gain, upstream):
    unused, pullback = jax.vjp(rms_scaled, inputs, gain)
    return pullback(upstream)


def gated(gate, upper):
    return jax.nn.gelu(gate, approximate=True) * upper


def matmul(left, right):
    return jnp.dot(left, right, preferred_element_type=f32)


def outer_sum(left, right):
    return lax.dot_general(left, right, (((0,), (0,)), ((), ())), preferred_element_type=f32)


def back_product(left, right):
    return lax.dot_general(left, right, (((1,), (1,)), ((), ())), preferred_element_type=f32)


mesh_ids = pl.DeviceIdType.MESH
roomy = pltpu.CompilerParams(vmem_limit_bytes=48 * 1024 * 1024)


def standing():
    wide, narrow = lax.axis_index("wide"), lax.axis_index("narrow")
    return wide // 2, wide % 2, narrow // 2, narrow % 2


def device_at(z, x, y, core):
    return (z * 2 + x, y * 2 + core)


def flips(x, y, core):
    far_x, far_y = 1 - x, 1 - y
    second = (x * (1 - core) + far_x * core, far_y * (1 - core) + y * core)
    first = (far_x * (1 - core) + x * core, y * (1 - core) + far_y * core)
    return ((x, y), second, first, (far_x, far_y))


def partners():
    z, x, y, core = standing()
    own, second, first, both = flips(x, y, core)
    along_z = [device_at((z + step) % 4, x, y, core) for step in (1, 2, 3)]
    return along_z, device_at(z, *second, core), device_at(z, *first, core), device_at(z, x, y, 1 - core)


def greet(devices):
    barrier = pltpu.get_barrier_semaphore()
    for device in devices:
        pl.semaphore_signal(barrier, inc=1, device_id=device, device_id_type=mesh_ids)
    pl.semaphore_wait(barrier, len(devices))


def remote(source, target, send_sem, recv_sem, index, device):
    return pltpu.make_async_remote_copy(
        src_ref=source,
        dst_ref=target,
        send_sem=send_sem.at[index],
        recv_sem=recv_sem.at[index],
        device_id=device,
        device_id_type=mesh_ids,
    )


def gather_kernel(count, *refs):
    shards, outs = refs[:count], refs[count:2 * count]
    send_sem, recv_sem, own_sem = refs[2 * count:]
    z, x, y, core = standing()
    sets = flips(x, y, core)
    along_z, second, first, sibling = partners()
    greet(along_z + [second, first, sibling])
    own_copies = []
    for chunk in range(count):
        own = pltpu.make_async_copy(
            shards[chunk], outs[chunk].at[z, x, y, core], own_sem.at[chunk]
        )
        own.start()
        own_copies.append(own)

    def stage(number, chunk):
        base = chunk * 10
        out = outs[chunk]
        if number == 0:
            return [
                remote(shards[chunk], out.at[z, x, y, core], send_sem, recv_sem, base + k, device)
                for k, device in enumerate(along_z)
            ]
        piece = lambda k: out.at[:, sets[k][0], sets[k][1], core]
        copies = []
        device = (second, first, sibling)[number - 1]
        amount = (1, 2, 4)[number - 1]
        for k in range(amount):
            copies.append(
                remote(piece(k), piece(k), send_sem, recv_sem, base + 2 + amount + k, device)
            )
        return copies

    flying = {}
    for step in range(count + 4):
        for number in (3, 2, 1, 0):
            chunk = step - number
            if 0 <= chunk < count:
                if number == 1:
                    own_copies[chunk].wait()
                if number > 0:
                    for copy in flying[number - 1, chunk]:
                        copy.wait_recv()
                flying[number, chunk] = stage(number, chunk)
                for copy in flying[number, chunk]:
                    copy.start()
        chunk = step - 4
        if chunk >= 0:
            for copy in flying[3, chunk]:
                copy.wait_recv()
    for copies in flying.values():
        for copy in copies:
            copy.wait_send()


def gather_weights(shards, special):
    if not special:
        return [lax.all_gather(shard, axes, axis=0, tiled=True) for shard in shards]
    count = len(shards)
    outs = pl.pallas_call(
        functools.partial(gather_kernel, count),
        out_shape=[jax.ShapeDtypeStruct((4, 2, 2, 2) + shard.shape, bf16) for shard in shards],
        in_specs=[pl.BlockSpec(memory_space=pltpu.VMEM)] * count,
        out_specs=[pl.BlockSpec(memory_space=pl.ANY)] * count,
        scratch_shapes=[
            pltpu.SemaphoreType.DMA((10 * count,)),
            pltpu.SemaphoreType.DMA((10 * count,)),
            pltpu.SemaphoreType.DMA((count,)),
        ],
        compiler_params=pltpu.CompilerParams(
            collective_id=1, has_side_effects=True, vmem_limit_bytes=48 * 1024 * 1024
        ),
    )(*shards)
    return [out.reshape(-1, out.shape[-1]) for out in outs]


def add_into(target, source):
    def quarter(index, unused):
        target[index] = (target[index].astype(f32) + source[index].astype(f32)).astype(bf16)
        return unused

    lax.fori_loop(0, 4, quarter, 0)


def reduce_kernel(count, *refs):
    grads, small = refs[:count], refs[count]
    outs, small_out = refs[count + 1:2 * count + 1], refs[2 * count + 1]
    scratch = refs[2 * count + 2:]
    kept, from_core, from_first, from_second, from_z = [
        scratch[k * count:(k + 1) * count] for k in range(5)
    ]
    small_in, send_sem, recv_sem, load_sem, small_send, small_recv = scratch[5 * count:]
    z, x, y, core = standing()
    sets = flips(x, y, core)
    sibling_sets = flips(x, y, 1 - core)
    along_z, second, first, sibling = partners()
    greet(along_z + [second, first, sibling])
    small_out[...] = small[...]

    loads = {}

    def stage(number, chunk):
        base = chunk * 10
        if number == 0:
            loads[chunk] = [
                pltpu.make_async_copy(
                    grads[chunk].at[:, sets[k][0], sets[k][1], core],
                    kept[chunk].at[k],
                    load_sem.at[4 * chunk + k],
                )
                for k in range(4)
            ]
            return [
                remote(
                    grads[chunk].at[:, sibling_sets[k][0], sibling_sets[k][1], 1 - core],
                    from_core[chunk].at[k],
                    send_sem,
                    recv_sem,
                    base + k,
                    sibling,
                )
                for k in range(4)
            ]
        if number == 1:
            return [
                remote(
                    kept[chunk].at[2 + k],
                    from_first[chunk].at[k],
                    send_sem,
                    recv_sem,
                    base + 4 + k,
                    first,
                )
                for k in range(2)
            ]
        if number == 2:
            return [
                remote(kept[chunk].at[1], from_second[chunk], send_sem, recv_sem, base + 6, second)
            ]
        return [
            remote(
                kept[chunk].at[0, (z + k + 1) % 4],
                from_z[chunk].at[k],
                send_sem,
                recv_sem,
                base + 7 + k,
                along_z[k],
            )
            for k in range(3)
        ]

    def settle(number, chunk):
        for copy in flying[number, chunk]:
            copy.wait_recv()
        if number == 0:
            for load in loads[chunk]:
                load.wait()
            for k in (2, 3, 1, 0):
                add_into(kept[chunk].at[k], from_core[chunk].at[k])
        elif number == 1:
            for k in (1, 0):
                add_into(kept[chunk].at[k], from_first[chunk].at[k])
        elif number == 2:
            add_into(kept[chunk].at[0], from_second[chunk])
        else:
            total = kept[chunk][0, z].astype(f32)
            for k in range(3):
                total = total + from_z[chunk][k].astype(f32)
            outs[chunk][...] = total

    flying = {}
    for step in range(count + 4):
        for number in (4, 3, 2, 1, 0):
            chunk = step - number
            if 0 <= chunk < count:
                if number > 0:
                    settle(number - 1, chunk)
                if number < 4:
                    flying[number, chunk] = stage(number, chunk)
                    for copy in flying[number, chunk] + (loads[chunk] if number == 0 else []):
                        copy.start()
        if step == 0:
            number = 0
            for group in ([sibling], [first], [second], along_z):
                copies = []
                for device in group:
                    copies.append(
                        remote(small_out, small_in.at[number], small_send, small_recv, number, device)
                    )
                    number += 1
                for copy in copies:
                    copy.start()
                for copy in copies:
                    copy.wait()
                total = small_out[...]
                for index in range(number - len(group), number):
                    total = total + small_in[index]
                small_out[...] = total
    for copies in flying.values():
        for copy in copies:
            copy.wait_send()


def reduce_grads(grads, small, special):
    if not special:
        sums = [lax.psum_scatter(grad, axes, scatter_dimension=0, tiled=True) for grad in grads]
        return [total.astype(f32) for total in sums], lax.psum(small, axes)
    count = len(grads)
    grads = [grad.reshape(4, 2, 2, 2, -1, grad.shape[-1]) for grad in grads]
    shapes = [grad.shape[4:] for grad in grads]
    several = lambda *lead: [pltpu.VMEM(lead + shape, bf16) for shape in shapes]
    results = pl.pallas_call(
        functools.partial(reduce_kernel, count),
        out_shape=[jax.ShapeDtypeStruct(shape, f32) for shape in shapes]
        + [jax.ShapeDtypeStruct(small.shape, f32)],
        in_specs=[pl.BlockSpec(memory_space=pl.ANY)] * count
        + [pl.BlockSpec(memory_space=pltpu.VMEM)],
        out_specs=[pl.BlockSpec(memory_space=pltpu.VMEM)] * (count + 1),
        scratch_shapes=several(4, 4)
        + several(4, 4)
        + several(2, 4)
        + several(4)
        + several(3)
        + [
            pltpu.VMEM((6,) + small.shape, f32),
            pltpu.SemaphoreType.DMA((10 * count,)),
            pltpu.SemaphoreType.DMA((10 * count,)),
            pltpu.SemaphoreType.DMA((4 * count,)),
            pltpu.SemaphoreType.DMA((6,)),
            pltpu.SemaphoreType.DMA((6,)),
        ],
        compiler_params=pltpu.CompilerParams(
            collective_id=2, has_side_effects=True, vmem_limit_bytes=60 * 1024 * 1024
        ),
    )(*grads, small)
    return results[:count], results[count]


def spread_heads(pair, head_size):
    lane = lax.broadcasted_iota(jnp.int32, pair.shape, 1)
    zero = jnp.zeros_like(pair)
    return jnp.concatenate(
        [jnp.where(lane < head_size, pair, zero), jnp.where(lane >= head_size, pair, zero)], axis=0
    )


def join_heads(spread, head_size):
    turned = spread.T
    rows = turned.shape[0] // 2
    lane = lax.broadcasted_iota(jnp.int32, (rows, turned.shape[1]), 1)
    return jnp.where(lane < head_size, turned[:rows], turned[rows:])


def down_product(left, right):
    return lax.dot_general(left, right, (((0,), (0,)), ((), ())), preferred_element_type=f32)


def column_softmax(scores):
    peak = jnp.max(scores, axis=0, keepdims=True)
    exponent = jnp.exp(scores - peak)
    return exponent / jnp.sum(exponent, axis=0, keepdims=True)


def self_forward_kernel(head_size, q_ref, k_ref, v_ref, bias_ref, keep_ref, out_ref, prob_ref):
    scale = head_size ** (-0.5)
    scores = back_product(k_ref[...], spread_heads(q_ref[...], head_size)) * scale
    length, both = scores.shape
    row = lax.broadcasted_iota(jnp.int32, scores.shape, 0)
    lane = lax.broadcasted_iota(jnp.int32, scores.shape, 1)
    query = jnp.where(lane >= length, lane - length, lane)
    bias = pltpu.roll(
        jnp.broadcast_to(bias_ref[0], scores.shape), 0, 1, stride=1, stride_axis=0
    )
    scores = jnp.where((row <= query) & (keep_ref[...] > 0.0), scores + bias, blocked)
    probs = column_softmax(scores).astype(bf16)
    prob_ref[0] = probs
    out_ref[...] = join_heads(down_product(v_ref[...], probs), head_size).astype(bf16)


def self_backward_kernel(
    head_size, q_ref, k_ref, v_ref, prob_ref, grad_ref, out_ref, bias_ref
):
    scale = head_size ** (-0.5)
    pair = pl.program_id(0)
    width = 2 * head_size
    model = out_ref.shape[1] // 3
    grad = spread_heads(grad_ref[...], head_size)
    probs = prob_ref[0]
    wide_probs = probs.astype(f32)
    grad_probs = back_product(v_ref[...], grad)
    center = jnp.sum(grad_probs * wide_probs, axis=0, keepdims=True)
    grad_scores = (wide_probs * (grad_probs - center)).astype(bf16)
    grad_value = matmul(probs, grad)
    grad_key = matmul(grad_scores, spread_heads(q_ref[...], head_size)) * scale
    grad_query = join_heads(down_product(k_ref[...], grad_scores), head_size) * scale
    out_ref[:, pl.ds(pl.multiple_of(pair * width, width), width)] = grad_query.astype(bf16)
    out_ref[:, pl.ds(pl.multiple_of(model + pair * width, width), width)] = grad_key.astype(bf16)
    out_ref[:, pl.ds(pl.multiple_of(2 * model + pair * width, width), width)] = grad_value.astype(
        bf16
    )
    folded = grad_scores.astype(f32)
    both = folded.shape[1]
    while folded.shape[0] % 16 == 0:
        rows = folded.shape[0] // 2
        folded = folded[:rows] + pltpu.roll(folded[rows:], both - rows, 1)
    total = folded[:8]
    for start in range(8, folded.shape[0], 8):
        total = total + pltpu.roll(folded[start:start + 8], both - start, 1)
    row = lax.broadcasted_iota(jnp.int32, total.shape, 0)
    for bit in (1, 2, 4):
        total = jnp.where((row // bit) % 2 == 1, pltpu.roll(total, both - bit, 1), total)
    bias_ref[0] = jnp.sum(total, axis=0, keepdims=True)


def cross_forward_kernel(head_size, q_ref, k_ref, v_ref, out_ref, prob_ref):
    scale = head_size ** (-0.5)
    scores = back_product(k_ref[...], spread_heads(q_ref[...], head_size)) * scale
    probs = column_softmax(scores).astype(bf16)
    prob_ref[0] = probs
    out_ref[...] = join_heads(down_product(v_ref[...], probs), head_size).astype(bf16)


def cross_backward_kernel(head_size, q_ref, k_ref, v_ref, prob_ref, grad_ref, out_ref, kv_ref):
    scale = head_size ** (-0.5)
    pair = pl.program_id(0)
    width = 2 * head_size
    model = kv_ref.shape[1] // 2
    grad = spread_heads(grad_ref[...], head_size)
    probs = prob_ref[0]
    wide_probs = probs.astype(f32)
    grad_probs = back_product(v_ref[...], grad)
    center = jnp.sum(grad_probs * wide_probs, axis=0, keepdims=True)
    grad_scores = (wide_probs * (grad_probs - center)).astype(bf16)
    grad_value = matmul(probs, grad)
    grad_key = matmul(grad_scores, spread_heads(q_ref[...], head_size)) * scale
    grad_query = join_heads(down_product(k_ref[...], grad_scores), head_size) * scale
    out_ref[...] = grad_query.astype(bf16)
    kv_ref[:, pl.ds(pl.multiple_of(pair * width, width), width)] = grad_key.astype(bf16)
    kv_ref[:, pl.ds(pl.multiple_of(model + pair * width, width), width)] = grad_value.astype(bf16)


def self_forward(merged, bias_rows, keep_rows, head_size):
    length, model = merged.shape[0], merged.shape[1] // 3
    width, pairs = 2 * head_size, model // (2 * head_size)
    both = 2 * length
    part = lambda offset: pl.BlockSpec((length, width), lambda p: (0, p + offset))
    return pl.pallas_call(
        functools.partial(self_forward_kernel, head_size),
        grid=(pairs,),
        out_shape=(
            jax.ShapeDtypeStruct((length, model), bf16),
            jax.ShapeDtypeStruct((pairs, length, both), bf16),
        ),
        in_specs=[
            part(0),
            part(pairs),
            part(2 * pairs),
            pl.BlockSpec((1, 1, both), lambda p: (p, 0, 0)),
            pl.BlockSpec((length, 1), lambda p: (0, 0)),
        ],
        out_specs=(part(0), pl.BlockSpec((1, length, both), lambda p: (p, 0, 0))),
        compiler_params=roomy,
        cost_estimate=pl.CostEstimate(flops=10**9, bytes_accessed=4 * 10**6, transcendentals=10**6),
    )(merged, merged, merged, bias_rows, keep_rows)


def self_backward(merged, probs, grad, head_size):
    length, model = grad.shape
    width, pairs = 2 * head_size, model // (2 * head_size)
    both = 2 * length
    part = lambda offset: pl.BlockSpec((length, width), lambda p: (0, p + offset))
    return pl.pallas_call(
        functools.partial(self_backward_kernel, head_size),
        grid=(pairs,),
        out_shape=(
            jax.ShapeDtypeStruct((length, 3 * model), bf16),
            jax.ShapeDtypeStruct((pairs, 1, both), f32),
        ),
        in_specs=[
            part(0),
            part(pairs),
            part(2 * pairs),
            pl.BlockSpec((1, length, both), lambda p: (p, 0, 0)),
            part(0),
        ],
        out_specs=(
            pl.BlockSpec((length, 3 * model), lambda p: (0, 0)),
            pl.BlockSpec((1, 1, both), lambda p: (p, 0, 0)),
        ),
        compiler_params=roomy,
        cost_estimate=pl.CostEstimate(flops=10**9, bytes_accessed=4 * 10**6, transcendentals=0),
    )(merged, merged, merged, probs, grad)


def cross_forward(queries, key_values, head_size):
    length, model = queries.shape
    memory_len = key_values.shape[0]
    width, pairs = 2 * head_size, model // (2 * head_size)
    both = 2 * length
    part = pl.BlockSpec((length, width), lambda p: (0, p))
    long_part = lambda offset: pl.BlockSpec((memory_len, width), lambda p: (0, p + offset))
    return pl.pallas_call(
        functools.partial(cross_forward_kernel, head_size),
        grid=(pairs,),
        out_shape=(
            jax.ShapeDtypeStruct((length, model), bf16),
            jax.ShapeDtypeStruct((pairs, memory_len, both), bf16),
        ),
        in_specs=[part, long_part(0), long_part(pairs)],
        out_specs=(part, pl.BlockSpec((1, memory_len, both), lambda p: (p, 0, 0))),
        compiler_params=roomy,
        cost_estimate=pl.CostEstimate(
            flops=4 * 10**9, bytes_accessed=13 * 10**6, transcendentals=4 * 10**6
        ),
    )(queries, key_values, key_values)


def cross_backward(queries, key_values, probs, grad, head_size):
    length, model = queries.shape
    memory_len = key_values.shape[0]
    width, pairs = 2 * head_size, model // (2 * head_size)
    both = 2 * length
    part = pl.BlockSpec((length, width), lambda p: (0, p))
    long_part = lambda offset: pl.BlockSpec((memory_len, width), lambda p: (0, p + offset))
    return pl.pallas_call(
        functools.partial(cross_backward_kernel, head_size),
        grid=(pairs,),
        out_shape=(
            jax.ShapeDtypeStruct((length, model), bf16),
            jax.ShapeDtypeStruct((memory_len, 2 * model), bf16),
        ),
        in_specs=[
            part,
            long_part(0),
            long_part(pairs),
            pl.BlockSpec((1, memory_len, both), lambda p: (p, 0, 0)),
            part,
        ],
        out_specs=(part, pl.BlockSpec((memory_len, 2 * model), lambda p: (0, 0))),
        compiler_params=roomy,
        cost_estimate=pl.CostEstimate(
            flops=8 * 10**9, bytes_accessed=18 * 10**6, transcendentals=0
        ),
    )(queries, key_values, key_values, probs, grad)


def body(
    target_ids,
    target_lengths,
    bucket_table,
    memory,
    table,
    self_qkv,
    self_out,
    cross_q,
    cross_kv,
    cross_out,
    ffn_in,
    ffn_out,
    gains,
    relative_bias,
    cotangent,
):
    pair_count, seq_len = target_ids.shape
    model_width = table.shape[1]
    bucket_count, head_count = relative_bias.shape
    head_size = model_width // head_count
    memory_len = memory.shape[1]
    wide_count = lax.axis_size("wide")
    narrow_count = lax.axis_size("narrow")
    owner_count = wide_count * narrow_count
    special = wide_count == 8 and narrow_count == 4
    ffn_width = ffn_out.shape[0] * owner_count // model_width
    token_count = pair_count * seq_len
    shard_rows = table.shape[0]
    capacity = max(2, (2 * token_count + owner_count - 1) // owner_count)
    slots = owner_count * capacity

    shards = [
        cross_kv.reshape(-1, 2 * model_width),
        self_qkv.reshape(-1, 3 * model_width),
        self_out.reshape(-1, model_width),
        cross_q.reshape(-1, model_width),
        cross_out.reshape(-1, model_width),
        *jnp.split(ffn_in.reshape(-1, 2 * ffn_width), 2, axis=1),
        ffn_out.reshape(-1, model_width),
    ]
    w_kv2, w_qkv, w_out1, w_q2, w_out2, w_gate, w_upper, w_out3 = gather_weights(shards, special)

    positions = jnp.arange(seq_len, dtype=jnp.int32)
    valid_flat = (positions[:, None] < target_lengths[0]).astype(f32)
    bucket_hits = (
        bucket_table[:, None] == jnp.arange(bucket_count, dtype=jnp.int32)[None, :]
    ).astype(f32)
    bias_rows = jnp.dot(relative_bias.T, bucket_hits.T, precision=top_precision).reshape(
        head_count // 2, 1, 2 * seq_len
    )

    flat_ids = target_ids.reshape(token_count)
    owner_index = flat_ids // shard_rows
    owner_hits = (owner_index[:, None] == jnp.arange(owner_count, dtype=jnp.int32)[None, :]).astype(
        jnp.int32
    )
    rank_within = jnp.sum(jnp.cumsum(owner_hits, axis=0) * owner_hits, axis=1) - 1
    slot_index = owner_index * capacity + rank_within
    slot_hits = slot_index[:, None] == jnp.arange(slots, dtype=jnp.int32)[None, :]
    outgoing = (
        jnp.sum(
            jnp.where(slot_hits, (flat_ids - owner_index * shard_rows + 1)[:, None], 0), axis=0
        )
        - 1
    )
    requests = lax.all_to_all(
        lax.all_to_all(
            outgoing.reshape(wide_count, narrow_count, capacity),
            "wide",
            split_axis=0,
            concat_axis=0,
            tiled=True,
        ),
        "narrow",
        split_axis=1,
        concat_axis=1,
        tiled=True,
    )
    found = table[jnp.maximum(requests, 0)]
    arrived = lax.all_to_all(
        lax.all_to_all(found, "wide", split_axis=0, concat_axis=0, tiled=True),
        "narrow",
        split_axis=1,
        concat_axis=1,
        tiled=True,
    ).reshape(slots, model_width)
    slot_pick = (slot_hits & (valid_flat > 0.0)).astype(bf16)
    embedded = matmul(slot_pick, arrived)

    memory_rows = memory.reshape(memory_len, model_width)
    key_values = matmul(memory_rows, w_kv2).astype(bf16)

    self_normalized = rms_scaled(embedded, gains[0]).astype(bf16)
    merged = matmul(self_normalized, w_qkv).astype(bf16)
    self_mixed, self_probs = self_forward(merged, bias_rows, valid_flat, head_size)
    after_self = embedded + matmul(self_mixed, w_out1)
    normed_cross = rms_scaled(after_self, gains[1]).astype(bf16)
    cross_queries = matmul(normed_cross, w_q2).astype(bf16)
    cross_mixed, cross_probs = cross_forward(cross_queries, key_values, head_size)
    after_cross = after_self + matmul(cross_mixed, w_out2)
    normed_ffn = rms_scaled(after_cross, gains[2]).astype(bf16)
    gate, upper = matmul(normed_ffn, w_gate), matmul(normed_ffn, w_upper)
    activated = gated(gate, upper).astype(bf16)
    hidden = (after_cross + matmul(activated, w_out3)) * valid_flat

    upstream = cotangent.reshape(token_count, model_width) * valid_flat
    grad_branch3 = upstream.astype(bf16)
    share_out3 = outer_sum(activated, grad_branch3).astype(bf16)
    grad_act = back_product(grad_branch3, w_out3)
    unused, gate_pull = jax.vjp(gated, gate, upper)
    grad_gate, grad_upper = [part.astype(bf16) for part in gate_pull(grad_act)]
    share_gate = outer_sum(normed_ffn, grad_gate).astype(bf16)
    share_upper = outer_sum(normed_ffn, grad_upper).astype(bf16)
    grad_normed3 = back_product(grad_gate, w_gate) + back_product(grad_upper, w_upper)
    grad_cross_state, grad_gain3 = norm_backward(after_cross, gains[2], grad_normed3)
    grad_cross_state = grad_cross_state + upstream

    grad_branch2 = grad_cross_state.astype(bf16)
    share_out2 = outer_sum(cross_mixed, grad_branch2).astype(bf16)
    grad_cross_mixed = back_product(grad_branch2, w_out2).astype(bf16)
    grad_cross_q, grad_kv = cross_backward(
        cross_queries, key_values, cross_probs, grad_cross_mixed, head_size
    )
    share_kv2 = outer_sum(memory_rows, grad_kv).astype(bf16)
    share_q2 = outer_sum(normed_cross, grad_cross_q).astype(bf16)
    grad_normed2 = back_product(grad_cross_q, w_q2)
    grad_self_state, grad_gain2 = norm_backward(after_self, gains[1], grad_normed2)
    grad_self_state = grad_self_state + grad_cross_state

    grad_branch1 = grad_self_state.astype(bf16)
    share_out1 = outer_sum(self_mixed, grad_branch1).astype(bf16)
    grad_self_mixed = back_product(grad_branch1, w_out1).astype(bf16)
    grad_joined, grad_distance = self_backward(merged, self_probs, grad_self_mixed, head_size)
    share_qkv = outer_sum(self_normalized, grad_joined).astype(bf16)
    grad_bias = jnp.dot(
        bucket_hits.T, grad_distance.reshape(head_count, seq_len).T, precision=top_precision
    )
    grad_first_normalized = back_product(grad_joined, w_qkv)
    grad_embedded, grad_gain1 = norm_backward(embedded, gains[0], grad_first_normalized)
    row_grads = (grad_embedded + grad_self_state).astype(bf16)
    slot_grads = outer_sum(slot_pick, row_grads).astype(bf16)
    returned = lax.all_to_all(
        lax.all_to_all(
            slot_grads.reshape(wide_count, narrow_count, capacity, model_width),
            "wide",
            split_axis=0,
            concat_axis=0,
            tiled=True,
        ),
        "narrow",
        split_axis=1,
        concat_axis=1,
        tiled=True,
    ).reshape(slots, model_width)
    row_hits = (
        jnp.arange(shard_rows, dtype=jnp.int32)[:, None] == requests.reshape(1, slots)
    ).astype(bf16)
    table_grad = matmul(row_hits, returned)
    memory_grad = back_product(grad_kv, w_kv2).astype(bf16)

    small = jnp.concatenate(
        [grad_gain1, grad_gain2, grad_gain3, grad_bias.reshape(-1)]
    )
    small_rows = -(-small.shape[0] // 1024) * 8
    small = jnp.pad(small, (0, small_rows * 128 - small.shape[0])).reshape(small_rows, 128)
    sums, small_sum = reduce_grads(
        [
            share_out3,
            share_gate,
            share_upper,
            share_kv2,
            share_out2,
            share_q2,
            share_out1,
            share_qkv,
        ],
        small,
        special,
    )
    sum_out3, sum_gate, sum_upper, sum_kv2, sum_out2, sum_q2, sum_out1, sum_qkv = sums
    small_sum = small_sum.reshape(-1)
    gain_count = 3 * model_width
    return (
        hidden.reshape(pair_count, seq_len, model_width),
        memory_grad.reshape(pair_count, memory_len, model_width),
        table_grad,
        sum_qkv.reshape(-1),
        sum_out1.reshape(-1),
        sum_q2.reshape(-1),
        sum_kv2.reshape(-1),
        sum_out2.reshape(-1),
        jnp.concatenate([sum_gate, sum_upper], axis=1).reshape(-1),
        sum_out3.reshape(-1),
        small_sum[:gain_count].reshape(3, model_width),
        small_sum[gain_count:gain_count + bucket_count * head_count].reshape(
            bucket_count, head_count
        ),
    )


def solution(mesh):
    split = P(axes)
    return jax.shard_map(
        body,
        mesh=mesh,
        in_specs=(
            P(axes, None),
            split,
            P(),
            P(axes, None, None),
            P(axes, None),
            split,
            split,
            split,
            split,
            split,
            split,
            split,
            P(),
            P(),
            P(axes, None, None),
        ),
        out_specs=(
            P(axes, None, None),
            P(axes, None, None),
            P(axes, None),
            split,
            split,
            split,
            split,
            split,
            split,
            split,
            P(),
            P(),
        ),
        check_vma=False,
    )
```

```python
import functools
from typing import NamedTuple

import jax
import jax.numpy as jnp
from jax import lax
from jax.experimental import pallas as pl
from jax.experimental.pallas import tpu as pltpu
from jax.sharding import PartitionSpec as P

epsilon = 1e-06
blocked = -1e30
top_precision = lax.Precision.HIGHEST
axes = ("wide", "narrow")
bf16 = jnp.bfloat16
f32 = jnp.float32


def rms_scaled(inputs, gain):
    return inputs * lax.rsqrt(jnp.mean(inputs * inputs, axis=-1, keepdims=True) + epsilon) * gain


def norm_backward(inputs, gain, upstream):
    unused, pullback = jax.vjp(rms_scaled, inputs, gain)
    return pullback(upstream)


def gated(gate, upper):
    return jax.nn.gelu(gate, approximate=True) * upper


def matmul(left, right):
    return jnp.dot(left, right, preferred_element_type=f32)


def outer_sum(left, right):
    return lax.dot_general(left, right, (((0,), (0,)), ((), ())), preferred_element_type=f32)


def back_product(left, right):
    return lax.dot_general(left, right, (((1,), (1,)), ((), ())), preferred_element_type=f32)


mesh_ids = pl.DeviceIdType.MESH
roomy = pltpu.CompilerParams(vmem_limit_bytes=48 * 1024 * 1024)


def standing():
    wide, narrow = lax.axis_index("wide"), lax.axis_index("narrow")
    return wide // 2, wide % 2, narrow // 2, narrow % 2


def device_at(z, x, y, core):
    return (z * 2 + x, y * 2 + core)


def flips(x, y, core):
    far_x, far_y = 1 - x, 1 - y
    second = (x * (1 - core) + far_x * core, far_y * (1 - core) + y * core)
    first = (far_x * (1 - core) + x * core, y * (1 - core) + far_y * core)
    return ((x, y), second, first, (far_x, far_y))


def partners():
    z, x, y, core = standing()
    own, second, first, both = flips(x, y, core)
    along_z = [device_at((z + step) % 4, x, y, core) for step in (1, 2, 3)]
    return along_z, device_at(z, *second, core), device_at(z, *first, core), device_at(z, x, y, 1 - core)


def greet(devices):
    barrier = pltpu.get_barrier_semaphore()
    for device in devices:
        pl.semaphore_signal(barrier, inc=1, device_id=device, device_id_type=mesh_ids)
    pl.semaphore_wait(barrier, len(devices))


def remote(source, target, send_sem, recv_sem, index, device):
    return pltpu.make_async_remote_copy(
        src_ref=source,
        dst_ref=target,
        send_sem=send_sem.at[index],
        recv_sem=recv_sem.at[index],
        device_id=device,
        device_id_type=mesh_ids,
    )


def spread_heads(pair, head_size):
    lane = lax.broadcasted_iota(jnp.int32, pair.shape, 1)
    zero = jnp.zeros_like(pair)
    return jnp.concatenate(
        [jnp.where(lane < head_size, pair, zero), jnp.where(lane >= head_size, pair, zero)], axis=0
    )


def join_heads(spread, head_size):
    turned = spread.T
    rows = turned.shape[0] // 2
    lane = lax.broadcasted_iota(jnp.int32, (rows, turned.shape[1]), 1)
    return jnp.where(lane < head_size, turned[:rows], turned[rows:])


def down_product(left, right):
    return lax.dot_general(left, right, (((0,), (0,)), ((), ())), preferred_element_type=f32)


def column_softmax(scores):
    peak = jnp.max(scores, axis=0, keepdims=True)
    exponent = jnp.exp(scores - peak)
    return exponent / jnp.sum(exponent, axis=0, keepdims=True)


def self_forward_kernel(head_size, q_ref, k_ref, v_ref, bias_ref, keep_ref, out_ref, prob_ref):
    scale = head_size ** (-0.5)
    scores = back_product(k_ref[...], spread_heads(q_ref[...], head_size)) * scale
    length, both = scores.shape
    row = lax.broadcasted_iota(jnp.int32, scores.shape, 0)
    lane = lax.broadcasted_iota(jnp.int32, scores.shape, 1)
    query = jnp.where(lane >= length, lane - length, lane)
    bias = pltpu.roll(
        jnp.broadcast_to(bias_ref[0], scores.shape), 0, 1, stride=1, stride_axis=0
    )
    scores = jnp.where((row <= query) & (keep_ref[...] > 0.0), scores + bias, blocked)
    probs = column_softmax(scores).astype(bf16)
    prob_ref[0] = probs
    out_ref[...] = join_heads(down_product(v_ref[...], probs), head_size).astype(bf16)


def self_backward_kernel(
    head_size, q_ref, k_ref, v_ref, prob_ref, grad_ref, out_ref, bias_ref
):
    scale = head_size ** (-0.5)
    pair = pl.program_id(0)
    width = 2 * head_size
    model = out_ref.shape[1] // 3
    grad = spread_heads(grad_ref[...], head_size)
    probs = prob_ref[0]
    wide_probs = probs.astype(f32)
    grad_probs = back_product(v_ref[...], grad)
    center = jnp.sum(grad_probs * wide_probs, axis=0, keepdims=True)
    grad_scores = (wide_probs * (grad_probs - center)).astype(bf16)
    grad_value = matmul(probs, grad)
    grad_key = matmul(grad_scores, spread_heads(q_ref[...], head_size)) * scale
    grad_query = join_heads(down_product(k_ref[...], grad_scores), head_size) * scale
    out_ref[:, pl.ds(pl.multiple_of(pair * width, width), width)] = grad_query.astype(bf16)
    out_ref[:, pl.ds(pl.multiple_of(model + pair * width, width), width)] = grad_key.astype(bf16)
    out_ref[:, pl.ds(pl.multiple_of(2 * model + pair * width, width), width)] = grad_value.astype(
        bf16
    )
    bias_ref[0] = fold_rows(grad_scores.astype(f32))


def cross_forward_kernel(head_size, q_ref, k_ref, v_ref, out_ref, prob_ref):
    scale = head_size ** (-0.5)
    scores = back_product(k_ref[...], spread_heads(q_ref[...], head_size)) * scale
    probs = column_softmax(scores).astype(bf16)
    prob_ref[0] = probs
    out_ref[...] = join_heads(down_product(v_ref[...], probs), head_size).astype(bf16)


def cross_backward_kernel(head_size, q_ref, k_ref, v_ref, prob_ref, grad_ref, out_ref, kv_ref):
    scale = head_size ** (-0.5)
    pair = pl.program_id(0)
    width = 2 * head_size
    model = kv_ref.shape[1] // 2
    grad = spread_heads(grad_ref[...], head_size)
    probs = prob_ref[0]
    wide_probs = probs.astype(f32)
    grad_probs = back_product(v_ref[...], grad)
    center = jnp.sum(grad_probs * wide_probs, axis=0, keepdims=True)
    grad_scores = (wide_probs * (grad_probs - center)).astype(bf16)
    grad_value = matmul(probs, grad)
    grad_key = matmul(grad_scores, spread_heads(q_ref[...], head_size)) * scale
    grad_query = join_heads(down_product(k_ref[...], grad_scores), head_size) * scale
    out_ref[...] = grad_query.astype(bf16)
    kv_ref[:, pl.ds(pl.multiple_of(pair * width, width), width)] = grad_key.astype(bf16)
    kv_ref[:, pl.ds(pl.multiple_of(model + pair * width, width), width)] = grad_value.astype(bf16)


def self_forward(merged, bias_rows, keep_rows, head_size):
    length, model = merged.shape[0], merged.shape[1] // 3
    width, pairs = 2 * head_size, model // (2 * head_size)
    both = 2 * length
    part = lambda offset: pl.BlockSpec((length, width), lambda p: (0, p + offset))
    return pl.pallas_call(
        functools.partial(self_forward_kernel, head_size),
        grid=(pairs,),
        out_shape=(
            jax.ShapeDtypeStruct((length, model), bf16),
            jax.ShapeDtypeStruct((pairs, length, both), bf16),
        ),
        in_specs=[
            part(0),
            part(pairs),
            part(2 * pairs),
            pl.BlockSpec((1, 1, both), lambda p: (p, 0, 0)),
            pl.BlockSpec((length, 1), lambda p: (0, 0)),
        ],
        out_specs=(part(0), pl.BlockSpec((1, length, both), lambda p: (p, 0, 0))),
        compiler_params=roomy,
        cost_estimate=pl.CostEstimate(flops=10**9, bytes_accessed=4 * 10**6, transcendentals=10**6),
    )(merged, merged, merged, bias_rows, keep_rows)


def self_backward(merged, probs, grad, head_size):
    length, model = grad.shape
    width, pairs = 2 * head_size, model // (2 * head_size)
    both = 2 * length
    part = lambda offset: pl.BlockSpec((length, width), lambda p: (0, p + offset))
    return pl.pallas_call(
        functools.partial(self_backward_kernel, head_size),
        grid=(pairs,),
        out_shape=(
            jax.ShapeDtypeStruct((length, 3 * model), bf16),
            jax.ShapeDtypeStruct((pairs, 1, both), f32),
        ),
        in_specs=[
            part(0),
            part(pairs),
            part(2 * pairs),
            pl.BlockSpec((1, length, both), lambda p: (p, 0, 0)),
            part(0),
        ],
        out_specs=(
            pl.BlockSpec((length, 3 * model), lambda p: (0, 0)),
            pl.BlockSpec((1, 1, both), lambda p: (p, 0, 0)),
        ),
        compiler_params=roomy,
        cost_estimate=pl.CostEstimate(flops=10**9, bytes_accessed=4 * 10**6, transcendentals=0),
    )(merged, merged, merged, probs, grad)


def cross_forward(queries, key_values, head_size):
    length, model = queries.shape
    memory_len = key_values.shape[0]
    width, pairs = 2 * head_size, model // (2 * head_size)
    both = 2 * length
    part = pl.BlockSpec((length, width), lambda p: (0, p))
    long_part = lambda offset: pl.BlockSpec((memory_len, width), lambda p: (0, p + offset))
    return pl.pallas_call(
        functools.partial(cross_forward_kernel, head_size),
        grid=(pairs,),
        out_shape=(
            jax.ShapeDtypeStruct((length, model), bf16),
            jax.ShapeDtypeStruct((pairs, memory_len, both), bf16),
        ),
        in_specs=[part, long_part(0), long_part(pairs)],
        out_specs=(part, pl.BlockSpec((1, memory_len, both), lambda p: (p, 0, 0))),
        compiler_params=roomy,
        cost_estimate=pl.CostEstimate(
            flops=4 * 10**9, bytes_accessed=13 * 10**6, transcendentals=4 * 10**6
        ),
    )(queries, key_values, key_values)


def cross_backward(queries, key_values, probs, grad, head_size):
    length, model = queries.shape
    memory_len = key_values.shape[0]
    width, pairs = 2 * head_size, model // (2 * head_size)
    both = 2 * length
    part = pl.BlockSpec((length, width), lambda p: (0, p))
    long_part = lambda offset: pl.BlockSpec((memory_len, width), lambda p: (0, p + offset))
    return pl.pallas_call(
        functools.partial(cross_backward_kernel, head_size),
        grid=(pairs,),
        out_shape=(
            jax.ShapeDtypeStruct((length, model), bf16),
            jax.ShapeDtypeStruct((memory_len, 2 * model), bf16),
        ),
        in_specs=[
            part,
            long_part(0),
            long_part(pairs),
            pl.BlockSpec((1, memory_len, both), lambda p: (p, 0, 0)),
            part,
        ],
        out_specs=(part, pl.BlockSpec((memory_len, 2 * model), lambda p: (0, 0))),
        compiler_params=roomy,
        cost_estimate=pl.CostEstimate(
            flops=8 * 10**9, bytes_accessed=18 * 10**6, transcendentals=0
        ),
    )(queries, key_values, key_values, probs, grad)


class Gather:
    def __init__(self, send_sem, recv_sem, own_sem):
        self.z, self.x, self.y, self.core = standing()
        self.sets = flips(self.x, self.y, self.core)
        self.along_z, self.second, self.first, self.sibling = partners()
        self.send_sem, self.recv_sem, self.own_sem = send_sem, recv_sem, own_sem
        self.chunks, self.flying, self.own, self.clock, self.after = [], {}, {}, 0, {}

    def add(self, shard, out, after=None):
        chunk = len(self.chunks)
        self.chunks.append((shard, out))
        self.after[chunk] = after
        own = pltpu.make_async_copy(
            shard, out.at[self.z, self.x, self.y, self.core], self.own_sem.at[chunk]
        )
        own.start()
        self.own[chunk] = own
        return chunk

    def copies(self, number, chunk):
        base = chunk * 10
        shard, out = self.chunks[chunk]
        if number == 0:
            return [
                remote(
                    shard,
                    out.at[self.z, self.x, self.y, self.core],
                    self.send_sem,
                    self.recv_sem,
                    base + k,
                    device,
                )
                for k, device in enumerate(self.along_z)
            ]
        piece = lambda k: out.at[:, self.sets[k][0], self.sets[k][1], self.core]
        device = (self.second, self.first, self.sibling)[number - 1]
        amount = (1, 2, 4)[number - 1]
        return [
            remote(piece(k), piece(k), self.send_sem, self.recv_sem, base + 2 + amount + k, device)
            for k in range(amount)
        ]

    def pump(self, spacing, steps=1):
        for unused in range(steps):
            for number in (4, 3, 2, 1, 0):
                chunk = self.clock - number * spacing
                if 0 <= chunk < len(self.chunks):
                    if number == 1:
                        self.own[chunk].wait()
                    if number > 0:
                        for copy in self.flying[number - 1, chunk]:
                            copy.wait_recv()
                    if number < 4:
                        self.flying[number, chunk] = self.copies(number, chunk)
                        for copy in self.flying[number, chunk]:
                            copy.start()
                    elif self.after[chunk] is not None:
                        self.after[chunk]()
            self.clock += 1

    def until(self, spacing, chunk):
        while self.clock <= chunk + 4 * spacing:
            self.pump(spacing)

    def finish(self):
        for copies in self.flying.values():
            for copy in copies:
                copy.wait_send()


def rms_rounded(rows, gain):
    turn = lax.rsqrt(jnp.mean(rows * rows, axis=-1, keepdims=True) + epsilon)
    return (rows * turn * gain).astype(bf16)


class Weights(NamedTuple):
    w_kv2: object
    w_qkv: object
    w_out1: object
    w_q2: object
    w_out2: object
    w_gate: object
    w_upper: object
    w_out3: object


class ForwardIn(NamedTuple):
    outgoing: object
    pick: object
    bias: object
    keep: object
    gains: object
    tail: object
    table: object
    memory: object


class ForwardOut(NamedTuple):
    key_values: object
    cross_probs: object
    requests: object
    embedded: object
    normed1: object
    merged: object
    self_probs: object
    mixed1: object
    after_self: object
    normed2: object
    queries: object
    mixed2: object
    after_cross: object
    normed3: object


class ForwardRefs(NamedTuple):
    outgoing: object
    pick: object
    bias: object
    keep: object
    gains: object
    tail: object
    table: object
    memory: object
    key_values: object
    cross_probs: object
    requests: object
    embedded: object
    normed1: object
    merged: object
    self_probs: object
    mixed1: object
    after_self: object
    normed2: object
    queries: object
    mixed2: object
    after_cross: object
    normed3: object
    kv2_v: object
    qkv_v: object
    out1_v: object
    q2_v: object
    out2_v: object
    memory_v: object
    kv_v: object
    table_v: object
    last_v: object
    found_f: object
    found_v: object
    arrived: object
    s_v: object
    p_v: object
    send: object
    recv: object
    own: object
    fetch: object
    id_send: object
    id_recv: object
    row_send: object
    row_recv: object


def every_other(me, owners, action):
    def one(step, unused):
        action(step, (me + step) % owners)
        return unused

    lax.fori_loop(1, owners, one, 0)


def forward_kernel(head_size, spacing, *refs):
    count = len(Weights._fields)
    shards, refs = refs[:count], refs[count:]
    inputs = len(ForwardIn._fields)
    whole = refs[inputs:inputs + count]
    at = ForwardRefs(*refs[:inputs], *refs[inputs + count:])
    scale = head_size ** (-0.5)
    width = 2 * head_size
    length, model = at.embedded.shape
    memory_len = at.memory.shape[0]
    pairs = model // width
    both = 2 * length
    owners = 32
    me = lax.axis_index("wide") * 4 + lax.axis_index("narrow")
    place_of = lambda other: (other // 4, other % 4)

    def fetch(index, source, target):
        copy = pltpu.make_async_copy(source, target, at.fetch.at[index])
        copy.start()
        return copy

    block = at.table_v.shape[1]
    blocks = at.table.shape[0] // block
    rest = (at.table.shape[0] - blocks * block) // 16 * 16
    get_table = {}
    table_block = lambda k: fetch(
        k, at.table.at[pl.ds(k * block, block), :], at.table_v.at[k % 3]
    )
    for k in range(3):
        get_table[k] = table_block(k)
    get_last = fetch(
        16, at.table.at[pl.ds(blocks * block, rest), :], at.last_v.at[0:rest, :]
    )
    get_memory = fetch(17, at.memory, at.memory_v)

    barrier = pltpu.get_barrier_semaphore()
    every_other(
        me,
        owners,
        lambda step, other: pl.semaphore_signal(
            barrier, inc=1, device_id=place_of(other), device_id_type=mesh_ids
        ),
    )
    pl.semaphore_wait(barrier, owners - 1)

    id_copy = lambda step, other: remote(
        at.outgoing.at[other],
        at.requests.at[me],
        at.id_send,
        at.id_recv,
        step - 1,
        place_of(other),
    )
    every_other(me, owners, lambda step, other: id_copy(step, other).start())

    gather = Gather(at.send, at.recv, at.own)
    got = {}
    order = {}

    def add(index, part, parts, kept=None):
        size = shards[index].shape[1] // parts
        lanes = pl.ds(part * size, size)
        out = whole[index].at[:, :, :, :, :, lanes]
        after = None
        chunk = len(gather.chunks)
        if kept is not None:

            def after():
                got[chunk] = fetch(18 + chunk, out, kept.at[:, :, :, :, :, lanes])

        gather.add(shards[index].at[:, lanes], out, after)
        order[index, part] = chunk

    for part in range(2):
        add(0, part, 2, at.kv2_v)
    for part in range(3):
        add(1, part, 3, at.qkv_v)
    add(2, 0, 1, at.out1_v)
    add(3, 0, 1, at.q2_v)
    add(4, 0, 1, at.out2_v)
    for index in (5, 6, 7):
        for part in range(2):
            add(index, part, 2)

    def ready(index, part):
        chunk = order[index, part]
        gather.until(spacing, chunk)
        if chunk in got:
            got.pop(chunk).wait()

    def weight(kept, start, size):
        return kept[:, :, :, :, :, start:start + size].reshape(model, size)

    gather.pump(spacing)
    at.requests[me] = at.outgoing[me]
    at.last_v[rest:rest + 16, :] = at.tail[...]
    at.last_v[rest + 16:, :] = jnp.zeros_like(at.last_v[rest + 16:, :])
    gather.pump(spacing)
    every_other(me, owners, lambda step, other: id_copy(step, other).wait())

    slots = owners * at.requests.shape[1]

    def hits(start, size):
        wanted = at.requests[...].reshape(slots, 128)
        lane = lax.broadcasted_iota(jnp.int32, (slots, 128), 1)
        offset = wanted - lane
        return jnp.concatenate(
            [
                jnp.where(offset == start + column, 1.0, 0.0).astype(bf16)
                for column in range(0, size, 128)
            ],
            axis=1,
        )

    get_last.wait()
    at.found_f[...] = matmul(hits(blocks * block, at.last_v.shape[0]), at.last_v[...])
    for k in range(blocks):
        get_table[k].wait()
        at.found_f[...] += matmul(hits(k * block, block), at.table_v[k % 3])
        if k + 3 < blocks:
            get_table[k + 3] = table_block(k + 3)
        if k % 3 == 2:
            gather.pump(spacing)
    at.found_v[...] = at.found_f[...].astype(bf16).reshape(at.found_v.shape)
    at.arrived[me] = at.found_v[me]
    row_copy = lambda step, other: remote(
        at.found_v.at[other],
        at.arrived.at[me],
        at.row_send,
        at.row_recv,
        step - 1,
        place_of(other),
    )
    every_other(me, owners, lambda step, other: row_copy(step, other).start())
    gather.pump(spacing)

    get_memory.wait()
    put_kv = []
    tile = 256
    for part in range(2):
        ready(0, part)
        for start in range(part * model, (part + 1) * model, tile):
            columns = weight(at.kv2_v, start, tile)
            for row in range(0, memory_len, 512):
                at.kv_v[row:row + 512, start:start + tile] = matmul(
                    at.memory_v[row:row + 512, :], columns
                ).astype(bf16)
        lanes = pl.ds(part * model, model)
        put_kv.append(fetch(32 + part, at.kv_v.at[:, lanes], at.key_values.at[:, lanes]))
        gather.pump(spacing)

    every_other(me, owners, lambda step, other: row_copy(step, other).wait())
    embedded = matmul(at.pick[...], at.arrived[...].reshape(slots, model))
    at.embedded[...] = embedded
    at.normed1[...] = rms_rounded(embedded, at.gains[0:1, :])
    for part in range(3):
        ready(1, part)
        for start in range(part * model, (part + 1) * model, tile):
            at.merged[:, start:start + tile] = matmul(
                at.normed1[...], weight(at.qkv_v, start, tile)
            ).astype(bf16)
    row = lax.broadcasted_iota(jnp.int32, (length, both), 0)
    lane = lax.broadcasted_iota(jnp.int32, (length, both), 1)
    query_row = jnp.where(lane >= length, lane - length, lane)
    seen = (row <= query_row) & (at.keep[...] > 0.0)
    for pair in range(pairs):
        lanes = slice(pair * width, (pair + 1) * width)
        key_lanes = slice(model + pair * width, model + (pair + 1) * width)
        value_lanes = slice(2 * model + pair * width, 2 * model + (pair + 1) * width)
        query = spread_heads(at.merged[:, lanes], head_size)
        scores = back_product(at.merged[:, key_lanes], query) * scale
        bias = pltpu.roll(
            jnp.broadcast_to(at.bias[pair], scores.shape), 0, 1, stride=1, stride_axis=0
        )
        probs = column_softmax(jnp.where(seen, scores + bias, blocked)).astype(bf16)
        at.self_probs[pair] = probs
        turned = down_product(at.merged[:, value_lanes], probs)
        at.mixed1[:, lanes] = join_heads(turned, head_size).astype(bf16)
        if pair % 2 == 1:
            gather.pump(spacing)
    ready(2, 0)
    for start in range(0, model, tile):
        at.after_self[:, start:start + tile] = at.embedded[:, start:start + tile] + matmul(
            at.mixed1[...], weight(at.out1_v, start, tile)
        )
    at.normed2[...] = rms_rounded(at.after_self[...], at.gains[1:2, :])
    ready(3, 0)
    for start in range(0, model, tile):
        at.queries[:, start:start + tile] = matmul(
            at.normed2[...], weight(at.q2_v, start, tile)
        ).astype(bf16)
    tiles = memory_len // tile
    put_probs = {}
    for pair in range(pairs):
        lanes = slice(pair * width, (pair + 1) * width)
        value_lanes = slice(model + pair * width, model + (pair + 1) * width)
        query = spread_heads(at.queries[:, lanes], head_size)
        if pair >= 2:
            put_probs[pair - 2].wait()
        probs = at.p_v.at[pair % 2]

        def score(index, peak):
            place = pl.ds(pl.multiple_of(index * tile, tile), tile)
            part = back_product(at.kv_v[place, lanes], query) * scale
            at.s_v[place, :] = part
            return jnp.maximum(peak, jnp.max(part.reshape(tile // 8, 8, both), axis=0))

        peak = lax.fori_loop(0, tiles, score, jnp.full((8, both), blocked, f32))
        peak = jnp.max(peak, axis=0, keepdims=True)

        def power(index, total):
            place = pl.ds(pl.multiple_of(index * tile, tile), tile)
            part = jnp.exp(at.s_v[place, :] - peak)
            at.s_v[place, :] = part
            return total + jnp.sum(part.reshape(tile // 8, 8, both), axis=0)

        total = lax.fori_loop(0, tiles, power, jnp.zeros((8, both), f32))
        share = 1.0 / jnp.sum(total, axis=0, keepdims=True)

        def normal(index, unused):
            place = pl.ds(pl.multiple_of(index * tile, tile), tile)
            probs[place, :] = (at.s_v[place, :] * share).astype(bf16)
            return unused

        lax.fori_loop(0, tiles, normal, 0)
        put_probs[pair] = fetch(34 + pair, probs, at.cross_probs.at[pair])
        turned = down_product(at.kv_v[:, value_lanes], probs[...])
        at.mixed2[:, lanes] = join_heads(turned, head_size).astype(bf16)
        gather.pump(spacing)
    ready(4, 0)
    for start in range(0, model, tile):
        at.after_cross[:, start:start + tile] = at.after_self[
            :, start:start + tile
        ] + matmul(at.mixed2[...], weight(at.out2_v, start, tile))
    at.normed3[...] = rms_rounded(at.after_cross[...], at.gains[2:3, :])
    gather.until(spacing, len(gather.chunks) - 1)
    gather.finish()
    for copy in put_kv + [put_probs[pairs - 2], put_probs[pairs - 1]]:
        copy.wait()


def forward_with_gather(inputs, shards, head_size):
    length, slots = inputs.pick.shape
    memory_len, model = inputs.memory.shape
    owners = 32
    room = slots // owners
    pairs = model // (2 * head_size)
    both = 2 * length
    rows = model // owners
    struct = jax.ShapeDtypeStruct
    tokens = lambda columns, kind: struct((length, columns), kind)
    far_outs = [struct((4, 2, 2, 2) + shard.shape, bf16) for shard in shards] + [
        struct((memory_len, 2 * model), bf16),
        struct((pairs, memory_len, both), bf16),
    ]
    near_outs = [
        struct((owners, room, 128), jnp.int32),
        tokens(model, f32),
        tokens(model, bf16),
        tokens(3 * model, bf16),
        struct((pairs, length, both), bf16),
        tokens(model, bf16),
        tokens(model, f32),
        tokens(model, bf16),
        tokens(model, bf16),
        tokens(model, bf16),
        tokens(model, f32),
        tokens(model, bf16),
    ]
    by_owner = lambda columns: pltpu.VMEM((4, 2, 2, 2, rows, columns), bf16)
    own = [
        by_owner(2 * model),
        by_owner(3 * model),
        by_owner(model),
        by_owner(model),
        by_owner(model),
        pltpu.VMEM((memory_len, model), bf16),
        pltpu.VMEM((memory_len, 2 * model), bf16),
        pltpu.VMEM((3, 512, model), bf16),
        pltpu.VMEM((256, model), bf16),
        pltpu.VMEM((slots, model), f32),
        pltpu.VMEM((owners, room, model), bf16),
        pltpu.VMEM((owners, room, model), bf16),
        pltpu.VMEM((memory_len, both), f32),
        pltpu.VMEM((2, memory_len, both), bf16),
    ]
    dma = pltpu.SemaphoreType.DMA
    chunks = 14
    others = owners - 1
    sems = [dma((size,)) for size in (10 * chunks, 10 * chunks, chunks, 40) + (others,) * 4]
    far = pl.BlockSpec(memory_space=pl.ANY)
    near = pl.BlockSpec(memory_space=pltpu.VMEM)
    results = pl.pallas_call(
        functools.partial(forward_kernel, head_size, 2),
        out_shape=far_outs + near_outs,
        in_specs=[near] * (len(shards) + len(inputs) - 2) + [far] * 2,
        out_specs=[far] * len(far_outs) + [near] * len(near_outs),
        scratch_shapes=own + sems,
        compiler_params=pltpu.CompilerParams(
            collective_id=1, has_side_effects=True, vmem_limit_bytes=63 * 1024 * 1024
        ),
    )(*shards, *inputs)
    count = len(shards)
    weights = Weights(*[whole.reshape(-1, whole.shape[-1]) for whole in results[:count]])
    return weights, ForwardOut(*results[count:])


class Sums:
    def __init__(self, send_sem, recv_sem, load_sem, free_sem):
        self.z, self.x, self.y, self.core = standing()
        self.sets = flips(self.x, self.y, self.core)
        self.sibling_sets = flips(self.x, self.y, 1 - self.core)
        self.along_z, self.second, self.first, self.sibling = partners()
        self.send_sem, self.recv_sem = send_sem, recv_sem
        self.load_sem, self.free_sem = load_sem, free_sem
        self.chunks, self.flying, self.loads, self.clock = [], {}, {}, 0

    def add(self, source, buffers, out, stride, offset, frees=None, needs=None):
        self.chunks.append((source, buffers, out, stride, offset, frees, needs))

    def copies(self, number, chunk):
        source, (kept, from_core, from_first, from_second, from_z) = self.chunks[chunk][:2]
        sets, others = self.sets, self.sibling_sets
        base = 10 * chunk
        go = lambda start, end, index, device: remote(
            start, end, self.send_sem, self.recv_sem, base + index, device
        )
        if number == 0:
            return [
                go(
                    source.at[:, others[k][0], others[k][1], 1 - self.core],
                    from_core.at[k],
                    k,
                    self.sibling,
                )
                for k in range(4)
            ]
        if number == 1:
            return [go(kept.at[2 + k], from_first.at[k], 4 + k, self.first) for k in range(2)]
        if number == 2:
            return [go(kept.at[1], from_second, 6, self.second)]
        return [
            go(kept.at[0, (self.z + k + 1) % 4], from_z.at[k], 7 + k, self.along_z[k])
            for k in range(3)
        ]

    def begin(self, number, chunk):
        source, buffers, unused, unused, unused, unused, needs = self.chunks[chunk]
        if number == 0:
            if needs is not None:
                pl.semaphore_wait(self.free_sem.at[needs], 6)
            self.loads[chunk] = [
                pltpu.make_async_copy(
                    source.at[:, self.sets[k][0], self.sets[k][1], self.core],
                    buffers[0].at[k],
                    self.load_sem.at[4 * chunk + k],
                )
                for k in range(4)
            ]
            for load in self.loads[chunk]:
                load.start()
        self.flying[number, chunk] = self.copies(number, chunk)
        for copy in self.flying[number, chunk]:
            copy.start()

    def settle(self, number, chunk):
        source, buffers, out, stride, offset, frees, unused = self.chunks[chunk]
        kept, from_core, from_first, from_second, from_z = buffers
        for copy in self.flying[number, chunk]:
            copy.wait_recv()
        if number == 0:
            for load in self.loads[chunk]:
                load.wait()
            for k in (2, 3, 1, 0):
                add_into(kept.at[k], from_core.at[k])
        elif number == 1:
            for k in (1, 0):
                add_into(kept.at[k], from_first.at[k])
        elif number == 2:
            add_into(kept.at[0], from_second)
        else:
            total = kept[0, self.z].astype(f32)
            for k in range(3):
                total = total + from_z[k].astype(f32)
            rows, width = total.shape
            for tile in range(width // 128):
                out[pl.ds(offset + tile, rows, stride), :] = total[:, tile * 128:(tile + 1) * 128]
            for stage in range(4):
                for copy in self.flying[stage, chunk]:
                    copy.wait_send()
            if frees is not None:
                for device in self.along_z + [self.second, self.first, self.sibling]:
                    pl.semaphore_signal(
                        self.free_sem.at[frees], inc=1, device_id=device, device_id_type=mesh_ids
                    )

    def pump(self, spacing, steps=1):
        for unused in range(steps):
            for number in (4, 3, 2, 1, 0):
                chunk = self.clock - number * spacing
                if 0 <= chunk < len(self.chunks):
                    if number > 0:
                        self.settle(number - 1, chunk)
                    if number < 4:
                        self.begin(number, chunk)
            self.clock += 1


def add_into(target, source):
    def quarter(index, unused):
        target[index] = (target[index].astype(f32) + source[index].astype(f32)).astype(bf16)
        return unused

    lax.fori_loop(0, 4, quarter, 0)


def norm_back(rows, gain, upstream):
    turn = lax.rsqrt(jnp.mean(rows * rows, axis=-1, keepdims=True) + epsilon)
    scaled = gain * upstream
    inner = jnp.sum(scaled * rows, axis=-1, keepdims=True) / rows.shape[1]
    gain_grad = jnp.sum(upstream * rows * turn, axis=0, keepdims=True)
    return turn * scaled - rows * (turn * turn * turn * inner), gain_grad


def share_into(target, left, right, turned, tile):
    depth, model = left.shape
    rows, width = target.shape[4], right.shape[1]
    half = model // 2
    block = min(depth, 256)
    for start in range(0, depth, block):
        size = min(block, depth - start)
        turned[:, start:start + size] = left[start:start + size, :].T

    for index in range(width // tile):
        place = slice(index * tile, (index + 1) * tile)
        for part in range(2):
            product = matmul(turned[part * half:(part + 1) * half, 0:depth], right[:, place])
            target[2 * part:2 * part + 2, :, :, :, :, place] = product.astype(bf16).reshape(
                2, 2, 2, 2, rows, tile
            )


def fold_rows(scores):
    both = scores.shape[1]
    while scores.shape[0] % 16 == 0:
        rows = scores.shape[0] // 2
        scores = scores[:rows] + pltpu.roll(scores[rows:], both - rows, 1)
    total = scores[:8]
    for start in range(8, scores.shape[0], 8):
        total = total + pltpu.roll(scores[start:start + 8], both - start, 1)
    row = lax.broadcasted_iota(jnp.int32, total.shape, 0)
    for bit in (1, 2, 4):
        total = jnp.where((row // bit) % 2 == 1, pltpu.roll(total, both - bit, 1), total)
    return jnp.sum(total, axis=0, keepdims=True)


class BackwardIn(NamedTuple):
    share_out3: object
    share_gate: object
    share_upper: object
    share_out2: object
    key_values: object
    cross_probs: object
    memory: object
    w_q2: object
    w_out1: object
    w_qkv: object
    w_kv2: object
    queries: object
    grad_cross: object
    normed2: object
    after_self: object
    grad_state: object
    mixed1: object
    merged: object
    self_probs: object
    normed1: object
    embedded: object
    gains: object
    pick: object
    gain3: object


class BackwardOut(NamedTuple):
    qkv: object
    out1: object
    q2: object
    kv2: object
    out2: object
    ffn: object
    out3: object
    small: object
    returned: object
    memory_grad: object


class BackwardRefs(NamedTuple):
    share_out3: object
    share_gate: object
    share_upper: object
    share_out2: object
    key_values: object
    cross_probs: object
    memory: object
    w_q2: object
    w_out1: object
    w_qkv: object
    w_kv2: object
    queries: object
    grad_cross: object
    normed2: object
    after_self: object
    grad_state: object
    mixed1: object
    merged: object
    self_probs: object
    normed1: object
    embedded: object
    gains: object
    pick: object
    gain3: object
    qkv: object
    out1: object
    q2: object
    kv2: object
    out2: object
    ffn: object
    out3: object
    small: object
    returned: object
    memory_grad: object
    kv_v: object
    p_v: object
    wq2_v: object
    wo1_v: object
    wqkv_v: object
    wkv_v: object
    turn_v: object
    ds_v: object
    dq_v: object
    dkv_v: object
    dqkv_v: object
    do_v: object
    rows_v: object
    slots_v: object
    s_kv: object
    s_q2: object
    s_out1: object
    s_qkv: object
    small_v: object
    small_in: object
    send: object
    recv: object
    load: object
    free: object
    fetch: object
    small_send: object
    small_recv: object
    slot_send: object
    slot_recv: object


backward_far = 11


def backward_kernel(head_size, spacing, *refs):
    names = len(BackwardRefs._fields)
    at = BackwardRefs(*refs[:names])
    buffers = refs[names:]
    groups = [buffers[5 * k:5 * k + 5] for k in range(len(buffers) // 5)]
    scale = head_size ** (-0.5)
    width = 2 * head_size
    length, model = at.queries.shape
    memory_len = at.kv_v.shape[0]
    pairs = model // width
    owners = 32
    me = lax.axis_index("wide") * 4 + lax.axis_index("narrow")

    def fetch(index, source, target):
        copy = pltpu.make_async_copy(source, target, at.fetch.at[index])
        copy.start()
        return copy

    probs_at = lambda pair: fetch(pair, at.cross_probs.at[pair], at.p_v.at[pair % 2])
    get_kv = fetch(6, at.key_values, at.kv_v)
    get_probs = {0: probs_at(0)}
    get_q2 = fetch(8, at.w_q2, at.wq2_v)
    get_out1 = fetch(9, at.w_out1, at.wo1_v)
    get_qkv = fetch(10, at.w_qkv, at.wqkv_v)
    get_kv2 = fetch(11, at.w_kv2, at.wkv_v)

    barrier = pltpu.get_barrier_semaphore()

    def hello(step, unused):
        other = (me + step) % owners
        pl.semaphore_signal(
            barrier, inc=1, device_id=(other // 4, other % 4), device_id_type=mesh_ids
        )
        return unused

    lax.fori_loop(1, owners, hello, 0)
    pl.semaphore_wait(barrier, owners - 1)

    sums = Sums(at.send, at.recv, at.load, at.free)
    gate_width = at.share_gate.shape[5] // 2
    model_tiles = model // 128
    gate_tiles = gate_width // 128
    half_model = model // 2

    def columns(ref, part, size):
        return ref.at[:, :, :, :, :, pl.ds(part * size, size)]

    def narrowed(group, size):
        return (
            group[0].at[:, :, :, pl.ds(0, size)],
            group[1].at[:, :, :, pl.ds(0, size)],
            group[2].at[:, :, :, pl.ds(0, size)],
            group[3].at[:, :, pl.ds(0, size)],
            group[4].at[:, :, pl.ds(0, size)],
        )

    for part in range(2):
        sums.add(
            columns(at.share_out3, part, half_model),
            groups[part],
            at.out3,
            model_tiles,
            part * model_tiles // 2,
        )
    for k, share in enumerate((at.share_gate, at.share_upper)):
        for part in range(2):
            sums.add(
                columns(share, part, gate_width),
                groups[2 + 2 * k + part],
                at.ffn,
                4 * gate_tiles,
                (2 * k + part) * gate_tiles,
                frees=2 * k + part,
            )
    sums.add(at.share_out2, groups[6], at.out2, model_tiles, 0)
    for part in range(2):
        sums.add(
            columns(at.s_kv, part, model),
            groups[7 + part],
            at.kv2,
            2 * model_tiles,
            part * model_tiles,
        )
    sums.add(at.s_q2, groups[9], at.q2, model_tiles, 0)
    sums.add(at.s_out1, narrowed(groups[2], model), at.out1, model_tiles, 0, needs=0)
    for part in range(3):
        sums.add(
            columns(at.s_qkv, part, model),
            narrowed(groups[3 + part], model),
            at.qkv,
            3 * model_tiles,
            part * model_tiles,
            needs=1 + part,
        )

    sums.pump(spacing, 3)
    get_kv.wait()
    tile = 256
    tiles = memory_len // tile
    for pair in range(pairs):
        lanes = slice(pair * width, (pair + 1) * width)
        value_lanes = slice(model + pair * width, model + (pair + 1) * width)
        get_probs[pair].wait()
        if pair + 1 < pairs:
            get_probs[pair + 1] = probs_at(pair + 1)
        probs = at.p_v.at[pair % 2]
        grad = spread_heads(at.grad_cross[:, lanes], head_size)
        query = spread_heads(at.queries[:, lanes], head_size)
        both = 2 * length

        def first_pass(index, center):
            place = pl.ds(pl.multiple_of(index * tile, tile), tile)
            product = back_product(at.kv_v[place, value_lanes], grad)
            part = (product * probs[place, :].astype(f32)).reshape(tile // 8, 8, both)
            return center + jnp.sum(part, axis=0)

        center = lax.fori_loop(0, tiles, first_pass, jnp.zeros((8, both), f32))
        center = jnp.sum(center, axis=0, keepdims=True)
        def second_pass(index, unused):
            place = pl.ds(pl.multiple_of(index * tile, tile), tile)
            weights = probs[place, :]
            product = back_product(at.kv_v[place, value_lanes], grad)
            scores = (weights.astype(f32) * (product - center)).astype(bf16)
            at.dkv_v[place, value_lanes] = matmul(weights, grad).astype(bf16)
            at.dkv_v[place, lanes] = (matmul(scores, query) * scale).astype(bf16)
            at.ds_v[place, :] = scores
            return unused

        lax.fori_loop(0, tiles, second_pass, 0)
        turned = down_product(at.kv_v[:, lanes], at.ds_v[...])
        at.dq_v[:, lanes] = (join_heads(turned, head_size) * scale).astype(bf16)
        if pair % 2 == 1:
            sums.pump(spacing)

    get_memory = fetch(7, at.memory, at.kv_v.at[:, 0:model])
    get_q2.wait()
    upstream = back_product(at.dq_v[...], at.wq2_v[...])
    grad_rows, gain2 = norm_back(at.after_self[...], at.gains[1:2, :], upstream)
    at.rows_v[...] = at.grad_state[...] + grad_rows
    get_out1.wait()
    branch = at.rows_v[...].astype(bf16)
    at.do_v[...] = back_product(branch, at.wo1_v[...]).astype(bf16)
    at.slots_v[0:length // 16] = branch.reshape(length // 16, 16, model)
    sums.pump(spacing)
    get_memory.wait()
    share_into(at.s_kv, at.kv_v.at[:, 0:model], at.dkv_v, at.turn_v, 256)
    sums.pump(spacing)

    for pair in range(pairs):
        lanes = slice(pair * width, (pair + 1) * width)
        key_lanes = slice(model + pair * width, model + (pair + 1) * width)
        value_lanes = slice(2 * model + pair * width, 2 * model + (pair + 1) * width)
        grad = spread_heads(at.do_v[:, lanes], head_size)
        query = spread_heads(at.merged[:, lanes], head_size)
        weights = at.self_probs[pair]
        wide = weights.astype(f32)
        product = back_product(at.merged[:, value_lanes], grad)
        center = jnp.sum(product * wide, axis=0, keepdims=True)
        scores = (wide * (product - center)).astype(bf16)
        at.dqkv_v[:, value_lanes] = matmul(weights, grad).astype(bf16)
        at.dqkv_v[:, key_lanes] = (matmul(scores, query) * scale).astype(bf16)
        turned = down_product(at.merged[:, key_lanes], scores)
        at.dqkv_v[:, lanes] = (join_heads(turned, head_size) * scale).astype(bf16)
        distance = fold_rows(scores.astype(f32))
        for part in range(3):
            at.small_v[18 + 3 * pair + part:19 + 3 * pair + part, :] = distance[
                :, part * 128:(part + 1) * 128
            ]
    sums.pump(spacing)
    get_qkv.wait()
    upstream = back_product(at.dqkv_v[...], at.wqkv_v[...])
    grad_rows, gain1 = norm_back(at.embedded[...], at.gains[0:1, :], upstream)
    row_grads = (at.rows_v[...] + grad_rows).astype(bf16)
    share_into(at.s_q2, at.normed2, at.dq_v, at.turn_v, 256)
    branch_rows = at.slots_v.at[0:length // 16]
    at.do_v[...] = branch_rows[...].reshape(length, model)
    sums.pump(spacing)
    share_into(at.s_out1, at.mixed1, at.do_v, at.turn_v, 256)
    sums.pump(spacing)
    share_into(at.s_qkv, at.normed1, at.dqkv_v, at.turn_v, 256)
    slots = down_product(at.pick[...], row_grads).astype(bf16)
    at.slots_v[...] = slots.reshape(at.slots_v.shape)
    at.returned[me] = at.slots_v[me]

    def slot_copy(step):
        other = (me + step) % owners
        return remote(
            at.slots_v.at[other],
            at.returned.at[me],
            at.slot_send,
            at.slot_recv,
            step - 1,
            (other // 4, other % 4),
        )

    def slot_start(step, unused):
        slot_copy(step).start()
        return unused

    lax.fori_loop(1, owners, slot_start, 0)
    for part in range(6):
        block = slice(part * 128, (part + 1) * 128)
        at.small_v[part:part + 1, :] = gain1[:, block]
        at.small_v[6 + part:7 + part, :] = gain2[:, block]
        at.small_v[12 + part:13 + part, :] = at.gain3[:, block]
    at.small_v[36:40, :] = jnp.zeros((4, 128), f32)
    at.small[...] = at.small_v[...]
    sums.pump(spacing)

    get_kv2.wait()

    def memory_tile(index, unused):
        place = pl.ds(pl.multiple_of(index * tile, tile), tile)
        at.kv_v[place, model:] = back_product(
            at.dkv_v[place, :], at.wkv_v[...]
        ).astype(bf16)
        return unused

    lax.fori_loop(0, tiles, memory_tile, 0)
    put_memory = fetch(12, at.kv_v.at[:, model:], at.memory_grad)

    groups_of = [[sums.sibling], [sums.first], [sums.second], sums.along_z]
    taken = 0
    for group in groups_of:
        copies = [
            remote(
                at.small,
                at.small_in.at[taken + k],
                at.small_send,
                at.small_recv,
                taken + k,
                device,
            )
            for k, device in enumerate(group)
        ]
        for copy in copies:
            copy.start()
        sums.pump(spacing)
        for copy in copies:
            copy.wait()
        total = at.small[...]
        for k in range(len(group)):
            total = total + at.small_in[taken + k]
        at.small[...] = total
        taken += len(group)
    while sums.clock < len(sums.chunks) + 4 * spacing:
        sums.pump(spacing)

    def slot_end(step, unused):
        slot_copy(step).wait()
        return unused

    lax.fori_loop(1, owners, slot_end, 0)
    put_memory.wait()


def backward_with_sums(inputs, head_size, slot_rows):
    length, model = inputs.queries.shape
    memory_len = inputs.memory.shape[0]
    owners = 32
    rows = model // owners
    pairs = model // (2 * head_size)
    both = 2 * length
    out3_rows = inputs.share_out3.shape[0] // owners
    ffn = inputs.share_gate.shape[1]
    by_owner = lambda share: share.reshape(4, 2, 2, 2, -1, share.shape[-1])
    inputs = [by_owner(share) for share in inputs[:4]] + list(inputs[4:])
    flat = lambda count, columns: jax.ShapeDtypeStruct((count * columns // 128, 128), f32)
    outs = [
        flat(rows, 3 * model),
        flat(rows, model),
        flat(rows, model),
        flat(rows, 2 * model),
        flat(rows, model),
        flat(rows, 2 * ffn),
        flat(out3_rows, model),
        jax.ShapeDtypeStruct((40, 128), f32),
        jax.ShapeDtypeStruct((owners, slot_rows, model), bf16),
        jax.ShapeDtypeStruct((memory_len, model), bf16),
    ]
    own = [
        pltpu.VMEM((memory_len, 2 * model), bf16),
        pltpu.VMEM((2, memory_len, both), bf16),
        pltpu.VMEM((model, model), bf16),
        pltpu.VMEM((model, model), bf16),
        pltpu.VMEM((model, 3 * model), bf16),
        pltpu.VMEM((model, 2 * model), bf16),
        pltpu.VMEM((model, memory_len), bf16),
        pltpu.VMEM((memory_len, both), bf16),
        pltpu.VMEM((length, model), bf16),
        pltpu.VMEM((memory_len, 2 * model), bf16),
        pltpu.VMEM((length, 3 * model), bf16),
        pltpu.VMEM((length, model), bf16),
        pltpu.VMEM((length, model), f32),
        pltpu.VMEM((owners, slot_rows, model), bf16),
        pltpu.VMEM((4, 2, 2, 2, rows, 2 * model), bf16),
        pltpu.VMEM((4, 2, 2, 2, rows, model), bf16),
        pltpu.VMEM((4, 2, 2, 2, rows, model), bf16),
        pltpu.VMEM((4, 2, 2, 2, rows, 3 * model), bf16),
        pltpu.VMEM((40, 128), f32),
        pltpu.VMEM((6, 40, 128), f32),
    ]
    chunks = 14
    dma = pltpu.SemaphoreType.DMA
    sems = [
        dma((10 * chunks,)),
        dma((10 * chunks,)),
        dma((4 * chunks,)),
        pltpu.SemaphoreType.REGULAR((4,)),
        dma((13,)),
        dma((6,)),
        dma((6,)),
        dma((owners - 1,)),
        dma((owners - 1,)),
    ]
    shapes = (
        [(out3_rows, model // 2)] * 2 + [(rows, ffn // 2)] * 4 + [(rows, model)] * 4
    )
    rooms = []
    for shape in shapes:
        for lead in ((4, 4), (4, 4), (2, 4), (4,), (3,)):
            rooms.append(pltpu.VMEM(lead + shape, bf16))
    far = pl.BlockSpec(memory_space=pl.ANY)
    near = pl.BlockSpec(memory_space=pltpu.VMEM)
    results = pl.pallas_call(
        functools.partial(backward_kernel, head_size, 2),
        out_shape=outs,
        in_specs=[far] * backward_far + [near] * (len(inputs) - backward_far),
        out_specs=[near] * (len(outs) - 1) + [far],
        scratch_shapes=own + sems + rooms,
        compiler_params=pltpu.CompilerParams(
            collective_id=2, has_side_effects=True, vmem_limit_bytes=63 * 1024 * 1024
        ),
    )(*inputs)
    return BackwardOut(*results)


def table_kernel(copies, ids_ref, rows_ref, *refs):
    sources, out_ref, targets = refs[:copies], refs[copies], refs[copies + 1:2 * copies + 1]
    rooms, sems = refs[2 * copies + 1:3 * copies + 1], refs[3 * copies + 1:]
    step = pl.program_id(0)

    def moves(inward):
        return [
            pltpu.make_async_copy(source, room, sems[0].at[k])
            if inward
            else pltpu.make_async_copy(room, target, sems[0].at[k])
            for k, (source, room, target) in enumerate(zip(sources, rooms, targets))
        ]

    if copies:

        @pl.when(step == 0)
        def enter():
            for copy in moves(True):
                copy.start()

        @pl.when(step == 1)
        def turn():
            for copy in moves(True):
                copy.wait()
            for copy in moves(False):
                copy.start()

        @pl.when(step == pl.num_programs(0) - 1)
        def leave():
            for copy in moves(False):
                copy.wait()

    block = out_ref.shape[0]
    row = lax.broadcasted_iota(jnp.int32, (block, ids_ref.shape[1]), 0)
    hits = jnp.where(row == ids_ref[...] - step * block, 1.0, 0.0).astype(bf16)
    out_ref[...] = matmul(hits, rows_ref[...])


def table_and_copies(requests, returned, shard_rows, copies):
    slots, model = returned.shape
    block = min(1024, -(-shard_rows // 16) * 8)
    whole = lambda value: pl.BlockSpec(value.shape, lambda i: (0,) * value.ndim)
    far = pl.BlockSpec(memory_space=pltpu.HBM)
    results = pl.pallas_call(
        functools.partial(table_kernel, len(copies)),
        grid=(-(-shard_rows // block),),
        out_shape=[jax.ShapeDtypeStruct((shard_rows, model), f32)]
        + [jax.ShapeDtypeStruct(value.shape, value.dtype) for value in copies],
        in_specs=[whole(requests), whole(returned)] + [far] * len(copies),
        out_specs=[pl.BlockSpec((block, model), lambda i: (i, 0))] + [far] * len(copies),
        scratch_shapes=[pltpu.VMEM(value.shape, value.dtype) for value in copies]
        + [pltpu.SemaphoreType.DMA((len(copies),))] * bool(copies),
        compiler_params=pltpu.CompilerParams(vmem_limit_bytes=63 * 1024 * 1024),
        cost_estimate=pl.CostEstimate(
            flops=2 * shard_rows * slots * model,
            bytes_accessed=4 * shard_rows * model,
            transcendentals=0,
        ),
    )(requests, returned, *copies)
    return results[0], results[1:]


def body(
    target_ids,
    target_lengths,
    bucket_table,
    memory,
    table,
    self_qkv,
    self_out,
    cross_q,
    cross_kv,
    cross_out,
    ffn_in,
    ffn_out,
    gains,
    relative_bias,
    cotangent,
):
    pair_count, seq_len = target_ids.shape
    model_width = table.shape[1]
    bucket_count, head_count = relative_bias.shape
    head_size = model_width // head_count
    memory_len = memory.shape[1]
    wide_count = lax.axis_size("wide")
    narrow_count = lax.axis_size("narrow")
    owner_count = wide_count * narrow_count
    special = wide_count == 8 and narrow_count == 4
    ffn_width = ffn_out.shape[0] * owner_count // model_width
    token_count = pair_count * seq_len
    shard_rows = table.shape[0]
    capacity = max(2, (2 * token_count + owner_count - 1) // owner_count)
    room = -(-capacity // 16) * 16 if special else capacity
    slots = owner_count * room

    shards = [
        cross_kv.reshape(-1, 2 * model_width),
        self_qkv.reshape(-1, 3 * model_width),
        self_out.reshape(-1, model_width),
        cross_q.reshape(-1, model_width),
        cross_out.reshape(-1, model_width),
        *jnp.split(ffn_in.reshape(-1, 2 * ffn_width), 2, axis=1),
        ffn_out.reshape(-1, model_width),
    ]
    positions = jnp.arange(seq_len, dtype=jnp.int32)
    valid_flat = (positions[:, None] < target_lengths[0]).astype(f32)
    bucket_hits = (
        bucket_table[:, None] == jnp.arange(bucket_count, dtype=jnp.int32)[None, :]
    ).astype(f32)
    bias_rows = jnp.dot(relative_bias.T, bucket_hits.T, precision=top_precision).reshape(
        head_count // 2, 1, 2 * seq_len
    )

    flat_ids = target_ids.reshape(token_count)
    owner_index = flat_ids // shard_rows
    owner_hits = (owner_index[:, None] == jnp.arange(owner_count, dtype=jnp.int32)[None, :]).astype(
        jnp.int32
    )
    rank_within = jnp.sum(jnp.cumsum(owner_hits, axis=0) * owner_hits, axis=1) - 1
    slot_index = owner_index * room + rank_within
    slot_hits = slot_index[:, None] == jnp.arange(slots, dtype=jnp.int32)[None, :]
    outgoing = (
        jnp.sum(
            jnp.where(slot_hits, (flat_ids - owner_index * shard_rows + 1)[:, None], 0), axis=0
        )
        - 1
    )
    slot_pick = (slot_hits & (valid_flat > 0.0)).astype(bf16)
    memory_rows = memory.reshape(memory_len, model_width)
    if special:
        main_rows = shard_rows // 16 * 16
        weights, done = forward_with_gather(
            ForwardIn(
                outgoing=jnp.broadcast_to(outgoing[:, None], (slots, 128)).reshape(
                    owner_count, room, 128
                ),
                pick=slot_pick,
                bias=bias_rows,
                keep=valid_flat,
                gains=gains,
                tail=jnp.pad(table[main_rows:], ((0, 16 - shard_rows % 16), (0, 0))),
                table=table,
                memory=memory_rows,
            ),
            shards,
            head_size,
        )
        requests = done.requests[:, :, 0]
        w_kv2, w_qkv, w_out1, w_q2, w_out2, w_gate, w_upper, w_out3 = weights
        key_values, cross_probs = done.key_values, done.cross_probs
        embedded, self_normalized = done.embedded, done.normed1
        merged, self_probs, self_mixed = done.merged, done.self_probs, done.mixed1
        after_self, normed_cross = done.after_self, done.normed2
        cross_queries, cross_mixed = done.queries, done.mixed2
        after_cross, normed_ffn = done.after_cross, done.normed3
    else:
        w_kv2, w_qkv, w_out1, w_q2, w_out2, w_gate, w_upper, w_out3 = [
            lax.all_gather(shard, axes, axis=0, tiled=True) for shard in shards
        ]
        requests = lax.all_to_all(
            lax.all_to_all(
                outgoing.reshape(wide_count, narrow_count, room),
                "wide",
                split_axis=0,
                concat_axis=0,
                tiled=True,
            ),
            "narrow",
            split_axis=1,
            concat_axis=1,
            tiled=True,
        )
        found = table[jnp.maximum(requests, 0)]
        arrived = lax.all_to_all(
            lax.all_to_all(found, "wide", split_axis=0, concat_axis=0, tiled=True),
            "narrow",
            split_axis=1,
            concat_axis=1,
            tiled=True,
        ).reshape(slots, model_width)
        embedded = matmul(slot_pick, arrived)
        key_values = matmul(memory_rows, w_kv2).astype(bf16)
        self_normalized = rms_scaled(embedded, gains[0]).astype(bf16)
        merged = matmul(self_normalized, w_qkv).astype(bf16)
        self_mixed, self_probs = self_forward(merged, bias_rows, valid_flat, head_size)
        after_self = embedded + matmul(self_mixed, w_out1)
        normed_cross = rms_scaled(after_self, gains[1]).astype(bf16)
        cross_queries = matmul(normed_cross, w_q2).astype(bf16)
        cross_mixed, cross_probs = cross_forward(cross_queries, key_values, head_size)
        after_cross = after_self + matmul(cross_mixed, w_out2)
        normed_ffn = rms_scaled(after_cross, gains[2]).astype(bf16)
    gate, upper = matmul(normed_ffn, w_gate), matmul(normed_ffn, w_upper)
    activated = gated(gate, upper).astype(bf16)
    hidden = (after_cross + matmul(activated, w_out3)) * valid_flat

    upstream = cotangent.reshape(token_count, model_width) * valid_flat
    grad_branch3 = upstream.astype(bf16)
    share_out3 = outer_sum(activated, grad_branch3).astype(bf16)
    grad_act = back_product(grad_branch3, w_out3)
    unused, gate_pull = jax.vjp(gated, gate, upper)
    grad_gate, grad_upper = [part.astype(bf16) for part in gate_pull(grad_act)]
    share_gate = outer_sum(normed_ffn, grad_gate).astype(bf16)
    share_upper = outer_sum(normed_ffn, grad_upper).astype(bf16)
    grad_normed3 = back_product(grad_gate, w_gate) + back_product(grad_upper, w_upper)
    grad_cross_state, grad_gain3 = norm_backward(after_cross, gains[2], grad_normed3)
    grad_cross_state = grad_cross_state + upstream

    grad_branch2 = grad_cross_state.astype(bf16)
    share_out2 = outer_sum(cross_mixed, grad_branch2).astype(bf16)
    grad_cross_mixed = back_product(grad_branch2, w_out2).astype(bf16)
    if special:
        sums = backward_with_sums(
            BackwardIn(
                share_out3=share_out3,
                share_gate=share_gate,
                share_upper=share_upper,
                share_out2=share_out2,
                key_values=key_values,
                cross_probs=cross_probs,
                memory=memory_rows,
                w_q2=w_q2,
                w_out1=w_out1,
                w_qkv=w_qkv,
                w_kv2=w_kv2,
                queries=cross_queries,
                grad_cross=grad_cross_mixed,
                normed2=normed_cross,
                after_self=after_self,
                grad_state=grad_cross_state,
                mixed1=self_mixed,
                merged=merged,
                self_probs=self_probs,
                normed1=self_normalized,
                embedded=embedded,
                gains=gains,
                pick=slot_pick,
                gain3=grad_gain3[None, :],
            ),
            head_size,
            room,
        )
        table_grad, copied = table_and_copies(
            requests.reshape(1, slots),
            sums.returned.reshape(slots, model_width),
            shard_rows,
            [*sums[:7], sums.memory_grad],
        )
        weight_sums, memory_grad = [value.reshape(-1) for value in copied[:7]], copied[7]
        small_sum = sums.small.reshape(-1)
        gain_sums = small_sum[:3 * model_width].reshape(3, model_width)
        distance_sums = small_sum[3 * model_width:3 * model_width + head_count * seq_len]
    else:
        grad_cross_q, grad_kv = cross_backward(
            cross_queries, key_values, cross_probs, grad_cross_mixed, head_size
        )
        grad_normed2 = back_product(grad_cross_q, w_q2)
        grad_self_state, grad_gain2 = norm_backward(after_self, gains[1], grad_normed2)
        grad_self_state = grad_self_state + grad_cross_state
        grad_branch1 = grad_self_state.astype(bf16)
        grad_self_mixed = back_product(grad_branch1, w_out1).astype(bf16)
        grad_joined, grad_distance = self_backward(merged, self_probs, grad_self_mixed, head_size)
        grad_first_normalized = back_product(grad_joined, w_qkv)
        grad_embedded, grad_gain1 = norm_backward(embedded, gains[0], grad_first_normalized)
        row_grads = (grad_embedded + grad_self_state).astype(bf16)
        slot_grads = outer_sum(slot_pick, row_grads).astype(bf16)
        returned = lax.all_to_all(
            lax.all_to_all(
                slot_grads.reshape(wide_count, narrow_count, room, model_width),
                "wide",
                split_axis=0,
                concat_axis=0,
                tiled=True,
            ),
            "narrow",
            split_axis=1,
            concat_axis=1,
            tiled=True,
        ).reshape(slots, model_width)
        table_grad, unused = table_and_copies(
            requests.reshape(1, slots), returned, shard_rows, []
        )
        memory_grad = back_product(grad_kv, w_kv2).astype(bf16)
        shares = (
            outer_sum(self_normalized, grad_joined).astype(bf16),
            outer_sum(self_mixed, grad_branch1).astype(bf16),
            outer_sum(normed_cross, grad_cross_q).astype(bf16),
            outer_sum(memory_rows, grad_kv).astype(bf16),
            share_out2,
            jnp.concatenate([share_gate, share_upper], axis=1),
            share_out3,
        )
        weight_sums = [
            lax.psum_scatter(share, axes, scatter_dimension=0, tiled=True)
            .astype(f32)
            .reshape(-1)
            for share in shares
        ]
        gain_sums, distance_sums = lax.psum(
            (jnp.stack([grad_gain1, grad_gain2, grad_gain3]), grad_distance.reshape(-1)), axes
        )

    bias_sums = jnp.dot(
        bucket_hits.T, distance_sums.reshape(head_count, seq_len).T, precision=top_precision
    )
    return (
        hidden.reshape(pair_count, seq_len, model_width),
        memory_grad.reshape(pair_count, memory_len, model_width),
        table_grad,
        *weight_sums,
        gain_sums,
        bias_sums,
    )


def solution(mesh):
    split = P(axes)
    return jax.shard_map(
        body,
        mesh=mesh,
        in_specs=(
            P(axes, None),
            split,
            P(),
            P(axes, None, None),
            P(axes, None),
            split,
            split,
            split,
            split,
            split,
            split,
            split,
            P(),
            P(),
            P(axes, None, None),
        ),
        out_specs=(
            P(axes, None, None),
            P(axes, None, None),
            P(axes, None),
            split,
            split,
            split,
            split,
            split,
            split,
            split,
            P(),
            P(),
        ),
        check_vma=False,
    )
```

```python
import functools
from typing import NamedTuple

import jax
import jax.numpy as jnp
import numpy as np
from jax import lax
from jax.experimental import pallas as pl
from jax.experimental.pallas import tpu as pltpu
from jax.sharding import PartitionSpec as P

epsilon = 1e-06
blocked = -1e30
top_precision = lax.Precision.HIGHEST
axes = ("wide", "narrow")
bf16 = jnp.bfloat16
f32 = jnp.float32


def rms_scaled(inputs, gain):
    return inputs * lax.rsqrt(jnp.mean(inputs * inputs, axis=-1, keepdims=True) + epsilon) * gain


def norm_backward(inputs, gain, upstream):
    unused, pullback = jax.vjp(rms_scaled, inputs, gain)
    return pullback(upstream)


def gated(gate, upper):
    return jax.nn.gelu(gate, approximate=True) * upper


def matmul(left, right):
    return jnp.dot(left, right, preferred_element_type=f32)


def outer_sum(left, right):
    return lax.dot_general(left, right, (((0,), (0,)), ((), ())), preferred_element_type=f32)


def back_product(left, right):
    return lax.dot_general(left, right, (((1,), (1,)), ((), ())), preferred_element_type=f32)


mesh_ids = pl.DeviceIdType.MESH
roomy = pltpu.CompilerParams(vmem_limit_bytes=48 * 1024 * 1024)


def standing():
    wide, narrow = lax.axis_index("wide"), lax.axis_index("narrow")
    return wide // 2, wide % 2, narrow // 2, narrow % 2


def device_at(z, x, y, core):
    return (z * 2 + x, y * 2 + core)


def flips(x, y, core):
    far_x, far_y = 1 - x, 1 - y
    second = (x * (1 - core) + far_x * core, far_y * (1 - core) + y * core)
    first = (far_x * (1 - core) + x * core, y * (1 - core) + far_y * core)
    return ((x, y), second, first, (far_x, far_y))


def partners():
    z, x, y, core = standing()
    own, second, first, both = flips(x, y, core)
    along_z = [device_at((z + step) % 4, x, y, core) for step in (1, 2, 3)]
    return along_z, device_at(z, *second, core), device_at(z, *first, core), device_at(z, x, y, 1 - core)


def greet(devices):
    barrier = pltpu.get_barrier_semaphore()
    for device in devices:
        pl.semaphore_signal(barrier, inc=1, device_id=device, device_id_type=mesh_ids)
    pl.semaphore_wait(barrier, len(devices))


def remote(source, target, send_sem, recv_sem, index, device):
    return pltpu.make_async_remote_copy(
        src_ref=source,
        dst_ref=target,
        send_sem=send_sem.at[index],
        recv_sem=recv_sem.at[index],
        device_id=device,
        device_id_type=mesh_ids,
    )


def spread_heads(pair, head_size):
    lane = lax.broadcasted_iota(jnp.int32, pair.shape, 1)
    zero = jnp.zeros_like(pair)
    return jnp.concatenate(
        [jnp.where(lane < head_size, pair, zero), jnp.where(lane >= head_size, pair, zero)], axis=0
    )


def join_heads(spread, head_size):
    turned = spread.T
    rows = turned.shape[0] // 2
    lane = lax.broadcasted_iota(jnp.int32, (rows, turned.shape[1]), 1)
    return jnp.where(lane < head_size, turned[:rows], turned[rows:])


def down_product(left, right):
    return lax.dot_general(left, right, (((0,), (0,)), ((), ())), preferred_element_type=f32)


def column_softmax(scores):
    peak = jnp.max(scores, axis=0, keepdims=True)
    exponent = jnp.exp(scores - peak)
    return exponent / jnp.sum(exponent, axis=0, keepdims=True)


def self_forward_kernel(head_size, q_ref, k_ref, v_ref, bias_ref, keep_ref, out_ref, prob_ref):
    scale = head_size ** (-0.5)
    scores = back_product(k_ref[...], spread_heads(q_ref[...], head_size)) * scale
    length, both = scores.shape
    row = lax.broadcasted_iota(jnp.int32, scores.shape, 0)
    lane = lax.broadcasted_iota(jnp.int32, scores.shape, 1)
    query = jnp.where(lane >= length, lane - length, lane)
    bias = pltpu.roll(
        jnp.broadcast_to(bias_ref[0], scores.shape), 0, 1, stride=1, stride_axis=0
    )
    scores = jnp.where((row <= query) & (keep_ref[...] > 0.0), scores + bias, blocked)
    probs = column_softmax(scores).astype(bf16)
    prob_ref[0] = probs
    out_ref[...] = join_heads(down_product(v_ref[...], probs), head_size).astype(bf16)


def self_backward_kernel(
    head_size, q_ref, k_ref, v_ref, prob_ref, grad_ref, out_ref, bias_ref
):
    scale = head_size ** (-0.5)
    pair = pl.program_id(0)
    width = 2 * head_size
    model = out_ref.shape[1] // 3
    grad = spread_heads(grad_ref[...], head_size)
    probs = prob_ref[0]
    wide_probs = probs.astype(f32)
    grad_probs = back_product(v_ref[...], grad)
    center = jnp.sum(grad_probs * wide_probs, axis=0, keepdims=True)
    grad_scores = (wide_probs * (grad_probs - center)).astype(bf16)
    grad_value = matmul(probs, grad)
    grad_key = matmul(grad_scores, spread_heads(q_ref[...], head_size)) * scale
    grad_query = join_heads(down_product(k_ref[...], grad_scores), head_size) * scale
    out_ref[:, pl.ds(pl.multiple_of(pair * width, width), width)] = grad_query.astype(bf16)
    out_ref[:, pl.ds(pl.multiple_of(model + pair * width, width), width)] = grad_key.astype(bf16)
    out_ref[:, pl.ds(pl.multiple_of(2 * model + pair * width, width), width)] = grad_value.astype(
        bf16
    )
    bias_ref[0] = fold_rows(grad_scores.astype(f32))


def cross_forward_kernel(head_size, q_ref, k_ref, v_ref, out_ref, prob_ref):
    scale = head_size ** (-0.5)
    scores = back_product(k_ref[...], spread_heads(q_ref[...], head_size)) * scale
    probs = column_softmax(scores).astype(bf16)
    prob_ref[0] = probs
    out_ref[...] = join_heads(down_product(v_ref[...], probs), head_size).astype(bf16)


def cross_backward_kernel(head_size, q_ref, k_ref, v_ref, prob_ref, grad_ref, out_ref, kv_ref):
    scale = head_size ** (-0.5)
    pair = pl.program_id(0)
    width = 2 * head_size
    model = kv_ref.shape[1] // 2
    grad = spread_heads(grad_ref[...], head_size)
    probs = prob_ref[0]
    wide_probs = probs.astype(f32)
    grad_probs = back_product(v_ref[...], grad)
    center = jnp.sum(grad_probs * wide_probs, axis=0, keepdims=True)
    grad_scores = (wide_probs * (grad_probs - center)).astype(bf16)
    grad_value = matmul(probs, grad)
    grad_key = matmul(grad_scores, spread_heads(q_ref[...], head_size)) * scale
    grad_query = join_heads(down_product(k_ref[...], grad_scores), head_size) * scale
    out_ref[...] = grad_query.astype(bf16)
    kv_ref[:, pl.ds(pl.multiple_of(pair * width, width), width)] = grad_key.astype(bf16)
    kv_ref[:, pl.ds(pl.multiple_of(model + pair * width, width), width)] = grad_value.astype(bf16)


def self_forward(merged, bias_rows, keep_rows, head_size):
    length, model = merged.shape[0], merged.shape[1] // 3
    width, pairs = 2 * head_size, model // (2 * head_size)
    both = 2 * length
    part = lambda offset: pl.BlockSpec((length, width), lambda p: (0, p + offset))
    return pl.pallas_call(
        functools.partial(self_forward_kernel, head_size),
        grid=(pairs,),
        out_shape=(
            jax.ShapeDtypeStruct((length, model), bf16),
            jax.ShapeDtypeStruct((pairs, length, both), bf16),
        ),
        in_specs=[
            part(0),
            part(pairs),
            part(2 * pairs),
            pl.BlockSpec((1, 1, both), lambda p: (p, 0, 0)),
            pl.BlockSpec((length, 1), lambda p: (0, 0)),
        ],
        out_specs=(part(0), pl.BlockSpec((1, length, both), lambda p: (p, 0, 0))),
        compiler_params=roomy,
        cost_estimate=pl.CostEstimate(flops=10**9, bytes_accessed=4 * 10**6, transcendentals=10**6),
    )(merged, merged, merged, bias_rows, keep_rows)


def self_backward(merged, probs, grad, head_size):
    length, model = grad.shape
    width, pairs = 2 * head_size, model // (2 * head_size)
    both = 2 * length
    part = lambda offset: pl.BlockSpec((length, width), lambda p: (0, p + offset))
    return pl.pallas_call(
        functools.partial(self_backward_kernel, head_size),
        grid=(pairs,),
        out_shape=(
            jax.ShapeDtypeStruct((length, 3 * model), bf16),
            jax.ShapeDtypeStruct((pairs, 1, both), f32),
        ),
        in_specs=[
            part(0),
            part(pairs),
            part(2 * pairs),
            pl.BlockSpec((1, length, both), lambda p: (p, 0, 0)),
            part(0),
        ],
        out_specs=(
            pl.BlockSpec((length, 3 * model), lambda p: (0, 0)),
            pl.BlockSpec((1, 1, both), lambda p: (p, 0, 0)),
        ),
        compiler_params=roomy,
        cost_estimate=pl.CostEstimate(flops=10**9, bytes_accessed=4 * 10**6, transcendentals=0),
    )(merged, merged, merged, probs, grad)


def cross_forward(queries, key_values, head_size):
    length, model = queries.shape
    memory_len = key_values.shape[0]
    width, pairs = 2 * head_size, model // (2 * head_size)
    both = 2 * length
    part = pl.BlockSpec((length, width), lambda p: (0, p))
    long_part = lambda offset: pl.BlockSpec((memory_len, width), lambda p: (0, p + offset))
    return pl.pallas_call(
        functools.partial(cross_forward_kernel, head_size),
        grid=(pairs,),
        out_shape=(
            jax.ShapeDtypeStruct((length, model), bf16),
            jax.ShapeDtypeStruct((pairs, memory_len, both), bf16),
        ),
        in_specs=[part, long_part(0), long_part(pairs)],
        out_specs=(part, pl.BlockSpec((1, memory_len, both), lambda p: (p, 0, 0))),
        compiler_params=roomy,
        cost_estimate=pl.CostEstimate(
            flops=4 * 10**9, bytes_accessed=13 * 10**6, transcendentals=4 * 10**6
        ),
    )(queries, key_values, key_values)


def cross_backward(queries, key_values, probs, grad, head_size):
    length, model = queries.shape
    memory_len = key_values.shape[0]
    width, pairs = 2 * head_size, model // (2 * head_size)
    both = 2 * length
    part = pl.BlockSpec((length, width), lambda p: (0, p))
    long_part = lambda offset: pl.BlockSpec((memory_len, width), lambda p: (0, p + offset))
    return pl.pallas_call(
        functools.partial(cross_backward_kernel, head_size),
        grid=(pairs,),
        out_shape=(
            jax.ShapeDtypeStruct((length, model), bf16),
            jax.ShapeDtypeStruct((memory_len, 2 * model), bf16),
        ),
        in_specs=[
            part,
            long_part(0),
            long_part(pairs),
            pl.BlockSpec((1, memory_len, both), lambda p: (p, 0, 0)),
            part,
        ],
        out_specs=(part, pl.BlockSpec((memory_len, 2 * model), lambda p: (0, 0))),
        compiler_params=roomy,
        cost_estimate=pl.CostEstimate(
            flops=8 * 10**9, bytes_accessed=18 * 10**6, transcendentals=0
        ),
    )(queries, key_values, key_values, probs, grad)


class Gather:
    def __init__(self, send_sem, recv_sem, own_sem):
        self.z, self.x, self.y, self.core = standing()
        self.sets = flips(self.x, self.y, self.core)
        self.along_z, self.second, self.first, self.sibling = partners()
        self.send_sem, self.recv_sem, self.own_sem = send_sem, recv_sem, own_sem
        self.chunks, self.flying, self.own, self.clock, self.after = [], {}, {}, 0, {}

    def add(self, shard, out, after=None):
        chunk = len(self.chunks)
        self.chunks.append((shard, out))
        self.after[chunk] = after
        own = pltpu.make_async_copy(
            shard, out.at[self.z, self.x, self.y, self.core], self.own_sem.at[chunk]
        )
        own.start()
        self.own[chunk] = own
        return chunk

    def copies(self, number, chunk):
        base = chunk * 10
        shard, out = self.chunks[chunk]
        if number == 0:
            return [
                remote(
                    shard,
                    out.at[self.z, self.x, self.y, self.core],
                    self.send_sem,
                    self.recv_sem,
                    base + k,
                    device,
                )
                for k, device in enumerate(self.along_z)
            ]
        piece = lambda k: out.at[:, self.sets[k][0], self.sets[k][1], self.core]
        device = (self.second, self.first, self.sibling)[number - 1]
        amount = (1, 2, 4)[number - 1]
        return [
            remote(piece(k), piece(k), self.send_sem, self.recv_sem, base + 2 + amount + k, device)
            for k in range(amount)
        ]

    def pump(self, spacing, steps=1):
        for unused in range(steps):
            for number in (4, 3, 2, 1, 0):
                chunk = self.clock - number * spacing
                if 0 <= chunk < len(self.chunks):
                    if number == 1:
                        self.own[chunk].wait()
                    if number > 0:
                        for copy in self.flying[number - 1, chunk]:
                            copy.wait_recv()
                    if number < 4:
                        self.flying[number, chunk] = self.copies(number, chunk)
                        for copy in self.flying[number, chunk]:
                            copy.start()
                    elif self.after[chunk] is not None:
                        self.after[chunk]()
            self.clock += 1

    def until(self, spacing, chunk):
        while self.clock <= chunk + 4 * spacing:
            self.pump(spacing)

    def finish(self):
        for copies in self.flying.values():
            for copy in copies:
                copy.wait_send()


def rms_rounded(rows, gain):
    turn = lax.rsqrt(jnp.mean(rows * rows, axis=-1, keepdims=True) + epsilon)
    return (rows * turn * gain).astype(bf16)


class Weights(NamedTuple):
    w_kv2: object
    w_qkv: object
    w_out1: object
    w_q2: object
    w_out2: object
    w_gate: object
    w_upper: object
    w_out3: object


class ForwardIn(NamedTuple):
    flat_kv2: object
    flat_qkv: object
    flat_out1: object
    flat_q2: object
    flat_out2: object
    flat_in: object
    flat_out3: object
    ids_row: object
    keep: object
    buckets: object
    relative: object
    gains: object
    tail: object
    table: object
    memory: object


class ForwardOut(NamedTuple):
    key_values: object
    cross_probs: object
    wanted: object
    pick: object
    embedded: object
    normed1: object
    merged: object
    self_probs: object
    mixed1: object
    after_self: object
    normed2: object
    queries: object
    mixed2: object
    after_cross: object
    normed3: object


class ForwardRefs(NamedTuple):
    flat_kv2: object
    flat_qkv: object
    flat_out1: object
    flat_q2: object
    flat_out2: object
    flat_in: object
    flat_out3: object
    ids_row: object
    keep: object
    buckets: object
    relative: object
    gains: object
    tail: object
    table: object
    memory: object
    key_values: object
    cross_probs: object
    wanted: object
    pick: object
    embedded: object
    normed1: object
    merged: object
    self_probs: object
    mixed1: object
    after_self: object
    normed2: object
    queries: object
    mixed2: object
    after_cross: object
    normed3: object
    wide_v: object
    bias_v: object
    p_kv2: object
    p_qkv: object
    p_out1: object
    p_q2: object
    p_out2: object
    p_gate: object
    p_upper: object
    p_out3: object
    outgoing: object
    requests: object
    kv2_v: object
    qkv_v: object
    out1_v: object
    q2_v: object
    out2_v: object
    memory_v: object
    kv_v: object
    table_v: object
    last_v: object
    found_f: object
    found_v: object
    arrived: object
    s_v: object
    p_v: object
    send: object
    recv: object
    own: object
    fetch: object
    id_send: object
    id_recv: object
    row_send: object
    row_recv: object


def every_other(me, owners, action):
    def one(step, unused):
        action(step, (me + step) % owners)
        return unused

    lax.fori_loop(1, owners, one, 0)


def forward_kernel(head_size, spacing, *refs):
    count = len(Weights._fields)
    inputs = len(ForwardIn._fields)
    whole = refs[inputs:inputs + count]
    at = ForwardRefs(*refs[:inputs], *refs[inputs + count:])
    shards = (
        at.p_kv2,
        at.p_qkv,
        at.p_out1,
        at.p_q2,
        at.p_out2,
        at.p_gate,
        at.p_upper,
        at.p_out3,
    )
    scale = head_size ** (-0.5)
    width = 2 * head_size
    length, model = at.embedded.shape
    memory_len = at.memory.shape[0]
    pairs = model // width
    both = 2 * length
    owners = 32
    me = lax.axis_index("wide") * 4 + lax.axis_index("narrow")
    place_of = lambda other: (other // 4, other % 4)

    def fetch(index, source, target):
        copy = pltpu.make_async_copy(source, target, at.fetch.at[index])
        copy.start()
        return copy

    block = at.table_v.shape[1]
    blocks = at.table.shape[0] // block
    rest = (at.table.shape[0] - blocks * block) // 16 * 16
    get_table = {}
    table_block = lambda k: fetch(
        k, at.table.at[pl.ds(k * block, block), :], at.table_v.at[k % 3]
    )
    for k in range(3):
        get_table[k] = table_block(k)
    get_last = fetch(
        16, at.table.at[pl.ds(blocks * block, rest), :], at.last_v.at[0:rest, :]
    )
    get_memory = fetch(17, at.memory, at.memory_v)

    barrier = pltpu.get_barrier_semaphore()
    every_other(
        me,
        owners,
        lambda step, other: pl.semaphore_signal(
            barrier, inc=1, device_id=place_of(other), device_id_type=mesh_ids
        ),
    )

    first = 0
    for flat, group in zip(
        refs[:7],
        (shards[:1], shards[1:2], shards[2:3], shards[3:4], shards[4:5], shards[5:7], shards[7:]),
    ):
        at.wide_v[first:first + flat.shape[0], :] = flat[...].astype(f32)
        stride = sum(shard.shape[1] for shard in group) // 128
        number = 0
        for shard in group:
            for start in range(0, shard.shape[1], 128):
                shard[:, start:start + 128] = at.wide_v[
                    pl.ds(first + number, shard.shape[0], stride), :
                ].astype(bf16)
                number += 1
        first += flat.shape[0]

    room = at.outgoing.shape[1]
    slots = owners * room
    shard_rows = float(at.table.shape[0])
    ids_row = at.ids_row[...].astype(f32)

    def numbers(shape, dim):
        return lax.broadcasted_iota(jnp.int32, shape, dim).astype(f32)

    def total(hits, dim):
        return jnp.sum(jnp.where(hits, 1.0, 0.0), axis=dim, keepdims=True)

    token, other_token = numbers((length, length), 0), numbers((length, length), 1)
    ids_column = jnp.sum(jnp.where(token == other_token, ids_row, 0.0), axis=1, keepdims=True)
    owner_column = total(ids_column >= (numbers((length, 128), 1) + 1.0) * shard_rows, 1)
    owner_row = total(ids_row >= (numbers((owners, length), 0) + 1.0) * shard_rows, 0)
    same = owner_column == owner_row
    slot_column = owner_column * room + total(same & (other_token < token), 1)
    slot_row = owner_row * room + total(same & (token < other_token), 0)
    at.pick[...] = jnp.where(
        (numbers((length, slots), 1) == slot_column) & (at.keep[...] > 0.0), 1.0, 0.0
    ).astype(bf16)
    local_row = jnp.max(
        jnp.where(
            numbers((slots, length), 0) == slot_row, ids_row - owner_row * shard_rows, -1.0
        ),
        axis=1,
        keepdims=True,
    )
    at.outgoing[...] = jnp.broadcast_to(local_row, (slots, 128)).reshape(owners, room, 128)
    buckets = at.buckets[...].astype(f32) == numbers((at.relative.shape[0], length), 0)
    for head in range(2 * pairs):
        row = jnp.sum(
            jnp.where(buckets, at.relative[:, head:head + 1], 0.0), axis=0, keepdims=True
        )
        start = head % 2 * length
        at.bias_v[head // 2, :, start:start + length] = row
    pl.semaphore_wait(barrier, owners - 1)

    id_copy = lambda step, other: remote(
        at.outgoing.at[other],
        at.requests.at[me],
        at.id_send,
        at.id_recv,
        step - 1,
        place_of(other),
    )
    every_other(me, owners, lambda step, other: id_copy(step, other).start())

    gather = Gather(at.send, at.recv, at.own)
    got = {}
    order = {}

    def add(index, part, parts, kept=None):
        size = shards[index].shape[1] // parts
        lanes = pl.ds(part * size, size)
        out = whole[index].at[:, :, :, :, :, lanes]
        after = None
        chunk = len(gather.chunks)
        if kept is not None:

            def after():
                got[chunk] = fetch(18 + chunk, out, kept.at[:, :, :, :, :, lanes])

        gather.add(shards[index].at[:, lanes], out, after)
        order[index, part] = chunk

    for part in range(2):
        add(0, part, 2, at.kv2_v)
    for part in range(3):
        add(1, part, 3, at.qkv_v)
    add(2, 0, 1, at.out1_v)
    add(3, 0, 1, at.q2_v)
    add(4, 0, 1, at.out2_v)
    for index in (5, 6, 7):
        for part in range(2):
            add(index, part, 2)

    def ready(index, part):
        chunk = order[index, part]
        gather.until(spacing, chunk)
        if chunk in got:
            got.pop(chunk).wait()

    def weight(kept, start, size):
        return kept[:, :, :, :, :, start:start + size].reshape(model, size)

    gather.pump(spacing)
    at.requests[me] = at.outgoing[me]
    at.last_v[rest:, :] = jnp.zeros_like(at.last_v[rest:, :])
    at.last_v[rest:rest + at.tail.shape[0], :] = at.tail[...]
    gather.pump(spacing)
    every_other(me, owners, lambda step, other: id_copy(step, other).wait())

    wanted = at.requests[...].reshape(slots, 128)
    at.wanted[...] = wanted.T[0:8, :]

    def hits(start, size):
        offset = at.requests[...].reshape(slots, 128) - numbers((slots, 128), 1)
        return jnp.concatenate(
            [
                jnp.where(offset == float(start + column), 1.0, 0.0).astype(bf16)
                for column in range(0, size, 128)
            ],
            axis=1,
        )

    get_last.wait()
    at.found_f[...] = matmul(hits(blocks * block, at.last_v.shape[0]), at.last_v[...])
    for k in range(blocks):
        get_table[k].wait()
        at.found_f[...] += matmul(hits(k * block, block), at.table_v[k % 3])
        if k + 3 < blocks:
            get_table[k + 3] = table_block(k + 3)
        if k % 3 == 2:
            gather.pump(spacing)
    at.found_v[...] = at.found_f[...].astype(bf16).reshape(at.found_v.shape)
    at.arrived[me] = at.found_v[me]
    row_copy = lambda step, other: remote(
        at.found_v.at[other],
        at.arrived.at[me],
        at.row_send,
        at.row_recv,
        step - 1,
        place_of(other),
    )
    every_other(me, owners, lambda step, other: row_copy(step, other).start())
    gather.pump(spacing)

    get_memory.wait()
    put_kv = []
    tile = 256
    for part in range(2):
        ready(0, part)
        for start in range(part * model, (part + 1) * model, tile):
            columns = weight(at.kv2_v, start, tile)
            for row in range(0, memory_len, 512):
                at.kv_v[row:row + 512, start:start + tile] = matmul(
                    at.memory_v[row:row + 512, :], columns
                ).astype(bf16)
        lanes = pl.ds(part * model, model)
        put_kv.append(fetch(32 + part, at.kv_v.at[:, lanes], at.key_values.at[:, lanes]))
        gather.pump(spacing)

    every_other(me, owners, lambda step, other: row_copy(step, other).wait())
    embedded = matmul(at.pick[...], at.arrived[...].reshape(slots, model))
    at.embedded[...] = embedded
    at.normed1[...] = rms_rounded(embedded, at.gains[0:1, :])
    for part in range(3):
        ready(1, part)
        for start in range(part * model, (part + 1) * model, tile):
            at.merged[:, start:start + tile] = matmul(
                at.normed1[...], weight(at.qkv_v, start, tile)
            ).astype(bf16)
    row = lax.broadcasted_iota(jnp.int32, (length, both), 0)
    lane = lax.broadcasted_iota(jnp.int32, (length, both), 1)
    query_row = jnp.where(lane >= length, lane - length, lane)
    seen = (row <= query_row) & (at.keep[...] > 0.0)
    for pair in range(pairs):
        lanes = slice(pair * width, (pair + 1) * width)
        key_lanes = slice(model + pair * width, model + (pair + 1) * width)
        value_lanes = slice(2 * model + pair * width, 2 * model + (pair + 1) * width)
        query = spread_heads(at.merged[:, lanes], head_size)
        scores = back_product(at.merged[:, key_lanes], query) * scale
        bias = pltpu.roll(
            jnp.broadcast_to(at.bias_v[pair], scores.shape), 0, 1, stride=1, stride_axis=0
        )
        probs = column_softmax(jnp.where(seen, scores + bias, blocked)).astype(bf16)
        at.self_probs[pair] = probs
        turned = down_product(at.merged[:, value_lanes], probs)
        at.mixed1[:, lanes] = join_heads(turned, head_size).astype(bf16)
        if pair % 2 == 1:
            gather.pump(spacing)
    ready(2, 0)
    for start in range(0, model, tile):
        at.after_self[:, start:start + tile] = at.embedded[:, start:start + tile] + matmul(
            at.mixed1[...], weight(at.out1_v, start, tile)
        )
    at.normed2[...] = rms_rounded(at.after_self[...], at.gains[1:2, :])
    ready(3, 0)
    for start in range(0, model, tile):
        at.queries[:, start:start + tile] = matmul(
            at.normed2[...], weight(at.q2_v, start, tile)
        ).astype(bf16)
    tiles = memory_len // tile
    put_probs = {}
    for pair in range(pairs):
        lanes = slice(pair * width, (pair + 1) * width)
        value_lanes = slice(model + pair * width, model + (pair + 1) * width)
        query = spread_heads(at.queries[:, lanes], head_size)
        if pair >= 2:
            put_probs[pair - 2].wait()
        probs = at.p_v.at[pair % 2]

        def score(index, peak):
            place = pl.ds(pl.multiple_of(index * tile, tile), tile)
            part = back_product(at.kv_v[place, lanes], query) * scale
            at.s_v[place, :] = part
            return jnp.maximum(peak, jnp.max(part.reshape(tile // 8, 8, both), axis=0))

        peak = lax.fori_loop(0, tiles, score, jnp.full((8, both), blocked, f32))
        peak = jnp.max(peak, axis=0, keepdims=True)

        def power(index, total):
            place = pl.ds(pl.multiple_of(index * tile, tile), tile)
            part = jnp.exp(at.s_v[place, :] - peak)
            at.s_v[place, :] = part
            return total + jnp.sum(part.reshape(tile // 8, 8, both), axis=0)

        total = lax.fori_loop(0, tiles, power, jnp.zeros((8, both), f32))
        share = 1.0 / jnp.sum(total, axis=0, keepdims=True)

        def normal(index, unused):
            place = pl.ds(pl.multiple_of(index * tile, tile), tile)
            probs[place, :] = (at.s_v[place, :] * share).astype(bf16)
            return unused

        lax.fori_loop(0, tiles, normal, 0)
        put_probs[pair] = fetch(34 + pair, probs, at.cross_probs.at[pair])
        turned = down_product(at.kv_v[:, value_lanes], probs[...])
        at.mixed2[:, lanes] = join_heads(turned, head_size).astype(bf16)
        gather.pump(spacing)
    ready(4, 0)
    for start in range(0, model, tile):
        at.after_cross[:, start:start + tile] = at.after_self[
            :, start:start + tile
        ] + matmul(at.mixed2[...], weight(at.out2_v, start, tile))
    at.normed3[...] = rms_rounded(at.after_cross[...], at.gains[2:3, :])
    gather.until(spacing, len(gather.chunks) - 1)
    gather.finish()
    for copy in put_kv + [put_probs[pairs - 2], put_probs[pairs - 1]]:
        copy.wait()


def forward_with_gather(inputs, shapes, room, head_size):
    length = inputs.keep.shape[0]
    memory_len, model = inputs.memory.shape
    owners = 32
    slots = owners * room
    pairs = model // (2 * head_size)
    both = 2 * length
    rows = model // owners
    struct = jax.ShapeDtypeStruct
    tokens = lambda columns, kind: struct((length, columns), kind)
    far_outs = [struct((4, 2, 2, 2) + shape, bf16) for shape in shapes] + [
        struct((memory_len, 2 * model), bf16),
        struct((pairs, memory_len, both), bf16),
    ]
    near_outs = [
        struct((8, slots), f32),
        tokens(slots, bf16),
        tokens(model, f32),
        tokens(model, bf16),
        tokens(3 * model, bf16),
        struct((pairs, length, both), bf16),
        tokens(model, bf16),
        tokens(model, f32),
        tokens(model, bf16),
        tokens(model, bf16),
        tokens(model, bf16),
        tokens(model, f32),
        tokens(model, bf16),
    ]
    by_owner = lambda columns: pltpu.VMEM((4, 2, 2, 2, rows, columns), bf16)
    own = [
        pltpu.VMEM((sum(flat.shape[0] for flat in inputs[:7]), 128), f32),
        pltpu.VMEM((pairs, 1, both), f32),
    ]
    own += [pltpu.VMEM(shape, bf16) for shape in shapes]
    own += [pltpu.VMEM((owners, room, 128), f32)] * 2
    own += [
        by_owner(2 * model),
        by_owner(3 * model),
        by_owner(model),
        by_owner(model),
        by_owner(model),
        pltpu.VMEM((memory_len, model), bf16),
        pltpu.VMEM((memory_len, 2 * model), bf16),
        pltpu.VMEM((3, 512, model), bf16),
        pltpu.VMEM((256, model), bf16),
        pltpu.VMEM((slots, model), f32),
        pltpu.VMEM((owners, room, model), bf16),
        pltpu.VMEM((owners, room, model), bf16),
        pltpu.VMEM((memory_len, both), f32),
        pltpu.VMEM((2, memory_len, both), bf16),
    ]
    dma = pltpu.SemaphoreType.DMA
    chunks = 14
    others = owners - 1
    sems = [dma((size,)) for size in (10 * chunks, 10 * chunks, chunks, 40) + (others,) * 4]
    far = pl.BlockSpec(memory_space=pl.ANY)
    near = pl.BlockSpec(memory_space=pltpu.VMEM)
    results = pl.pallas_call(
        functools.partial(forward_kernel, head_size, 2),
        out_shape=far_outs + near_outs,
        in_specs=[near] * (len(inputs) - 2) + [far] * 2,
        out_specs=[far] * len(far_outs) + [near] * len(near_outs),
        scratch_shapes=own + sems,
        compiler_params=pltpu.CompilerParams(
            collective_id=1, has_side_effects=True, vmem_limit_bytes=63 * 1024 * 1024
        ),
    )(*inputs)
    count = len(shapes)
    weights = Weights(*[whole.reshape(-1, whole.shape[-1]) for whole in results[:count]])
    return weights, ForwardOut(*results[count:])


class Sums:
    def __init__(self, send_sem, recv_sem, free_sem, spacing):
        self.z, self.x, self.y, self.core = standing()
        self.sets = flips(self.x, self.y, self.core)
        self.sibling_sets = flips(self.x, self.y, 1 - self.core)
        self.along_z, self.second, self.first, self.sibling = partners()
        self.send_sem, self.recv_sem, self.free_sem = send_sem, recv_sem, free_sem
        self.spacing = spacing
        self.chunks, self.flying, self.starts, self.clock, self.ready = [], {}, [], 0, 0

    def add(self, source, buffers, out, stride, offset, frees=None, needs=None):
        self.chunks.append((source, buffers, out, stride, offset, frees, needs))

    def copies(self, number, chunk):
        source, (kept, from_first, from_second, from_z) = self.chunks[chunk][:2]
        others = self.sibling_sets
        base = 10 * chunk
        go = lambda start, end, index, device: remote(
            start, end, self.send_sem, self.recv_sem, base + index, device
        )
        if number == 0:
            return [
                go(
                    source.at[:, others[k][0], others[k][1], 1 - self.core],
                    kept.at[k],
                    k,
                    self.sibling,
                )
                for k in range(4)
            ]
        if number == 1:
            return [go(kept.at[2 + k], from_first.at[k], 4 + k, self.first) for k in range(2)]
        if number == 2:
            return [go(kept.at[1], from_second, 6, self.second)]
        return [
            go(kept.at[0, (self.z + k + 1) % 4], from_z.at[k], 7 + k, self.along_z[k])
            for k in range(3)
        ]

    def begin(self, number, chunk):
        needs = self.chunks[chunk][6]
        if number == 0 and needs is not None:
            pl.semaphore_wait(self.free_sem.at[needs], 6)
        self.flying[number, chunk] = self.copies(number, chunk)
        for copy in self.flying[number, chunk]:
            copy.start()

    def settle(self, number, chunk):
        source, buffers, out, stride, offset, frees, unused = self.chunks[chunk]
        kept, from_first, from_second, from_z = buffers
        for copy in self.flying[number, chunk]:
            copy.wait_recv()
            if number == 0:
                copy.wait_send()
        if number == 0:
            for k in (2, 3, 1, 0):
                own = source.at[:, self.sets[k][0], self.sets[k][1], self.core]
                add_into(kept.at[k], own)
        elif number == 1:
            for k in (1, 0):
                add_into(kept.at[k], from_first.at[k])
        elif number == 2:
            add_into(kept.at[0], from_second)
        else:
            total = kept[0, self.z].astype(f32)
            for k in range(3):
                total = total + from_z[k].astype(f32)
            rows, width = total.shape
            for tile in range(width // 128):
                out[pl.ds(offset + tile, rows, stride), :] = total[:, tile * 128:(tile + 1) * 128]
            for stage in range(1, 4):
                for copy in self.flying[stage, chunk]:
                    copy.wait_send()
            if frees is not None:
                for device in self.along_z + [self.second, self.first, self.sibling]:
                    pl.semaphore_signal(
                        self.free_sem.at[frees], inc=1, device_id=device, device_id_type=mesh_ids
                    )

    def pump(self, steps=1):
        for unused in range(steps):
            for chunk, start in enumerate(self.starts):
                number, odd = divmod(self.clock - start, self.spacing)
                if odd == 0 and number <= 4:
                    self.settle(number - 1, chunk)
                    if number < 4:
                        self.begin(number, chunk)
            following = len(self.starts)
            if following < self.ready:
                self.begin(0, following)
                self.starts.append(self.clock)
            self.clock += 1

    def finish(self):
        self.ready = len(self.chunks)
        while (
            len(self.starts) < len(self.chunks)
            or self.clock <= self.starts[-1] + 4 * self.spacing
        ):
            self.pump()


def add_into(target, source):
    def quarter(index, unused):
        target[index] = (target[index].astype(f32) + source[index].astype(f32)).astype(bf16)
        return unused

    lax.fori_loop(0, 4, quarter, 0)


def norm_back(rows, gain, upstream):
    turn = lax.rsqrt(jnp.mean(rows * rows, axis=-1, keepdims=True) + epsilon)
    scaled = gain * upstream
    inner = jnp.sum(scaled * rows, axis=-1, keepdims=True) / rows.shape[1]
    gain_grad = jnp.sum(upstream * rows * turn, axis=0, keepdims=True)
    return turn * scaled - rows * (turn * turn * turn * inner), gain_grad


def share_into(target, left, right, tile, turned=None):
    depth, model = left.shape
    rows, width = target.shape[4], right.shape[1]
    half = model // 2
    if turned is not None:
        for start in range(0, depth, 256):
            turned[:, start:start + 256] = left[start:start + 256, :].T
    for part in range(2):
        mine = slice(part * half, (part + 1) * half)
        upright = left[:, mine].T if turned is None else None
        for start in range(0, width, tile):
            place = slice(start, start + tile)
            product = matmul(turned[mine, :] if upright is None else upright, right[:, place])
            target[2 * part:2 * part + 2, :, :, :, :, place] = product.astype(bf16).reshape(
                2, 2, 2, 2, rows, tile
            )


def gelu_parts(gate):
    slope, cubic = (2.0 / np.pi) ** 0.5, 0.044715
    curve = jnp.tanh(slope * (gate + cubic * gate * gate * gate))
    rise = 0.5 * (1.0 + curve)
    steep = 0.5 * gate * (1.0 - curve * curve) * (slope * (1.0 + 3.0 * cubic * gate * gate))
    return gate * rise, rise + steep


def fold_rows(scores):
    both = scores.shape[1]
    while scores.shape[0] % 16 == 0:
        rows = scores.shape[0] // 2
        scores = scores[:rows] + pltpu.roll(scores[rows:], both - rows, 1)
    total = scores[:8]
    for start in range(8, scores.shape[0], 8):
        total = total + pltpu.roll(scores[start:start + 8], both - start, 1)
    row = lax.broadcasted_iota(jnp.int32, total.shape, 0)
    for bit in (1, 2, 4):
        total = jnp.where((row // bit) % 2 == 1, pltpu.roll(total, both - bit, 1), total)
    return jnp.sum(total, axis=0, keepdims=True)


class BackwardIn(NamedTuple):
    key_values: object
    cross_probs: object
    memory: object
    w_q2: object
    w_out1: object
    w_qkv: object
    w_kv2: object
    w_gate: object
    w_upper: object
    w_out3: object
    w_out2: object
    after_self: object
    embedded: object
    merged: object
    self_probs: object
    normed1: object
    normed2: object
    mixed1: object
    queries: object
    mixed2: object
    normed3: object
    after_cross: object
    cotangent: object
    keep: object
    gains: object
    pick: object


class BackwardOut(NamedTuple):
    qkv: object
    out1: object
    q2: object
    kv2: object
    out2: object
    ffn: object
    out3: object
    hidden: object
    small: object
    returned: object
    memory_grad: object


class BackwardRefs(NamedTuple):
    key_values: object
    cross_probs: object
    memory: object
    w_q2: object
    w_out1: object
    w_qkv: object
    w_kv2: object
    w_gate: object
    w_upper: object
    w_out3: object
    w_out2: object
    after_self: object
    embedded: object
    merged: object
    self_probs: object
    normed1: object
    normed2: object
    mixed1: object
    queries: object
    mixed2: object
    normed3: object
    after_cross: object
    cotangent: object
    keep: object
    gains: object
    pick: object
    qkv: object
    out1: object
    q2: object
    kv2: object
    out2: object
    ffn: object
    out3: object
    hidden: object
    small: object
    returned: object
    memory_grad: object
    kv_v: object
    dkv_v: object
    p_v: object
    wq2_v: object
    wo1_v: object
    wqkv_v: object
    turn_v: object
    ds_v: object
    dq_v: object
    dqkv_v: object
    do_v: object
    gc_v: object
    rows_v: object
    slots_v: object
    s_kv: object
    s_pair: object
    s_qkv: object
    s_out3: object
    s_out2: object
    gate_v: object
    upper_v: object
    u_v: object
    dgu_v: object
    sp_v: object
    small_v: object
    small_in: object
    send: object
    recv: object
    free: object
    fetch: object
    small_send: object
    small_recv: object
    slot_send: object
    slot_recv: object


backward_far = 18


def backward_kernel(head_size, spacing, *refs):
    names = len(BackwardRefs._fields)
    at = BackwardRefs(*refs[:names])
    buffers = refs[names:]
    groups = [buffers[4 * k:4 * k + 4] for k in range(len(buffers) // 4)]
    scale = head_size ** (-0.5)
    width = 2 * head_size
    length, model = at.queries.shape
    memory_len = at.kv_v.shape[0]
    ffn = at.u_v.shape[1]
    half_ffn = ffn // 2
    pairs = model // width
    both = 2 * length
    tile = 256
    owners = 32
    me = lax.axis_index("wide") * 4 + lax.axis_index("narrow")
    place_of = lambda other: (other // 4, other % 4)
    waiting = []

    def fetch(source, target):
        copy = pltpu.make_async_copy(source, target, at.fetch.at[len(waiting)])
        waiting.append(copy)
        copy.start()
        return copy

    get_gate = [
        fetch(
            at.w_gate.at[:, pl.ds(part * half_ffn, half_ffn)],
            at.kv_v.at[pl.ds(part * model, model), pl.ds(0, half_ffn)],
        )
        for part in range(2)
    ]
    get_upper = [
        fetch(
            at.w_upper.at[:, pl.ds(part * half_ffn, half_ffn)],
            at.dkv_v.at[pl.ds(part * model, model), pl.ds(0, half_ffn)],
        )
        for part in range(2)
    ]
    pieces = [
        at.turn_v.at[:, pl.ds(0, model)],
        at.turn_v.at[:, pl.ds(model, model)],
        at.wq2_v.at[pl.ds(0, ffn - 2 * model), :],
    ]
    get_out3 = [
        fetch(at.w_out3.at[pl.ds(k * model, piece.shape[0]), :], piece)
        for k, piece in enumerate(pieces)
    ]
    get_out2 = fetch(at.w_out2, at.wqkv_v.at[:, pl.ds(0, model)])
    get_out1 = fetch(at.w_out1, at.wo1_v)
    get_self = fetch(at.self_probs, at.sp_v)

    barrier = pltpu.get_barrier_semaphore()
    every_other(
        me,
        owners,
        lambda step, other: pl.semaphore_signal(
            barrier, inc=1, device_id=place_of(other), device_id_type=mesh_ids
        ),
    )
    pl.semaphore_wait(barrier, owners - 1)

    sums = Sums(at.send, at.recv, at.free, spacing)
    model_tiles = model // 128
    half_tiles = half_ffn // 128
    half_model = model // 2

    def columns(ref, start, size):
        return ref.at[:, :, :, :, :, pl.ds(start, size)]

    def narrowed(group, size):
        lanes = pl.ds(0, size)
        return (
            group[0].at[:, :, :, lanes],
            group[1].at[:, :, :, lanes],
            group[2].at[:, :, lanes],
            group[3].at[:, :, lanes],
        )

    for part in range(2):
        sums.add(
            columns(at.s_out3, part * half_model, half_model),
            groups[part],
            at.out3,
            model_tiles,
            part * model_tiles // 2,
        )
    ffn_sources = (
        columns(at.s_qkv, 0, half_ffn),
        columns(at.s_qkv, half_ffn, half_ffn),
        columns(at.s_kv, 0, half_ffn),
        columns(at.s_pair, 0, half_ffn),
    )
    for k, source in enumerate(ffn_sources):
        sums.add(source, groups[2 + k], at.ffn, 4 * half_tiles, k * half_tiles, frees=k)
    sums.add(at.s_out2, groups[6], at.out2, model_tiles, 0)
    for part in range(2):
        sums.add(
            columns(at.s_kv, part * model, model),
            groups[7 + part],
            at.kv2,
            2 * model_tiles,
            part * model_tiles,
        )
    sums.add(columns(at.s_pair, 0, model), groups[9], at.q2, model_tiles, 0)
    sums.add(
        columns(at.s_pair, model, model),
        narrowed(groups[2], model),
        at.out1,
        model_tiles,
        0,
        needs=0,
    )
    for part in range(3):
        sums.add(
            columns(at.s_qkv, part * model, model),
            narrowed(groups[3 + part], model),
            at.qkv,
            3 * model_tiles,
            part * model_tiles,
            needs=1 + part,
        )

    def half_of(ref, start):
        part, offset = divmod(start, half_ffn)
        return ref[part * model:(part + 1) * model, offset:offset + tile]

    for copy in get_gate + get_upper:
        copy.wait()
    for start in range(0, ffn, tile):
        lanes = slice(start, start + tile)
        gate = matmul(at.normed3[...], half_of(at.kv_v, start))
        upper = matmul(at.normed3[...], half_of(at.dkv_v, start))
        at.gate_v[:, lanes] = gate
        at.upper_v[:, lanes] = upper
        at.u_v[:, lanes] = (gelu_parts(gate)[0] * upper).astype(bf16)
    at.rows_v[...] = at.cotangent[...] * at.keep[...]
    at.do_v[...] = at.rows_v[...].astype(bf16)
    share_into(at.s_out3, at.u_v, at.do_v, tile)
    sums.ready = 2
    sums.pump(2)
    for copy in get_out3:
        copy.wait()
    for start in range(0, ffn, tile):
        lanes = slice(start, start + tile)
        piece, offset = divmod(start, model)
        grad = back_product(at.do_v[...], pieces[piece][offset:offset + tile, :])
        value, slope = gelu_parts(at.gate_v[:, lanes])
        at.dgu_v[:, lanes] = (grad * at.upper_v[:, lanes] * slope).astype(bf16)
        at.dgu_v[:, ffn + start:ffn + start + tile] = (grad * value).astype(bf16)
    sums.pump()
    share_into(
        columns(at.s_qkv, 0, ffn), at.normed3, at.dgu_v.at[:, pl.ds(0, ffn)], tile
    )
    sums.ready = 4
    sums.pump()
    for start in range(0, model, tile):
        lanes = slice(start, start + tile)
        total = at.after_cross[:, lanes]
        for k, piece in enumerate(pieces):
            total = total + matmul(
                at.u_v[:, k * model:k * model + piece.shape[0]], piece[:, lanes]
            )
        at.hidden[:, lanes] = total * at.keep[...]
    sums.pump()
    get_q2 = fetch(at.w_q2, at.wq2_v)
    get_normed2 = fetch(at.normed2, at.u_v.at[:, pl.ds(0, model)])
    get_after = fetch(at.after_self, at.gate_v.at[:, pl.ds(0, model)])
    get_embedded = fetch(at.embedded, at.upper_v.at[:, pl.ds(0, model)])
    upstream = jnp.zeros((length, model), f32)
    for k, ref in enumerate((at.kv_v, at.kv_v, at.dkv_v, at.dkv_v)):
        upstream = upstream + back_product(
            at.dgu_v[:, k * half_ffn:(k + 1) * half_ffn],
            ref[(k % 2) * model:(k % 2 + 1) * model, 0:half_ffn],
        )
    get_kv = fetch(at.key_values, at.kv_v)
    probs_at = lambda pair: fetch(at.cross_probs.at[pair], at.p_v.at[pair % 2])
    get_probs = {0: probs_at(0)}
    grad_rows, gain3 = norm_back(at.after_cross[...], at.gains[2:3, :], upstream)
    for part in range(6):
        at.small_v[12 + part:13 + part, :] = gain3[:, part * 128:(part + 1) * 128]
    at.rows_v[...] = at.rows_v[...] + grad_rows
    at.do_v[...] = at.rows_v[...].astype(bf16)
    get_out2.wait()
    at.gc_v[...] = back_product(at.do_v[...], at.wqkv_v[:, 0:model]).astype(bf16)
    get_qkv = fetch(at.w_qkv, at.wqkv_v)
    share_into(
        columns(at.s_kv, 0, half_ffn), at.normed3, at.dgu_v.at[:, pl.ds(ffn, half_ffn)], tile
    )
    sums.ready = 5
    sums.pump()
    share_into(
        columns(at.s_pair, 0, half_ffn),
        at.normed3,
        at.dgu_v.at[:, pl.ds(ffn + half_ffn, half_ffn)],
        tile,
    )
    get_merged = fetch(at.merged, at.dgu_v.at[:, pl.ds(0, 3 * model)])
    get_normed1 = fetch(at.normed1, at.dgu_v.at[:, pl.ds(3 * model, model)])
    get_mixed1 = fetch(at.mixed1, at.dgu_v.at[:, pl.ds(4 * model, model)])
    sums.ready = 6
    sums.pump()
    share_into(at.s_out2, at.mixed2, at.do_v, tile)
    sums.ready = 7
    sums.pump()

    get_kv.wait()
    tiles = memory_len // tile
    for pair in range(pairs):
        lanes = slice(pair * width, (pair + 1) * width)
        value_lanes = slice(model + pair * width, model + (pair + 1) * width)
        get_probs[pair].wait()
        if pair + 1 < pairs:
            get_probs[pair + 1] = probs_at(pair + 1)
        probs = at.p_v.at[pair % 2]
        grad = spread_heads(at.gc_v[:, lanes], head_size)
        query = spread_heads(at.queries[:, lanes], head_size)

        def first_pass(index, center):
            place = pl.ds(pl.multiple_of(index * tile, tile), tile)
            product = back_product(at.kv_v[place, value_lanes], grad)
            part = (product * probs[place, :].astype(f32)).reshape(tile // 8, 8, both)
            return center + jnp.sum(part, axis=0)

        center = lax.fori_loop(0, tiles, first_pass, jnp.zeros((8, both), f32))
        center = jnp.sum(center, axis=0, keepdims=True)

        def second_pass(index, unused):
            place = pl.ds(pl.multiple_of(index * tile, tile), tile)
            weights = probs[place, :]
            product = back_product(at.kv_v[place, value_lanes], grad)
            scores = (weights.astype(f32) * (product - center)).astype(bf16)
            at.dkv_v[place, value_lanes] = matmul(weights, grad).astype(bf16)
            at.dkv_v[place, lanes] = (matmul(scores, query) * scale).astype(bf16)
            at.ds_v[place, :] = scores
            return unused

        lax.fori_loop(0, tiles, second_pass, 0)
        turned = down_product(at.kv_v[:, lanes], at.ds_v[...])
        at.dq_v[:, lanes] = (join_heads(turned, head_size) * scale).astype(bf16)
        sums.pump()

    get_memory = fetch(at.memory, at.kv_v.at[:, pl.ds(0, model)])
    get_q2.wait()
    get_after.wait()
    upstream = back_product(at.dq_v[...], at.wq2_v[...])
    grad_rows, gain2 = norm_back(at.gate_v[:, 0:model], at.gains[1:2, :], upstream)
    at.rows_v[...] = at.rows_v[...] + grad_rows
    get_out1.wait()
    at.do_v[...] = at.rows_v[...].astype(bf16)
    at.gc_v[...] = back_product(at.do_v[...], at.wo1_v[...]).astype(bf16)
    sums.pump()
    get_memory.wait()
    share_into(
        at.s_kv, at.kv_v.at[:, pl.ds(0, model)], at.dkv_v, tile, at.turn_v
    )
    get_kv2 = fetch(at.w_kv2, at.turn_v)
    sums.ready = 9
    sums.pump()

    get_merged.wait()
    get_self.wait()
    for pair in range(pairs):
        lanes = slice(pair * width, (pair + 1) * width)
        key_lanes = slice(model + pair * width, model + (pair + 1) * width)
        value_lanes = slice(2 * model + pair * width, 2 * model + (pair + 1) * width)
        grad = spread_heads(at.gc_v[:, lanes], head_size)
        query = spread_heads(at.dgu_v[:, lanes], head_size)
        weights = at.sp_v[pair]
        wide = weights.astype(f32)
        product = back_product(at.dgu_v[:, value_lanes], grad)
        center = jnp.sum(product * wide, axis=0, keepdims=True)
        scores = (wide * (product - center)).astype(bf16)
        at.dqkv_v[:, value_lanes] = matmul(weights, grad).astype(bf16)
        at.dqkv_v[:, key_lanes] = (matmul(scores, query) * scale).astype(bf16)
        turned = down_product(at.dgu_v[:, key_lanes], scores)
        at.dqkv_v[:, lanes] = (join_heads(turned, head_size) * scale).astype(bf16)
        distance = fold_rows(scores.astype(f32))
        for part in range(3):
            at.small_v[18 + 3 * pair + part:19 + 3 * pair + part, :] = distance[
                :, part * 128:(part + 1) * 128
            ]
        if pair % 3 == 2:
            sums.pump()
    get_qkv.wait()
    get_embedded.wait()
    upstream = back_product(at.dqkv_v[...], at.wqkv_v[...])
    grad_rows, gain1 = norm_back(at.upper_v[:, 0:model], at.gains[0:1, :], upstream)
    row_grads = (at.rows_v[...] + grad_rows).astype(bf16)
    slots = down_product(at.pick[...], row_grads).astype(bf16)
    at.slots_v[...] = slots.reshape(at.slots_v.shape)
    at.returned[me] = at.slots_v[me]
    slot_copy = lambda step, other: remote(
        at.slots_v.at[other],
        at.returned.at[me],
        at.slot_send,
        at.slot_recv,
        step - 1,
        place_of(other),
    )
    every_other(me, owners, lambda step, other: slot_copy(step, other).start())
    for part in range(6):
        block = slice(part * 128, (part + 1) * 128)
        at.small_v[part:part + 1, :] = gain1[:, block]
        at.small_v[6 + part:7 + part, :] = gain2[:, block]
    at.small_v[36:40, :] = jnp.zeros((4, 128), f32)
    at.small[...] = at.small_v[...]
    get_normed2.wait()
    share_into(
        columns(at.s_pair, 0, model), at.u_v.at[:, pl.ds(0, model)], at.dq_v, tile
    )
    get_mixed1.wait()
    share_into(
        columns(at.s_pair, model, model),
        at.dgu_v.at[:, pl.ds(4 * model, model)],
        at.do_v,
        tile,
    )
    sums.ready = 11
    sums.pump()
    get_normed1.wait()
    share_into(at.s_qkv, at.dgu_v.at[:, pl.ds(3 * model, model)], at.dqkv_v, tile)
    sums.ready = 14
    sums.pump()

    get_kv2.wait()

    def memory_tile(index, unused):
        place = pl.ds(pl.multiple_of(index * tile, tile), tile)
        at.kv_v[place, model:] = back_product(at.dkv_v[place, :], at.turn_v[...]).astype(bf16)
        return unused

    lax.fori_loop(0, tiles, memory_tile, 0)
    put_memory = fetch(at.kv_v.at[:, pl.ds(model, model)], at.memory_grad)

    taken = 0
    for group in ([sums.sibling], [sums.first], [sums.second], sums.along_z):
        copies = [
            remote(
                at.small,
                at.small_in.at[taken + k],
                at.small_send,
                at.small_recv,
                taken + k,
                device,
            )
            for k, device in enumerate(group)
        ]
        for copy in copies:
            copy.start()
        sums.pump()
        for copy in copies:
            copy.wait()
        total = at.small[...]
        for k in range(len(group)):
            total = total + at.small_in[taken + k]
        at.small[...] = total
        taken += len(group)
    sums.finish()
    every_other(me, owners, lambda step, other: slot_copy(step, other).wait())
    put_memory.wait()


def backward_with_sums(inputs, head_size, slot_rows):
    length, model = inputs.queries.shape
    memory_len = inputs.memory.shape[0]
    owners = 32
    rows = model // owners
    pairs = model // (2 * head_size)
    both = 2 * length
    ffn = inputs.w_gate.shape[1]
    out3_rows = ffn // owners
    flat = lambda count, columns: jax.ShapeDtypeStruct((count * columns // 128, 128), f32)
    outs = BackwardOut(
        qkv=flat(rows, 3 * model),
        out1=flat(rows, model),
        q2=flat(rows, model),
        kv2=flat(rows, 2 * model),
        out2=flat(rows, model),
        ffn=flat(rows, 2 * ffn),
        out3=flat(out3_rows, model),
        hidden=jax.ShapeDtypeStruct((length, model), f32),
        small=jax.ShapeDtypeStruct((40, 128), f32),
        returned=jax.ShapeDtypeStruct((owners, slot_rows, model), bf16),
        memory_grad=jax.ShapeDtypeStruct((memory_len, model), bf16),
    )
    by_owner = lambda count, columns: pltpu.VMEM((4, 2, 2, 2, count, columns), bf16)
    own = [
        pltpu.VMEM((memory_len, 2 * model), bf16),
        pltpu.VMEM((memory_len, 2 * model), bf16),
        pltpu.VMEM((2, memory_len, both), bf16),
        pltpu.VMEM((model, model), bf16),
        pltpu.VMEM((model, model), bf16),
        pltpu.VMEM((model, 3 * model), bf16),
        pltpu.VMEM((model, memory_len), bf16),
        pltpu.VMEM((memory_len, both), bf16),
        pltpu.VMEM((length, model), bf16),
        pltpu.VMEM((length, 3 * model), bf16),
        pltpu.VMEM((length, model), bf16),
        pltpu.VMEM((length, model), bf16),
        pltpu.VMEM((length, model), f32),
        pltpu.VMEM((owners, slot_rows, model), bf16),
        by_owner(rows, 2 * model),
        by_owner(rows, 2 * model),
        by_owner(rows, 3 * model),
        by_owner(out3_rows, model),
        by_owner(rows, model),
        pltpu.VMEM((length, ffn), f32),
        pltpu.VMEM((length, ffn), f32),
        pltpu.VMEM((length, ffn), bf16),
        pltpu.VMEM((length, max(2 * ffn, 5 * model)), bf16),
        pltpu.VMEM((pairs, length, both), bf16),
        pltpu.VMEM((40, 128), f32),
        pltpu.VMEM((6, 40, 128), f32),
    ]
    chunks = 14
    dma = pltpu.SemaphoreType.DMA
    sems = [
        dma((10 * chunks,)),
        dma((10 * chunks,)),
        pltpu.SemaphoreType.REGULAR((4,)),
        dma((40,)),
        dma((6,)),
        dma((6,)),
        dma((owners - 1,)),
        dma((owners - 1,)),
    ]
    shapes = (
        [(out3_rows, model // 2)] * 2 + [(rows, ffn // 2)] * 4 + [(rows, model)] * 4
    )
    rooms = []
    for shape in shapes:
        for lead in ((4, 4), (2, 4), (4,), (3,)):
            rooms.append(pltpu.VMEM(lead + shape, bf16))
    far = pl.BlockSpec(memory_space=pl.ANY)
    near = pl.BlockSpec(memory_space=pltpu.VMEM)
    results = pl.pallas_call(
        functools.partial(backward_kernel, head_size, 2),
        out_shape=list(outs),
        in_specs=[far] * backward_far + [near] * (len(inputs) - backward_far),
        out_specs=[near] * (len(outs) - 1) + [far],
        scratch_shapes=own + sems + rooms,
        compiler_params=pltpu.CompilerParams(
            collective_id=2, has_side_effects=True, vmem_limit_bytes=63 * 1024 * 1024
        ),
    )(*inputs)
    return BackwardOut(*results)


def table_kernel(copies, ids_ref, rows_ref, *refs):
    sources, out_ref, targets = refs[:copies], refs[copies], refs[copies + 1:2 * copies + 1]
    rooms, sems = refs[2 * copies + 1:3 * copies + 1], refs[3 * copies + 1:]
    step = pl.program_id(0)

    def moves(inward):
        return [
            pltpu.make_async_copy(source, room, sems[0].at[k])
            if inward
            else pltpu.make_async_copy(room, target, sems[0].at[k])
            for k, (source, room, target) in enumerate(zip(sources, rooms, targets))
        ]

    if copies:

        @pl.when(step == 0)
        def enter():
            for copy in moves(True):
                copy.start()

        @pl.when(step == 1)
        def turn():
            for copy in moves(True):
                copy.wait()
            for copy in moves(False):
                copy.start()

        @pl.when(step == pl.num_programs(0) - 1)
        def leave():
            for copy in moves(False):
                copy.wait()

    block = out_ref.shape[0]
    row = lax.broadcasted_iota(jnp.int32, (block, ids_ref.shape[1]), 0)
    wanted = ids_ref[0:1, :].astype(jnp.int32) - step * block
    hits = jnp.where(row == wanted, 1.0, 0.0).astype(bf16)
    out_ref[...] = matmul(hits, rows_ref[...])


def table_and_copies(requests, returned, shard_rows, copies):
    slots, model = returned.shape
    block = min(1024, -(-shard_rows // 16) * 8)
    whole = lambda value: pl.BlockSpec(value.shape, lambda i: (0,) * value.ndim)
    far = pl.BlockSpec(memory_space=pltpu.HBM)
    results = pl.pallas_call(
        functools.partial(table_kernel, len(copies)),
        grid=(-(-shard_rows // block),),
        out_shape=[jax.ShapeDtypeStruct((shard_rows, model), f32)]
        + [jax.ShapeDtypeStruct(value.shape, value.dtype) for value in copies],
        in_specs=[whole(requests), whole(returned)] + [far] * len(copies),
        out_specs=[pl.BlockSpec((block, model), lambda i: (i, 0))] + [far] * len(copies),
        scratch_shapes=[pltpu.VMEM(value.shape, value.dtype) for value in copies]
        + [pltpu.SemaphoreType.DMA((len(copies),))] * bool(copies),
        compiler_params=pltpu.CompilerParams(vmem_limit_bytes=63 * 1024 * 1024),
        cost_estimate=pl.CostEstimate(
            flops=2 * shard_rows * slots * model,
            bytes_accessed=4 * shard_rows * model,
            transcendentals=0,
        ),
    )(requests, returned, *copies)
    return results[0], results[1:]


def body(
    target_ids,
    target_lengths,
    bucket_table,
    memory,
    table,
    self_qkv,
    self_out,
    cross_q,
    cross_kv,
    cross_out,
    ffn_in,
    ffn_out,
    gains,
    relative_bias,
    cotangent,
):
    pair_count, seq_len = target_ids.shape
    model_width = table.shape[1]
    bucket_count, head_count = relative_bias.shape
    head_size = model_width // head_count
    memory_len = memory.shape[1]
    wide_count = lax.axis_size("wide")
    narrow_count = lax.axis_size("narrow")
    owner_count = wide_count * narrow_count
    special = wide_count == 8 and narrow_count == 4
    ffn_width = ffn_out.shape[0] * owner_count // model_width
    token_count = pair_count * seq_len
    shard_rows = table.shape[0]
    capacity = max(2, (2 * token_count + owner_count - 1) // owner_count)
    room = -(-capacity // 16) * 16 if special else capacity
    slots = owner_count * room

    positions = jnp.arange(seq_len, dtype=jnp.int32)
    valid_flat = (positions[:, None] < target_lengths[0]).astype(f32)
    bucket_hits = (
        bucket_table[:, None] == jnp.arange(bucket_count, dtype=jnp.int32)[None, :]
    ).astype(f32)
    memory_rows = memory.reshape(memory_len, model_width)
    if special:
        main_rows = shard_rows // 16 * 16
        row_count = model_width // owner_count
        widths = (2 * model_width, 3 * model_width) + (model_width,) * 3 + (ffn_width,) * 2
        shapes = [(row_count, columns) for columns in widths]
        shapes.append((ffn_width // owner_count, model_width))
        weights, done = forward_with_gather(
            ForwardIn(
                flat_kv2=cross_kv.reshape(-1, 128),
                flat_qkv=self_qkv.reshape(-1, 128),
                flat_out1=self_out.reshape(-1, 128),
                flat_q2=cross_q.reshape(-1, 128),
                flat_out2=cross_out.reshape(-1, 128),
                flat_in=ffn_in.reshape(-1, 128),
                flat_out3=ffn_out.reshape(-1, 128),
                ids_row=target_ids.reshape(1, token_count),
                keep=valid_flat,
                buckets=bucket_table.reshape(1, seq_len),
                relative=relative_bias,
                gains=gains,
                tail=table[main_rows:],
                table=table,
                memory=memory_rows,
            ),
            shapes,
            room,
            head_size,
        )
        requests, slot_pick = done.wanted, done.pick
        w_kv2, w_qkv, w_out1, w_q2, w_out2, w_gate, w_upper, w_out3 = weights
        key_values, cross_probs = done.key_values, done.cross_probs
        embedded, self_normalized = done.embedded, done.normed1
        merged, self_probs, self_mixed = done.merged, done.self_probs, done.mixed1
        after_self, normed_cross = done.after_self, done.normed2
        cross_queries, cross_mixed = done.queries, done.mixed2
        after_cross, normed_ffn = done.after_cross, done.normed3
    else:
        flat_ids = target_ids.reshape(token_count)
        owner_index = flat_ids // shard_rows
        owner_hits = (owner_index[:, None] == jnp.arange(owner_count, dtype=jnp.int32)[None, :]).astype(
            jnp.int32
        )
        rank_within = jnp.sum(jnp.cumsum(owner_hits, axis=0) * owner_hits, axis=1) - 1
        slot_index = owner_index * room + rank_within
        slot_hits = slot_index[:, None] == jnp.arange(slots, dtype=jnp.int32)[None, :]
        outgoing = (
            jnp.sum(
                jnp.where(slot_hits, (flat_ids - owner_index * shard_rows + 1)[:, None], 0), axis=0
            )
            - 1
        )
        slot_pick = (slot_hits & (valid_flat > 0.0)).astype(bf16)
        shards = [
            cross_kv.reshape(-1, 2 * model_width),
            self_qkv.reshape(-1, 3 * model_width),
            self_out.reshape(-1, model_width),
            cross_q.reshape(-1, model_width),
            cross_out.reshape(-1, model_width),
            *jnp.split(ffn_in.reshape(-1, 2 * ffn_width), 2, axis=1),
            ffn_out.reshape(-1, model_width),
        ]
        w_kv2, w_qkv, w_out1, w_q2, w_out2, w_gate, w_upper, w_out3 = [
            lax.all_gather(shard, axes, axis=0, tiled=True) for shard in shards
        ]
        requests = lax.all_to_all(
            lax.all_to_all(
                outgoing.reshape(wide_count, narrow_count, room),
                "wide",
                split_axis=0,
                concat_axis=0,
                tiled=True,
            ),
            "narrow",
            split_axis=1,
            concat_axis=1,
            tiled=True,
        )
        found = table[jnp.maximum(requests, 0)]
        arrived = lax.all_to_all(
            lax.all_to_all(found, "wide", split_axis=0, concat_axis=0, tiled=True),
            "narrow",
            split_axis=1,
            concat_axis=1,
            tiled=True,
        ).reshape(slots, model_width)
        embedded = matmul(slot_pick, arrived)
        key_values = matmul(memory_rows, w_kv2).astype(bf16)
        self_normalized = rms_scaled(embedded, gains[0]).astype(bf16)
        merged = matmul(self_normalized, w_qkv).astype(bf16)
        bias_rows = jnp.dot(relative_bias.T, bucket_hits.T, precision=top_precision).reshape(
            head_count // 2, 1, 2 * seq_len
        )
        self_mixed, self_probs = self_forward(merged, bias_rows, valid_flat, head_size)
        after_self = embedded + matmul(self_mixed, w_out1)
        normed_cross = rms_scaled(after_self, gains[1]).astype(bf16)
        cross_queries = matmul(normed_cross, w_q2).astype(bf16)
        cross_mixed, cross_probs = cross_forward(cross_queries, key_values, head_size)
        after_cross = after_self + matmul(cross_mixed, w_out2)
        normed_ffn = rms_scaled(after_cross, gains[2]).astype(bf16)
    if special:
        sums = backward_with_sums(
            BackwardIn(
                key_values=key_values,
                cross_probs=cross_probs,
                memory=memory_rows,
                w_q2=w_q2,
                w_out1=w_out1,
                w_qkv=w_qkv,
                w_kv2=w_kv2,
                w_gate=w_gate,
                w_upper=w_upper,
                w_out3=w_out3,
                w_out2=w_out2,
                after_self=after_self,
                embedded=embedded,
                merged=merged,
                self_probs=self_probs,
                normed1=self_normalized,
                normed2=normed_cross,
                mixed1=self_mixed,
                queries=cross_queries,
                mixed2=cross_mixed,
                normed3=normed_ffn,
                after_cross=after_cross,
                cotangent=cotangent.reshape(token_count, model_width),
                keep=valid_flat,
                gains=gains,
                pick=slot_pick,
            ),
            head_size,
            room,
        )
        table_grad, copied = table_and_copies(
            requests,
            sums.returned.reshape(slots, model_width),
            shard_rows,
            [*sums[:8], sums.memory_grad],
        )
        weight_sums = [value.reshape(-1) for value in copied[:7]]
        hidden, memory_grad = copied[7:]
        small_sum = sums.small.reshape(-1)
        gain_sums = small_sum[:3 * model_width].reshape(3, model_width)
        distance_sums = small_sum[3 * model_width:3 * model_width + head_count * seq_len]
    else:
        gate, upper = matmul(normed_ffn, w_gate), matmul(normed_ffn, w_upper)
        activated = gated(gate, upper).astype(bf16)
        hidden = (after_cross + matmul(activated, w_out3)) * valid_flat

        upstream = cotangent.reshape(token_count, model_width) * valid_flat
        grad_branch3 = upstream.astype(bf16)
        share_out3 = outer_sum(activated, grad_branch3).astype(bf16)
        grad_act = back_product(grad_branch3, w_out3)
        unused, gate_pull = jax.vjp(gated, gate, upper)
        grad_gate, grad_upper = [part.astype(bf16) for part in gate_pull(grad_act)]
        share_gate = outer_sum(normed_ffn, grad_gate).astype(bf16)
        share_upper = outer_sum(normed_ffn, grad_upper).astype(bf16)
        grad_normed3 = back_product(grad_gate, w_gate) + back_product(grad_upper, w_upper)
        grad_cross_state, grad_gain3 = norm_backward(after_cross, gains[2], grad_normed3)
        grad_cross_state = grad_cross_state + upstream

        grad_branch2 = grad_cross_state.astype(bf16)
        share_out2 = outer_sum(cross_mixed, grad_branch2).astype(bf16)
        grad_cross_mixed = back_product(grad_branch2, w_out2).astype(bf16)
        grad_cross_q, grad_kv = cross_backward(
            cross_queries, key_values, cross_probs, grad_cross_mixed, head_size
        )
        grad_normed2 = back_product(grad_cross_q, w_q2)
        grad_self_state, grad_gain2 = norm_backward(after_self, gains[1], grad_normed2)
        grad_self_state = grad_self_state + grad_cross_state
        grad_branch1 = grad_self_state.astype(bf16)
        grad_self_mixed = back_product(grad_branch1, w_out1).astype(bf16)
        grad_joined, grad_distance = self_backward(merged, self_probs, grad_self_mixed, head_size)
        grad_first_normalized = back_product(grad_joined, w_qkv)
        grad_embedded, grad_gain1 = norm_backward(embedded, gains[0], grad_first_normalized)
        row_grads = (grad_embedded + grad_self_state).astype(bf16)
        slot_grads = outer_sum(slot_pick, row_grads).astype(bf16)
        returned = lax.all_to_all(
            lax.all_to_all(
                slot_grads.reshape(wide_count, narrow_count, room, model_width),
                "wide",
                split_axis=0,
                concat_axis=0,
                tiled=True,
            ),
            "narrow",
            split_axis=1,
            concat_axis=1,
            tiled=True,
        ).reshape(slots, model_width)
        table_grad, unused = table_and_copies(
            requests.reshape(1, slots), returned, shard_rows, []
        )
        memory_grad = back_product(grad_kv, w_kv2).astype(bf16)
        shares = (
            outer_sum(self_normalized, grad_joined).astype(bf16),
            outer_sum(self_mixed, grad_branch1).astype(bf16),
            outer_sum(normed_cross, grad_cross_q).astype(bf16),
            outer_sum(memory_rows, grad_kv).astype(bf16),
            share_out2,
            jnp.concatenate([share_gate, share_upper], axis=1),
            share_out3,
        )
        weight_sums = [
            lax.psum_scatter(share, axes, scatter_dimension=0, tiled=True)
            .astype(f32)
            .reshape(-1)
            for share in shares
        ]
        gain_sums, distance_sums = lax.psum(
            (jnp.stack([grad_gain1, grad_gain2, grad_gain3]), grad_distance.reshape(-1)), axes
        )

    bias_sums = jnp.dot(
        bucket_hits.T, distance_sums.reshape(head_count, seq_len).T, precision=top_precision
    )
    return (
        hidden.reshape(pair_count, seq_len, model_width),
        memory_grad.reshape(pair_count, memory_len, model_width),
        table_grad,
        *weight_sums,
        gain_sums,
        bias_sums,
    )


def solution(mesh):
    split = P(axes)
    return jax.shard_map(
        body,
        mesh=mesh,
        in_specs=(
            P(axes, None),
            split,
            P(),
            P(axes, None, None),
            P(axes, None),
            split,
            split,
            split,
            split,
            split,
            split,
            split,
            P(),
            P(),
            P(axes, None, None),
        ),
        out_specs=(
            P(axes, None, None),
            P(axes, None, None),
            P(axes, None),
            split,
            split,
            split,
            split,
            split,
            split,
            split,
            P(),
            P(),
        ),
        check_vma=False,
    )
```

```python
import functools
from typing import NamedTuple

import jax
import jax.numpy as jnp
import numpy as np
from jax import lax
from jax.experimental import pallas as pl
from jax.experimental.pallas import tpu as pltpu
from jax.sharding import PartitionSpec as P

epsilon = 1e-06
blocked = -1e30
top_precision = lax.Precision.HIGHEST
axes = ("wide", "narrow")
bf16 = jnp.bfloat16
f32 = jnp.float32


def rms_scaled(inputs, gain):
    return inputs * lax.rsqrt(jnp.mean(inputs * inputs, axis=-1, keepdims=True) + epsilon) * gain


def norm_backward(inputs, gain, upstream):
    unused, pullback = jax.vjp(rms_scaled, inputs, gain)
    return pullback(upstream)


def gated(gate, upper):
    return jax.nn.gelu(gate, approximate=True) * upper


def matmul(left, right):
    return jnp.dot(left, right, preferred_element_type=f32)


def outer_sum(left, right):
    return lax.dot_general(left, right, (((0,), (0,)), ((), ())), preferred_element_type=f32)


def back_product(left, right):
    return lax.dot_general(left, right, (((1,), (1,)), ((), ())), preferred_element_type=f32)


mesh_ids = pl.DeviceIdType.MESH
roomy = pltpu.CompilerParams(vmem_limit_bytes=48 * 1024 * 1024)


def standing():
    wide, narrow = lax.axis_index("wide"), lax.axis_index("narrow")
    return wide // 2, wide % 2, narrow // 2, narrow % 2


def device_at(z, x, y, core):
    return (z * 2 + x, y * 2 + core)


def flips(x, y, core):
    far_x, far_y = 1 - x, 1 - y
    second = (x * (1 - core) + far_x * core, far_y * (1 - core) + y * core)
    first = (far_x * (1 - core) + x * core, y * (1 - core) + far_y * core)
    return ((x, y), second, first, (far_x, far_y))


def partners():
    z, x, y, core = standing()
    own, second, first, both = flips(x, y, core)
    along_z = [device_at((z + step) % 4, x, y, core) for step in (1, 2, 3)]
    return along_z, device_at(z, *second, core), device_at(z, *first, core), device_at(z, x, y, 1 - core)


def greet(devices):
    barrier = pltpu.get_barrier_semaphore()
    for device in devices:
        pl.semaphore_signal(barrier, inc=1, device_id=device, device_id_type=mesh_ids)
    pl.semaphore_wait(barrier, len(devices))


def remote(source, target, send_sem, recv_sem, index, device):
    return pltpu.make_async_remote_copy(
        src_ref=source,
        dst_ref=target,
        send_sem=send_sem.at[index],
        recv_sem=recv_sem.at[index],
        device_id=device,
        device_id_type=mesh_ids,
    )


def spread_heads(pair, head_size):
    lane = lax.broadcasted_iota(jnp.int32, pair.shape, 1)
    zero = jnp.zeros_like(pair)
    return jnp.concatenate(
        [jnp.where(lane < head_size, pair, zero), jnp.where(lane >= head_size, pair, zero)], axis=0
    )


def join_heads(spread, head_size):
    turned = spread.T
    rows = turned.shape[0] // 2
    lane = lax.broadcasted_iota(jnp.int32, (rows, turned.shape[1]), 1)
    return jnp.where(lane < head_size, turned[:rows], turned[rows:])


def down_product(left, right):
    return lax.dot_general(left, right, (((0,), (0,)), ((), ())), preferred_element_type=f32)


def column_softmax(scores):
    peak = jnp.max(scores, axis=0, keepdims=True)
    exponent = jnp.exp(scores - peak)
    return exponent / jnp.sum(exponent, axis=0, keepdims=True)


def self_forward_kernel(head_size, q_ref, k_ref, v_ref, bias_ref, keep_ref, out_ref, prob_ref):
    scale = head_size ** (-0.5)
    scores = back_product(k_ref[...], spread_heads(q_ref[...], head_size)) * scale
    length, both = scores.shape
    row = lax.broadcasted_iota(jnp.int32, scores.shape, 0)
    lane = lax.broadcasted_iota(jnp.int32, scores.shape, 1)
    query = jnp.where(lane >= length, lane - length, lane)
    bias = pltpu.roll(
        jnp.broadcast_to(bias_ref[0], scores.shape), 0, 1, stride=1, stride_axis=0
    )
    scores = jnp.where((row <= query) & (keep_ref[...] > 0.0), scores + bias, blocked)
    probs = column_softmax(scores).astype(bf16)
    prob_ref[0] = probs
    out_ref[...] = join_heads(down_product(v_ref[...], probs), head_size).astype(bf16)


def self_backward_kernel(
    head_size, q_ref, k_ref, v_ref, prob_ref, grad_ref, out_ref, bias_ref
):
    scale = head_size ** (-0.5)
    pair = pl.program_id(0)
    width = 2 * head_size
    model = out_ref.shape[1] // 3
    grad = spread_heads(grad_ref[...], head_size)
    probs = prob_ref[0]
    wide_probs = probs.astype(f32)
    grad_probs = back_product(v_ref[...], grad)
    center = jnp.sum(grad_probs * wide_probs, axis=0, keepdims=True)
    grad_scores = (wide_probs * (grad_probs - center)).astype(bf16)
    grad_value = matmul(probs, grad)
    grad_key = matmul(grad_scores, spread_heads(q_ref[...], head_size)) * scale
    grad_query = join_heads(down_product(k_ref[...], grad_scores), head_size) * scale
    out_ref[:, pl.ds(pl.multiple_of(pair * width, width), width)] = grad_query.astype(bf16)
    out_ref[:, pl.ds(pl.multiple_of(model + pair * width, width), width)] = grad_key.astype(bf16)
    out_ref[:, pl.ds(pl.multiple_of(2 * model + pair * width, width), width)] = grad_value.astype(
        bf16
    )
    bias_ref[0] = fold_rows(grad_scores.astype(f32))


def cross_forward_kernel(head_size, q_ref, k_ref, v_ref, out_ref, prob_ref):
    scale = head_size ** (-0.5)
    scores = back_product(k_ref[...], spread_heads(q_ref[...], head_size)) * scale
    probs = column_softmax(scores).astype(bf16)
    prob_ref[0] = probs
    out_ref[...] = join_heads(down_product(v_ref[...], probs), head_size).astype(bf16)


def cross_backward_kernel(head_size, q_ref, k_ref, v_ref, prob_ref, grad_ref, out_ref, kv_ref):
    scale = head_size ** (-0.5)
    pair = pl.program_id(0)
    width = 2 * head_size
    model = kv_ref.shape[1] // 2
    grad = spread_heads(grad_ref[...], head_size)
    probs = prob_ref[0]
    wide_probs = probs.astype(f32)
    grad_probs = back_product(v_ref[...], grad)
    center = jnp.sum(grad_probs * wide_probs, axis=0, keepdims=True)
    grad_scores = (wide_probs * (grad_probs - center)).astype(bf16)
    grad_value = matmul(probs, grad)
    grad_key = matmul(grad_scores, spread_heads(q_ref[...], head_size)) * scale
    grad_query = join_heads(down_product(k_ref[...], grad_scores), head_size) * scale
    out_ref[...] = grad_query.astype(bf16)
    kv_ref[:, pl.ds(pl.multiple_of(pair * width, width), width)] = grad_key.astype(bf16)
    kv_ref[:, pl.ds(pl.multiple_of(model + pair * width, width), width)] = grad_value.astype(bf16)


def self_forward(merged, bias_rows, keep_rows, head_size):
    length, model = merged.shape[0], merged.shape[1] // 3
    width, pairs = 2 * head_size, model // (2 * head_size)
    both = 2 * length
    part = lambda offset: pl.BlockSpec((length, width), lambda p: (0, p + offset))
    return pl.pallas_call(
        functools.partial(self_forward_kernel, head_size),
        grid=(pairs,),
        out_shape=(
            jax.ShapeDtypeStruct((length, model), bf16),
            jax.ShapeDtypeStruct((pairs, length, both), bf16),
        ),
        in_specs=[
            part(0),
            part(pairs),
            part(2 * pairs),
            pl.BlockSpec((1, 1, both), lambda p: (p, 0, 0)),
            pl.BlockSpec((length, 1), lambda p: (0, 0)),
        ],
        out_specs=(part(0), pl.BlockSpec((1, length, both), lambda p: (p, 0, 0))),
        compiler_params=roomy,
        cost_estimate=pl.CostEstimate(flops=10**9, bytes_accessed=4 * 10**6, transcendentals=10**6),
    )(merged, merged, merged, bias_rows, keep_rows)


def self_backward(merged, probs, grad, head_size):
    length, model = grad.shape
    width, pairs = 2 * head_size, model // (2 * head_size)
    both = 2 * length
    part = lambda offset: pl.BlockSpec((length, width), lambda p: (0, p + offset))
    return pl.pallas_call(
        functools.partial(self_backward_kernel, head_size),
        grid=(pairs,),
        out_shape=(
            jax.ShapeDtypeStruct((length, 3 * model), bf16),
            jax.ShapeDtypeStruct((pairs, 1, both), f32),
        ),
        in_specs=[
            part(0),
            part(pairs),
            part(2 * pairs),
            pl.BlockSpec((1, length, both), lambda p: (p, 0, 0)),
            part(0),
        ],
        out_specs=(
            pl.BlockSpec((length, 3 * model), lambda p: (0, 0)),
            pl.BlockSpec((1, 1, both), lambda p: (p, 0, 0)),
        ),
        compiler_params=roomy,
        cost_estimate=pl.CostEstimate(flops=10**9, bytes_accessed=4 * 10**6, transcendentals=0),
    )(merged, merged, merged, probs, grad)


def cross_forward(queries, key_values, head_size):
    length, model = queries.shape
    memory_len = key_values.shape[0]
    width, pairs = 2 * head_size, model // (2 * head_size)
    both = 2 * length
    part = pl.BlockSpec((length, width), lambda p: (0, p))
    long_part = lambda offset: pl.BlockSpec((memory_len, width), lambda p: (0, p + offset))
    return pl.pallas_call(
        functools.partial(cross_forward_kernel, head_size),
        grid=(pairs,),
        out_shape=(
            jax.ShapeDtypeStruct((length, model), bf16),
            jax.ShapeDtypeStruct((pairs, memory_len, both), bf16),
        ),
        in_specs=[part, long_part(0), long_part(pairs)],
        out_specs=(part, pl.BlockSpec((1, memory_len, both), lambda p: (p, 0, 0))),
        compiler_params=roomy,
        cost_estimate=pl.CostEstimate(
            flops=4 * 10**9, bytes_accessed=13 * 10**6, transcendentals=4 * 10**6
        ),
    )(queries, key_values, key_values)


def cross_backward(queries, key_values, probs, grad, head_size):
    length, model = queries.shape
    memory_len = key_values.shape[0]
    width, pairs = 2 * head_size, model // (2 * head_size)
    both = 2 * length
    part = pl.BlockSpec((length, width), lambda p: (0, p))
    long_part = lambda offset: pl.BlockSpec((memory_len, width), lambda p: (0, p + offset))
    return pl.pallas_call(
        functools.partial(cross_backward_kernel, head_size),
        grid=(pairs,),
        out_shape=(
            jax.ShapeDtypeStruct((length, model), bf16),
            jax.ShapeDtypeStruct((memory_len, 2 * model), bf16),
        ),
        in_specs=[
            part,
            long_part(0),
            long_part(pairs),
            pl.BlockSpec((1, memory_len, both), lambda p: (p, 0, 0)),
            part,
        ],
        out_specs=(part, pl.BlockSpec((memory_len, 2 * model), lambda p: (0, 0))),
        compiler_params=roomy,
        cost_estimate=pl.CostEstimate(
            flops=8 * 10**9, bytes_accessed=18 * 10**6, transcendentals=0
        ),
    )(queries, key_values, key_values, probs, grad)


class Gather:
    def __init__(self, send_sem, recv_sem, own_sem):
        self.z, self.x, self.y, self.core = standing()
        self.sets = flips(self.x, self.y, self.core)
        self.along_z, self.second, self.first, self.sibling = partners()
        self.send_sem, self.recv_sem, self.own_sem = send_sem, recv_sem, own_sem
        self.chunks, self.flying, self.own, self.clock, self.after = [], {}, {}, 0, {}

    def add(self, shard, out, after=None):
        chunk = len(self.chunks)
        self.chunks.append((shard, out))
        self.after[chunk] = after
        own = pltpu.make_async_copy(
            shard, out.at[self.z, self.x, self.y, self.core], self.own_sem.at[chunk]
        )
        own.start()
        self.own[chunk] = own
        return chunk

    def copies(self, number, chunk):
        base = chunk * 10
        shard, out = self.chunks[chunk]
        if number == 0:
            return [
                remote(
                    shard,
                    out.at[self.z, self.x, self.y, self.core],
                    self.send_sem,
                    self.recv_sem,
                    base + k,
                    device,
                )
                for k, device in enumerate(self.along_z)
            ]
        piece = lambda k: out.at[:, self.sets[k][0], self.sets[k][1], self.core]
        device = (self.second, self.first, self.sibling)[number - 1]
        amount = (1, 2, 4)[number - 1]
        return [
            remote(piece(k), piece(k), self.send_sem, self.recv_sem, base + 2 + amount + k, device)
            for k in range(amount)
        ]

    def pump(self, spacing, steps=1):
        for unused in range(steps):
            for number in (4, 3, 2, 1, 0):
                chunk = self.clock - number * spacing
                if 0 <= chunk < len(self.chunks):
                    if number == 1:
                        self.own[chunk].wait()
                    if number > 0:
                        for copy in self.flying[number - 1, chunk]:
                            copy.wait_recv()
                    if number < 4:
                        self.flying[number, chunk] = self.copies(number, chunk)
                        for copy in self.flying[number, chunk]:
                            copy.start()
                    elif self.after[chunk] is not None:
                        self.after[chunk]()
            self.clock += 1

    def until(self, spacing, chunk):
        while self.clock <= chunk + 4 * spacing:
            self.pump(spacing)

    def finish(self):
        for copies in self.flying.values():
            for copy in copies:
                copy.wait_send()


def rms_rounded(rows, gain):
    turn = lax.rsqrt(jnp.mean(rows * rows, axis=-1, keepdims=True) + epsilon)
    return (rows * turn * gain).astype(bf16)


class Weights(NamedTuple):
    w_kv2: object
    w_qkv: object
    w_out1: object
    w_q2: object
    w_out2: object
    w_gate: object
    w_upper: object
    w_out3: object


class ForwardIn(NamedTuple):
    flat_kv2: object
    flat_qkv: object
    flat_out1: object
    flat_q2: object
    flat_out2: object
    flat_in: object
    flat_out3: object
    ids_row: object
    keep: object
    buckets: object
    relative: object
    gains: object
    tail: object
    table: object
    memory: object


class ForwardOut(NamedTuple):
    key_values: object
    cross_probs: object
    embedded: object
    merged: object
    self_probs: object
    after_self: object
    wanted: object
    pick: object
    normed1: object
    mixed1: object
    normed2: object
    queries: object
    mixed2: object
    after_cross: object
    normed3: object


class ForwardRefs(NamedTuple):
    flat_kv2: object
    flat_qkv: object
    flat_out1: object
    flat_q2: object
    flat_out2: object
    flat_in: object
    flat_out3: object
    ids_row: object
    keep: object
    buckets: object
    relative: object
    gains: object
    tail: object
    table: object
    memory: object
    key_values: object
    cross_probs: object
    embedded_o: object
    merged_o: object
    self_probs_o: object
    after_self_o: object
    wanted: object
    pick: object
    normed1: object
    mixed1: object
    normed2: object
    queries: object
    mixed2: object
    after_cross: object
    normed3: object
    embedded: object
    merged: object
    self_probs: object
    after_self: object
    wide_v: object
    bias_v: object
    p_kv2: object
    p_qkv: object
    p_out1: object
    p_q2: object
    p_out2: object
    p_gate: object
    p_upper: object
    p_out3: object
    outgoing: object
    requests: object
    kv2_v: object
    qkv_v: object
    out1_v: object
    q2_v: object
    out2_v: object
    memory_v: object
    kv_v: object
    table_v: object
    last_v: object
    found_f: object
    found_v: object
    arrived: object
    s_v: object
    p_v: object
    send: object
    recv: object
    own: object
    fetch: object
    id_send: object
    id_recv: object
    row_send: object
    row_recv: object


def every_other(me, owners, action):
    def one(step, unused):
        action(step, (me + step) % owners)
        return unused

    lax.fori_loop(1, owners, one, 0)


def forward_kernel(head_size, spacing, *refs):
    count = len(Weights._fields)
    inputs = len(ForwardIn._fields)
    whole = refs[inputs:inputs + count]
    at = ForwardRefs(*refs[:inputs], *refs[inputs + count:])
    shards = (
        at.p_kv2,
        at.p_qkv,
        at.p_out1,
        at.p_q2,
        at.p_out2,
        at.p_gate,
        at.p_upper,
        at.p_out3,
    )
    scale = head_size ** (-0.5)
    width = 2 * head_size
    length, model = at.embedded.shape
    memory_len = at.memory.shape[0]
    pairs = model // width
    both = 2 * length
    owners = 32
    me = lax.axis_index("wide") * 4 + lax.axis_index("narrow")
    place_of = lambda other: (other // 4, other % 4)

    def fetch(index, source, target):
        copy = pltpu.make_async_copy(source, target, at.fetch.at[index])
        copy.start()
        return copy

    block = at.table_v.shape[1]
    blocks = at.table.shape[0] // block
    rest = (at.table.shape[0] - blocks * block) // 16 * 16
    get_table = {}
    table_block = lambda k: fetch(
        k, at.table.at[pl.ds(k * block, block), :], at.table_v.at[k % 3]
    )
    for k in range(3):
        get_table[k] = table_block(k)
    get_last = fetch(
        16, at.table.at[pl.ds(blocks * block, rest), :], at.last_v.at[0:rest, :]
    )
    get_memory = fetch(17, at.memory, at.memory_v)

    barrier = pltpu.get_barrier_semaphore()
    every_other(
        me,
        owners,
        lambda step, other: pl.semaphore_signal(
            barrier, inc=1, device_id=place_of(other), device_id_type=mesh_ids
        ),
    )

    first = 0
    for flat, group in zip(
        refs[:7],
        (shards[:1], shards[1:2], shards[2:3], shards[3:4], shards[4:5], shards[5:7], shards[7:]),
    ):
        at.wide_v[first:first + flat.shape[0], :] = flat[...].astype(f32)
        stride = sum(shard.shape[1] for shard in group) // 128
        number = 0
        for shard in group:
            for start in range(0, shard.shape[1], 128):
                shard[:, start:start + 128] = at.wide_v[
                    pl.ds(first + number, shard.shape[0], stride), :
                ].astype(bf16)
                number += 1
        first += flat.shape[0]

    room = at.outgoing.shape[1]
    slots = owners * room
    shard_rows = float(at.table.shape[0])
    ids_row = at.ids_row[...].astype(f32)

    def numbers(shape, dim):
        return lax.broadcasted_iota(jnp.int32, shape, dim).astype(f32)

    def total(hits, dim):
        return jnp.sum(jnp.where(hits, 1.0, 0.0), axis=dim, keepdims=True)

    token, other_token = numbers((length, length), 0), numbers((length, length), 1)
    ids_column = jnp.sum(jnp.where(token == other_token, ids_row, 0.0), axis=1, keepdims=True)
    owner_column = total(ids_column >= (numbers((length, 128), 1) + 1.0) * shard_rows, 1)
    owner_row = total(ids_row >= (numbers((owners, length), 0) + 1.0) * shard_rows, 0)
    same = owner_column == owner_row
    slot_column = owner_column * room + total(same & (other_token < token), 1)
    slot_row = owner_row * room + total(same & (token < other_token), 0)
    at.pick[...] = jnp.where(
        (numbers((length, slots), 1) == slot_column) & (at.keep[...] > 0.0), 1.0, 0.0
    ).astype(bf16)
    local_row = jnp.max(
        jnp.where(
            numbers((slots, length), 0) == slot_row, ids_row - owner_row * shard_rows, -1.0
        ),
        axis=1,
        keepdims=True,
    )
    at.outgoing[...] = jnp.broadcast_to(local_row, (slots, 128)).reshape(owners, room, 128)
    count = at.relative.shape[1]
    buckets = at.buckets[...].astype(f32) == numbers((count, length), 0)
    diagonal = numbers((count, count), 0) == numbers((count, count), 1)
    for head in range(2 * pairs):
        column = jnp.sum(
            jnp.where(diagonal, at.relative[head:head + 1, :], 0.0), axis=1, keepdims=True
        )
        row = jnp.sum(jnp.where(buckets, column, 0.0), axis=0, keepdims=True)
        start = head % 2 * length
        at.bias_v[head // 2, :, start:start + length] = row
    pl.semaphore_wait(barrier, owners - 1)

    id_copy = lambda step, other: remote(
        at.outgoing.at[other],
        at.requests.at[me],
        at.id_send,
        at.id_recv,
        step - 1,
        place_of(other),
    )
    every_other(me, owners, lambda step, other: id_copy(step, other).start())

    gather = Gather(at.send, at.recv, at.own)
    got = {}
    order = {}

    def add(index, part, parts, kept=None):
        size = shards[index].shape[1] // parts
        lanes = pl.ds(part * size, size)
        out = whole[index].at[:, :, :, :, :, lanes]
        after = None
        chunk = len(gather.chunks)
        if kept is not None:

            def after():
                got[chunk] = fetch(18 + chunk, out, kept.at[:, :, :, :, :, lanes])

        gather.add(shards[index].at[:, lanes], out, after)
        order[index, part] = chunk

    for part in range(2):
        add(0, part, 2, at.kv2_v)
    for part in range(3):
        add(1, part, 3, at.qkv_v)
    add(2, 0, 1, at.out1_v)
    add(3, 0, 1, at.q2_v)
    add(4, 0, 1, at.out2_v)
    for index in (5, 6, 7):
        for part in range(2):
            add(index, part, 2)

    def ready(index, part):
        chunk = order[index, part]
        gather.until(spacing, chunk)
        if chunk in got:
            got.pop(chunk).wait()

    def weight(kept, start, size):
        return kept[:, :, :, :, :, start:start + size].reshape(model, size)

    gather.pump(spacing)
    at.requests[me] = at.outgoing[me]
    at.last_v[rest:, :] = jnp.zeros_like(at.last_v[rest:, :])
    at.last_v[rest:rest + at.tail.shape[0], :] = at.tail[...]
    gather.pump(spacing)
    every_other(me, owners, lambda step, other: id_copy(step, other).wait())

    wanted = at.requests[...].reshape(slots, 128)
    at.wanted[...] = wanted.T[0:8, :]

    def hits(start, size):
        offset = at.requests[...].reshape(slots, 128) - numbers((slots, 128), 1)
        return jnp.concatenate(
            [
                jnp.where(offset == float(start + column), 1.0, 0.0).astype(bf16)
                for column in range(0, size, 128)
            ],
            axis=1,
        )

    get_last.wait()
    at.found_f[...] = matmul(hits(blocks * block, at.last_v.shape[0]), at.last_v[...])
    for k in range(blocks):
        get_table[k].wait()
        at.found_f[...] += matmul(hits(k * block, block), at.table_v[k % 3])
        if k + 3 < blocks:
            get_table[k + 3] = table_block(k + 3)
        if k % 3 == 2:
            gather.pump(spacing)
    at.found_v[...] = at.found_f[...].astype(bf16).reshape(at.found_v.shape)
    at.arrived[me] = at.found_v[me]
    row_copy = lambda step, other: remote(
        at.found_v.at[other],
        at.arrived.at[me],
        at.row_send,
        at.row_recv,
        step - 1,
        place_of(other),
    )
    every_other(me, owners, lambda step, other: row_copy(step, other).start())
    gather.pump(spacing)

    get_memory.wait()
    put_kv = []
    tile = 256
    for part in range(2):
        ready(0, part)
        for start in range(part * model, (part + 1) * model, tile):
            columns = weight(at.kv2_v, start, tile)
            for row in range(0, memory_len, 512):
                at.kv_v[row:row + 512, start:start + tile] = matmul(
                    at.memory_v[row:row + 512, :], columns
                ).astype(bf16)
        lanes = pl.ds(part * model, model)
        put_kv.append(fetch(32 + part, at.kv_v.at[:, lanes], at.key_values.at[:, lanes]))
        gather.pump(spacing)

    every_other(me, owners, lambda step, other: row_copy(step, other).wait())
    embedded = matmul(at.pick[...], at.arrived[...].reshape(slots, model))
    at.embedded[...] = embedded
    put_kv.append(fetch(40, at.embedded, at.embedded_o))
    at.normed1[...] = rms_rounded(embedded, at.gains[0:1, :])
    for part in range(3):
        ready(1, part)
        for start in range(part * model, (part + 1) * model, tile):
            at.merged[:, start:start + tile] = matmul(
                at.normed1[...], weight(at.qkv_v, start, tile)
            ).astype(bf16)
    put_kv.append(fetch(41, at.merged, at.merged_o))
    row = lax.broadcasted_iota(jnp.int32, (length, both), 0)
    lane = lax.broadcasted_iota(jnp.int32, (length, both), 1)
    query_row = jnp.where(lane >= length, lane - length, lane)
    seen = (row <= query_row) & (at.keep[...] > 0.0)
    for pair in range(pairs):
        lanes = slice(pair * width, (pair + 1) * width)
        key_lanes = slice(model + pair * width, model + (pair + 1) * width)
        value_lanes = slice(2 * model + pair * width, 2 * model + (pair + 1) * width)
        query = spread_heads(at.merged[:, lanes], head_size)
        scores = back_product(at.merged[:, key_lanes], query) * scale
        bias = pltpu.roll(
            jnp.broadcast_to(at.bias_v[pair], scores.shape), 0, 1, stride=1, stride_axis=0
        )
        probs = column_softmax(jnp.where(seen, scores + bias, blocked)).astype(bf16)
        at.self_probs[pair] = probs
        turned = down_product(at.merged[:, value_lanes], probs)
        at.mixed1[:, lanes] = join_heads(turned, head_size).astype(bf16)
        if pair % 2 == 1:
            gather.pump(spacing)
    put_kv.append(fetch(42, at.self_probs, at.self_probs_o))
    ready(2, 0)
    for start in range(0, model, tile):
        at.after_self[:, start:start + tile] = at.embedded[:, start:start + tile] + matmul(
            at.mixed1[...], weight(at.out1_v, start, tile)
        )
    put_kv.append(fetch(43, at.after_self, at.after_self_o))
    at.normed2[...] = rms_rounded(at.after_self[...], at.gains[1:2, :])
    ready(3, 0)
    for start in range(0, model, tile):
        at.queries[:, start:start + tile] = matmul(
            at.normed2[...], weight(at.q2_v, start, tile)
        ).astype(bf16)
    tiles = memory_len // tile
    put_probs = {}
    for pair in range(pairs):
        lanes = slice(pair * width, (pair + 1) * width)
        value_lanes = slice(model + pair * width, model + (pair + 1) * width)
        query = spread_heads(at.queries[:, lanes], head_size)
        if pair >= 2:
            put_probs[pair - 2].wait()
        probs = at.p_v.at[pair % 2]

        def score(index, peak):
            place = pl.ds(pl.multiple_of(index * tile, tile), tile)
            part = back_product(at.kv_v[place, lanes], query) * scale
            at.s_v[place, :] = part
            return jnp.maximum(peak, jnp.max(part.reshape(tile // 8, 8, both), axis=0))

        peak = lax.fori_loop(0, tiles, score, jnp.full((8, both), blocked, f32))
        peak = jnp.max(peak, axis=0, keepdims=True)

        def power(index, total):
            place = pl.ds(pl.multiple_of(index * tile, tile), tile)
            part = jnp.exp(at.s_v[place, :] - peak)
            at.s_v[place, :] = part
            return total + jnp.sum(part.reshape(tile // 8, 8, both), axis=0)

        total = lax.fori_loop(0, tiles, power, jnp.zeros((8, both), f32))
        share = 1.0 / jnp.sum(total, axis=0, keepdims=True)

        def normal(index, unused):
            place = pl.ds(pl.multiple_of(index * tile, tile), tile)
            probs[place, :] = (at.s_v[place, :] * share).astype(bf16)
            return unused

        lax.fori_loop(0, tiles, normal, 0)
        put_probs[pair] = fetch(34 + pair, probs, at.cross_probs.at[pair])
        turned = down_product(at.kv_v[:, value_lanes], probs[...])
        at.mixed2[:, lanes] = join_heads(turned, head_size).astype(bf16)
        if pair % 2 == 1:
            gather.pump(spacing)
    ready(4, 0)
    for start in range(0, model, tile):
        at.after_cross[:, start:start + tile] = at.after_self[
            :, start:start + tile
        ] + matmul(at.mixed2[...], weight(at.out2_v, start, tile))
    at.normed3[...] = rms_rounded(at.after_cross[...], at.gains[2:3, :])
    gather.until(spacing, len(gather.chunks) - 1)
    gather.finish()
    for copy in put_kv + [put_probs[pairs - 2], put_probs[pairs - 1]]:
        copy.wait()


def forward_with_gather(inputs, shapes, room, head_size):
    length = inputs.keep.shape[0]
    memory_len, model = inputs.memory.shape
    owners = 32
    slots = owners * room
    pairs = model // (2 * head_size)
    both = 2 * length
    rows = model // owners
    struct = jax.ShapeDtypeStruct
    tokens = lambda columns, kind: struct((length, columns), kind)
    far_outs = [struct((4, 2, 2, 2) + shape, bf16) for shape in shapes] + [
        struct((memory_len, 2 * model), bf16),
        struct((pairs, memory_len, both), bf16),
        tokens(model, f32),
        tokens(3 * model, bf16),
        struct((pairs, length, both), bf16),
        tokens(model, f32),
    ]
    near_outs = [
        struct((8, slots), f32),
        tokens(slots, bf16),
        tokens(model, bf16),
        tokens(model, bf16),
        tokens(model, bf16),
        tokens(model, bf16),
        tokens(model, bf16),
        tokens(model, f32),
        tokens(model, bf16),
    ]
    by_owner = lambda columns: pltpu.VMEM((4, 2, 2, 2, rows, columns), bf16)
    own = [
        pltpu.VMEM((length, model), f32),
        pltpu.VMEM((length, 3 * model), bf16),
        pltpu.VMEM((pairs, length, both), bf16),
        pltpu.VMEM((length, model), f32),
        pltpu.VMEM((sum(flat.shape[0] for flat in inputs[:7]), 128), f32),
        pltpu.VMEM((pairs, 1, both), f32),
    ]
    own += [pltpu.VMEM(shape, bf16) for shape in shapes]
    own += [pltpu.VMEM((owners, room, 128), f32)] * 2
    own += [
        by_owner(2 * model),
        by_owner(3 * model),
        by_owner(model),
        by_owner(model),
        by_owner(model),
        pltpu.VMEM((memory_len, model), bf16),
        pltpu.VMEM((memory_len, 2 * model), bf16),
        pltpu.VMEM((3, 512, model), bf16),
        pltpu.VMEM((256, model), bf16),
        pltpu.VMEM((slots, model), f32),
        pltpu.VMEM((owners, room, model), bf16),
        pltpu.VMEM((owners, room, model), bf16),
        pltpu.VMEM((memory_len, both), f32),
        pltpu.VMEM((2, memory_len, both), bf16),
    ]
    dma = pltpu.SemaphoreType.DMA
    chunks = 14
    others = owners - 1
    sems = [dma((size,)) for size in (10 * chunks, 10 * chunks, chunks, 44) + (others,) * 4]
    far = pl.BlockSpec(memory_space=pl.ANY)
    near = pl.BlockSpec(memory_space=pltpu.VMEM)
    results = pl.pallas_call(
        functools.partial(forward_kernel, head_size, 2),
        out_shape=far_outs + near_outs,
        in_specs=[near] * (len(inputs) - 2) + [far] * 2,
        out_specs=[far] * len(far_outs) + [near] * len(near_outs),
        scratch_shapes=own + sems,
        compiler_params=pltpu.CompilerParams(
            collective_id=1, has_side_effects=True, vmem_limit_bytes=63 * 1024 * 1024
        ),
    )(*inputs)
    count = len(shapes)
    weights = Weights(*[whole.reshape(-1, whole.shape[-1]) for whole in results[:count]])
    return weights, ForwardOut(*results[count:])


class Sums:
    def __init__(self, send_sem, recv_sem, free_sem, spacing):
        self.z, self.x, self.y, self.core = standing()
        self.sets = flips(self.x, self.y, self.core)
        self.sibling_sets = flips(self.x, self.y, 1 - self.core)
        self.along_z, self.second, self.first, self.sibling = partners()
        self.send_sem, self.recv_sem, self.free_sem = send_sem, recv_sem, free_sem
        self.spacing = spacing
        self.chunks, self.flying, self.starts, self.clock, self.ready = [], {}, [], 0, 0

    def add(self, source, buffers, out, stride, offset, frees=None, needs=None):
        self.chunks.append((source, buffers, out, stride, offset, frees, needs))

    def copies(self, number, chunk):
        source, (kept, from_first, from_second, from_z) = self.chunks[chunk][:2]
        others = self.sibling_sets
        base = 10 * chunk
        go = lambda start, end, index, device: remote(
            start, end, self.send_sem, self.recv_sem, base + index, device
        )
        if number == 0:
            return [
                go(
                    source.at[:, others[k][0], others[k][1], 1 - self.core],
                    kept.at[k],
                    k,
                    self.sibling,
                )
                for k in range(4)
            ]
        if number == 1:
            return [go(kept.at[2 + k], from_first.at[k], 4 + k, self.first) for k in range(2)]
        if number == 2:
            return [go(kept.at[1], from_second, 6, self.second)]
        return [
            go(kept.at[0, (self.z + k + 1) % 4], from_z.at[k], 7 + k, self.along_z[k])
            for k in range(3)
        ]

    def begin(self, number, chunk):
        needs = self.chunks[chunk][6]
        if number == 0 and needs is not None:
            pl.semaphore_wait(self.free_sem.at[needs], 6)
        self.flying[number, chunk] = self.copies(number, chunk)
        for copy in self.flying[number, chunk]:
            copy.start()

    def settle(self, number, chunk):
        source, buffers, out, stride, offset, frees, unused = self.chunks[chunk]
        kept, from_first, from_second, from_z = buffers
        for copy in self.flying[number, chunk]:
            copy.wait_recv()
            if number == 0:
                copy.wait_send()
        if number == 0:
            for k in (2, 3, 1, 0):
                own = source.at[:, self.sets[k][0], self.sets[k][1], self.core]
                add_into(kept.at[k], own)
        elif number == 1:
            for k in (1, 0):
                add_into(kept.at[k], from_first.at[k])
        elif number == 2:
            add_into(kept.at[0], from_second)
        else:
            total = kept[0, self.z].astype(f32)
            for k in range(3):
                total = total + from_z[k].astype(f32)
            rows, width = total.shape
            for tile in range(width // 128):
                out[pl.ds(offset + tile, rows, stride), :] = total[:, tile * 128:(tile + 1) * 128]
            for stage in range(1, 4):
                for copy in self.flying[stage, chunk]:
                    copy.wait_send()
            if frees is not None:
                for device in self.along_z + [self.second, self.first, self.sibling]:
                    pl.semaphore_signal(
                        self.free_sem.at[frees], inc=1, device_id=device, device_id_type=mesh_ids
                    )

    def pump(self, steps=1):
        for unused in range(steps):
            for chunk, start in enumerate(self.starts):
                number, odd = divmod(self.clock - start, self.spacing)
                if odd == 0 and number <= 4:
                    self.settle(number - 1, chunk)
                    if number < 4:
                        self.begin(number, chunk)
            following = len(self.starts)
            if following < self.ready:
                self.begin(0, following)
                self.starts.append(self.clock)
            self.clock += 1

    def finish(self):
        self.ready = len(self.chunks)
        while (
            len(self.starts) < len(self.chunks)
            or self.clock <= self.starts[-1] + 4 * self.spacing
        ):
            self.pump()


def add_into(target, source):
    def quarter(index, unused):
        target[index] = (target[index].astype(f32) + source[index].astype(f32)).astype(bf16)
        return unused

    lax.fori_loop(0, 4, quarter, 0)


def norm_back(rows, gain, upstream):
    turn = lax.rsqrt(jnp.mean(rows * rows, axis=-1, keepdims=True) + epsilon)
    scaled = gain * upstream
    inner = jnp.sum(scaled * rows, axis=-1, keepdims=True) / rows.shape[1]
    gain_grad = jnp.sum(upstream * rows * turn, axis=0, keepdims=True)
    return turn * scaled - rows * (turn * turn * turn * inner), gain_grad


def share_into(target, left, right, tile, turned=None):
    depth, model = left.shape
    rows, width = target.shape[4], right.shape[1]
    half = model // 2
    if turned is not None:
        for start in range(0, depth, 256):
            turned[:, start:start + 256] = left[start:start + 256, :].T
    for part in range(2):
        mine = slice(part * half, (part + 1) * half)
        upright = left[:, mine].T if turned is None else None
        for start in range(0, width, tile):
            place = slice(start, start + tile)
            product = matmul(turned[mine, :] if upright is None else upright, right[:, place])
            target[2 * part:2 * part + 2, :, :, :, :, place] = product.astype(bf16).reshape(
                2, 2, 2, 2, rows, tile
            )


def gelu_parts(gate):
    slope, cubic = (2.0 / np.pi) ** 0.5, 0.044715
    curve = jnp.tanh(slope * (gate + cubic * gate * gate * gate))
    rise = 0.5 * (1.0 + curve)
    steep = 0.5 * gate * (1.0 - curve * curve) * (slope * (1.0 + 3.0 * cubic * gate * gate))
    return gate * rise, rise + steep


def fold_rows(scores):
    both = scores.shape[1]
    while scores.shape[0] % 16 == 0:
        rows = scores.shape[0] // 2
        scores = scores[:rows] + pltpu.roll(scores[rows:], both - rows, 1)
    total = scores[:8]
    for start in range(8, scores.shape[0], 8):
        total = total + pltpu.roll(scores[start:start + 8], both - start, 1)
    row = lax.broadcasted_iota(jnp.int32, total.shape, 0)
    for bit in (1, 2, 4):
        total = jnp.where((row // bit) % 2 == 1, pltpu.roll(total, both - bit, 1), total)
    return jnp.sum(total, axis=0, keepdims=True)


class BackwardIn(NamedTuple):
    key_values: object
    cross_probs: object
    memory: object
    w_q2: object
    w_out1: object
    w_qkv: object
    w_kv2: object
    w_gate: object
    w_upper: object
    w_out3: object
    w_out2: object
    after_self: object
    embedded: object
    merged: object
    self_probs: object
    normed1: object
    normed2: object
    mixed1: object
    queries: object
    mixed2: object
    normed3: object
    after_cross: object
    cotangent: object
    keep: object
    gains: object
    pick: object


class BackwardOut(NamedTuple):
    qkv: object
    out1: object
    q2: object
    kv2: object
    out2: object
    ffn: object
    out3: object
    hidden: object
    small: object
    returned: object
    memory_grad: object


class BackwardRefs(NamedTuple):
    key_values: object
    cross_probs: object
    memory: object
    w_q2: object
    w_out1: object
    w_qkv: object
    w_kv2: object
    w_gate: object
    w_upper: object
    w_out3: object
    w_out2: object
    after_self: object
    embedded: object
    merged: object
    self_probs: object
    normed1: object
    normed2: object
    mixed1: object
    queries: object
    mixed2: object
    normed3: object
    after_cross: object
    cotangent: object
    keep: object
    gains: object
    pick: object
    qkv: object
    out1: object
    q2: object
    kv2: object
    out2: object
    ffn: object
    out3: object
    hidden: object
    small: object
    returned: object
    memory_grad: object
    kv_v: object
    dkv_v: object
    p_v: object
    wq2_v: object
    wo1_v: object
    wqkv_v: object
    turn_v: object
    ds_v: object
    dq_v: object
    dqkv_v: object
    do_v: object
    gc_v: object
    rows_v: object
    slots_v: object
    s_kv: object
    s_pair: object
    s_qkv: object
    s_out3: object
    s_out2: object
    gate_v: object
    upper_v: object
    u_v: object
    dgu_v: object
    sp_v: object
    small_v: object
    small_in: object
    send: object
    recv: object
    free: object
    fetch: object
    small_send: object
    small_recv: object
    slot_send: object
    slot_recv: object


backward_far = 18


def backward_kernel(head_size, spacing, *refs):
    names = len(BackwardRefs._fields)
    at = BackwardRefs(*refs[:names])
    buffers = refs[names:]
    groups = [buffers[4 * k:4 * k + 4] for k in range(len(buffers) // 4)]
    scale = head_size ** (-0.5)
    width = 2 * head_size
    length, model = at.queries.shape
    memory_len = at.kv_v.shape[0]
    ffn = at.u_v.shape[1]
    half_ffn = ffn // 2
    pairs = model // width
    both = 2 * length
    tile = 256
    owners = 32
    me = lax.axis_index("wide") * 4 + lax.axis_index("narrow")
    place_of = lambda other: (other // 4, other % 4)
    waiting = []

    def fetch(source, target):
        copy = pltpu.make_async_copy(source, target, at.fetch.at[len(waiting)])
        waiting.append(copy)
        copy.start()
        return copy

    get_gate = [
        fetch(
            at.w_gate.at[:, pl.ds(part * half_ffn, half_ffn)],
            at.kv_v.at[pl.ds(part * model, model), pl.ds(0, half_ffn)],
        )
        for part in range(2)
    ]
    get_upper = [
        fetch(
            at.w_upper.at[:, pl.ds(part * half_ffn, half_ffn)],
            at.dkv_v.at[pl.ds(part * model, model), pl.ds(0, half_ffn)],
        )
        for part in range(2)
    ]
    pieces = [
        at.turn_v.at[:, pl.ds(0, model)],
        at.turn_v.at[:, pl.ds(model, model)],
        at.wq2_v.at[pl.ds(0, ffn - 2 * model), :],
    ]
    get_out3 = [
        fetch(at.w_out3.at[pl.ds(k * model, piece.shape[0]), :], piece)
        for k, piece in enumerate(pieces)
    ]
    get_out2 = fetch(at.w_out2, at.wqkv_v.at[:, pl.ds(0, model)])
    get_out1 = fetch(at.w_out1, at.wo1_v)
    get_self = fetch(at.self_probs, at.sp_v)

    barrier = pltpu.get_barrier_semaphore()
    every_other(
        me,
        owners,
        lambda step, other: pl.semaphore_signal(
            barrier, inc=1, device_id=place_of(other), device_id_type=mesh_ids
        ),
    )
    pl.semaphore_wait(barrier, owners - 1)

    sums = Sums(at.send, at.recv, at.free, spacing)
    model_tiles = model // 128
    half_tiles = half_ffn // 128
    half_model = model // 2

    def columns(ref, start, size):
        return ref.at[:, :, :, :, :, pl.ds(start, size)]

    def narrowed(group, size):
        lanes = pl.ds(0, size)
        return (
            group[0].at[:, :, :, lanes],
            group[1].at[:, :, :, lanes],
            group[2].at[:, :, lanes],
            group[3].at[:, :, lanes],
        )

    for part in range(2):
        sums.add(
            columns(at.s_out3, part * half_model, half_model),
            groups[part],
            at.out3,
            model_tiles,
            part * model_tiles // 2,
        )
    ffn_sources = (
        columns(at.s_qkv, 0, half_ffn),
        columns(at.s_qkv, half_ffn, half_ffn),
        columns(at.s_kv, 0, half_ffn),
        columns(at.s_pair, 0, half_ffn),
    )
    for k, source in enumerate(ffn_sources):
        sums.add(source, groups[2 + k], at.ffn, 4 * half_tiles, k * half_tiles, frees=k)
    sums.add(at.s_out2, groups[6], at.out2, model_tiles, 0, frees=4)
    for part in range(2):
        sums.add(
            columns(at.s_kv, part * model, model),
            groups[7 + part],
            at.kv2,
            2 * model_tiles,
            part * model_tiles,
        )
    sums.add(columns(at.s_pair, 0, model), groups[9], at.q2, model_tiles, 0)
    sums.add(
        columns(at.s_pair, model, model),
        narrowed(groups[2], model),
        at.out1,
        model_tiles,
        0,
        needs=0,
    )
    for part in range(2):
        sums.add(
            columns(at.s_qkv, part * model, model),
            narrowed(groups[3 + part], model),
            at.qkv,
            3 * model_tiles,
            part * model_tiles,
            needs=1 + part,
        )
    for part in range(2):
        sums.add(
            columns(at.s_qkv, 2 * model + part * half_model, half_model),
            narrowed(groups[5 + part], half_model),
            at.qkv,
            3 * model_tiles,
            2 * model_tiles + part * model_tiles // 2,
            needs=3 + part,
        )

    def half_of(ref, start):
        part, offset = divmod(start, half_ffn)
        return ref[part * model:(part + 1) * model, offset:offset + tile]

    for copy in get_gate + get_upper:
        copy.wait()
    for start in range(0, ffn, tile):
        lanes = slice(start, start + tile)
        gate = matmul(at.normed3[...], half_of(at.kv_v, start))
        upper = matmul(at.normed3[...], half_of(at.dkv_v, start))
        at.gate_v[:, lanes] = gate
        at.upper_v[:, lanes] = upper
        at.u_v[:, lanes] = (gelu_parts(gate)[0] * upper).astype(bf16)
    at.rows_v[...] = at.cotangent[...] * at.keep[...]
    at.do_v[...] = at.rows_v[...].astype(bf16)
    share_into(at.s_out3, at.u_v, at.do_v, tile)
    sums.ready = 2
    sums.pump(2)
    for copy in get_out3:
        copy.wait()
    for start in range(0, ffn, tile):
        lanes = slice(start, start + tile)
        piece, offset = divmod(start, model)
        grad = back_product(at.do_v[...], pieces[piece][offset:offset + tile, :])
        value, slope = gelu_parts(at.gate_v[:, lanes])
        at.dgu_v[:, lanes] = (grad * at.upper_v[:, lanes] * slope).astype(bf16)
        at.dgu_v[:, ffn + start:ffn + start + tile] = (grad * value).astype(bf16)
    sums.pump()
    share_into(
        columns(at.s_qkv, 0, ffn), at.normed3, at.dgu_v.at[:, pl.ds(0, ffn)], tile
    )
    sums.ready = 4
    sums.pump()
    for start in range(0, model, tile):
        lanes = slice(start, start + tile)
        total = at.after_cross[:, lanes]
        for k, piece in enumerate(pieces):
            total = total + matmul(
                at.u_v[:, k * model:k * model + piece.shape[0]], piece[:, lanes]
            )
        at.hidden[:, lanes] = total * at.keep[...]
    sums.pump()
    get_q2 = fetch(at.w_q2, at.wq2_v)
    get_normed2 = fetch(at.normed2, at.u_v.at[:, pl.ds(0, model)])
    get_after = fetch(at.after_self, at.gate_v.at[:, pl.ds(0, model)])
    get_embedded = fetch(at.embedded, at.upper_v.at[:, pl.ds(0, model)])
    upstream = jnp.zeros((length, model), f32)
    for k, ref in enumerate((at.kv_v, at.kv_v, at.dkv_v, at.dkv_v)):
        upstream = upstream + back_product(
            at.dgu_v[:, k * half_ffn:(k + 1) * half_ffn],
            ref[(k % 2) * model:(k % 2 + 1) * model, 0:half_ffn],
        )
    get_kv = fetch(at.key_values, at.kv_v)
    probs_at = lambda pair: fetch(at.cross_probs.at[pair], at.p_v.at[pair % 2])
    get_probs = {0: probs_at(0)}
    grad_rows, gain3 = norm_back(at.after_cross[...], at.gains[2:3, :], upstream)
    for part in range(6):
        at.small_v[12 + part:13 + part, :] = gain3[:, part * 128:(part + 1) * 128]
    at.rows_v[...] = at.rows_v[...] + grad_rows
    at.do_v[...] = at.rows_v[...].astype(bf16)
    get_out2.wait()
    at.gc_v[...] = back_product(at.do_v[...], at.wqkv_v[:, 0:model]).astype(bf16)
    get_qkv = fetch(at.w_qkv, at.wqkv_v)
    share_into(
        columns(at.s_kv, 0, half_ffn), at.normed3, at.dgu_v.at[:, pl.ds(ffn, half_ffn)], tile
    )
    sums.ready = 5
    sums.pump()
    share_into(
        columns(at.s_pair, 0, half_ffn),
        at.normed3,
        at.dgu_v.at[:, pl.ds(ffn + half_ffn, half_ffn)],
        tile,
    )
    get_merged = fetch(at.merged, at.dgu_v.at[:, pl.ds(0, 3 * model)])
    get_normed1 = fetch(at.normed1, at.dgu_v.at[:, pl.ds(3 * model, model)])
    get_mixed1 = fetch(at.mixed1, at.dgu_v.at[:, pl.ds(4 * model, model)])
    sums.ready = 6
    sums.pump()
    share_into(at.s_out2, at.mixed2, at.do_v, tile)
    sums.ready = 7
    sums.pump()

    get_kv.wait()
    tiles = memory_len // tile
    for pair in range(pairs):
        lanes = slice(pair * width, (pair + 1) * width)
        value_lanes = slice(model + pair * width, model + (pair + 1) * width)
        get_probs[pair].wait()
        if pair + 1 < pairs:
            get_probs[pair + 1] = probs_at(pair + 1)
        probs = at.p_v.at[pair % 2]
        grad = spread_heads(at.gc_v[:, lanes], head_size)
        query = spread_heads(at.queries[:, lanes], head_size)

        def first_pass(index, center):
            place = pl.ds(pl.multiple_of(index * tile, tile), tile)
            product = back_product(at.kv_v[place, value_lanes], grad)
            part = (product * probs[place, :].astype(f32)).reshape(tile // 8, 8, both)
            return center + jnp.sum(part, axis=0)

        center = lax.fori_loop(0, tiles, first_pass, jnp.zeros((8, both), f32))
        center = jnp.sum(center, axis=0, keepdims=True)

        def second_pass(index, unused):
            place = pl.ds(pl.multiple_of(index * tile, tile), tile)
            weights = probs[place, :]
            product = back_product(at.kv_v[place, value_lanes], grad)
            scores = (weights.astype(f32) * (product - center)).astype(bf16)
            at.dkv_v[place, value_lanes] = matmul(weights, grad).astype(bf16)
            at.dkv_v[place, lanes] = (matmul(scores, query) * scale).astype(bf16)
            at.ds_v[place, :] = scores
            return unused

        lax.fori_loop(0, tiles, second_pass, 0)
        turned = down_product(at.kv_v[:, lanes], at.ds_v[...])
        at.dq_v[:, lanes] = (join_heads(turned, head_size) * scale).astype(bf16)
        sums.pump()

    get_memory = fetch(at.memory, at.kv_v.at[:, pl.ds(0, model)])
    get_q2.wait()
    get_after.wait()
    upstream = back_product(at.dq_v[...], at.wq2_v[...])
    grad_rows, gain2 = norm_back(at.gate_v[:, 0:model], at.gains[1:2, :], upstream)
    at.rows_v[...] = at.rows_v[...] + grad_rows
    get_out1.wait()
    at.do_v[...] = at.rows_v[...].astype(bf16)
    at.gc_v[...] = back_product(at.do_v[...], at.wo1_v[...]).astype(bf16)
    sums.pump()
    get_memory.wait()
    share_into(
        at.s_kv, at.kv_v.at[:, pl.ds(0, model)], at.dkv_v, tile, at.turn_v
    )
    get_kv2 = fetch(at.w_kv2, at.turn_v)
    sums.ready = 9
    sums.pump()

    get_merged.wait()
    get_self.wait()
    for pair in range(pairs):
        lanes = slice(pair * width, (pair + 1) * width)
        key_lanes = slice(model + pair * width, model + (pair + 1) * width)
        value_lanes = slice(2 * model + pair * width, 2 * model + (pair + 1) * width)
        grad = spread_heads(at.gc_v[:, lanes], head_size)
        query = spread_heads(at.dgu_v[:, lanes], head_size)
        weights = at.sp_v[pair]
        wide = weights.astype(f32)
        product = back_product(at.dgu_v[:, value_lanes], grad)
        center = jnp.sum(product * wide, axis=0, keepdims=True)
        scores = (wide * (product - center)).astype(bf16)
        at.dqkv_v[:, value_lanes] = matmul(weights, grad).astype(bf16)
        at.dqkv_v[:, key_lanes] = (matmul(scores, query) * scale).astype(bf16)
        turned = down_product(at.dgu_v[:, key_lanes], scores)
        at.dqkv_v[:, lanes] = (join_heads(turned, head_size) * scale).astype(bf16)
        distance = fold_rows(scores.astype(f32))
        for part in range(3):
            at.small_v[18 + 3 * pair + part:19 + 3 * pair + part, :] = distance[
                :, part * 128:(part + 1) * 128
            ]
        if pair % 3 == 2:
            sums.pump()
    get_qkv.wait()
    get_embedded.wait()
    upstream = back_product(at.dqkv_v[...], at.wqkv_v[...])
    grad_rows, gain1 = norm_back(at.upper_v[:, 0:model], at.gains[0:1, :], upstream)
    row_grads = (at.rows_v[...] + grad_rows).astype(bf16)
    slots = down_product(at.pick[...], row_grads).astype(bf16)
    at.slots_v[...] = slots.reshape(at.slots_v.shape)
    at.returned[me] = at.slots_v[me]
    slot_copy = lambda step, other: remote(
        at.slots_v.at[other],
        at.returned.at[me],
        at.slot_send,
        at.slot_recv,
        step - 1,
        place_of(other),
    )
    every_other(me, owners, lambda step, other: slot_copy(step, other).start())
    for part in range(6):
        block = slice(part * 128, (part + 1) * 128)
        at.small_v[part:part + 1, :] = gain1[:, block]
        at.small_v[6 + part:7 + part, :] = gain2[:, block]
    at.small_v[36:40, :] = jnp.zeros((4, 128), f32)
    at.small[...] = at.small_v[...]
    get_normed2.wait()
    share_into(
        columns(at.s_pair, 0, model), at.u_v.at[:, pl.ds(0, model)], at.dq_v, tile
    )
    get_mixed1.wait()
    share_into(
        columns(at.s_pair, model, model),
        at.dgu_v.at[:, pl.ds(4 * model, model)],
        at.do_v,
        tile,
    )
    sums.ready = 11
    sums.pump()
    get_normed1.wait()
    share_into(at.s_qkv, at.dgu_v.at[:, pl.ds(3 * model, model)], at.dqkv_v, tile)
    sums.ready = 15
    sums.pump()

    get_kv2.wait()

    def memory_tile(index, unused):
        place = pl.ds(pl.multiple_of(index * tile, tile), tile)
        at.kv_v[place, model:] = back_product(at.dkv_v[place, :], at.turn_v[...]).astype(bf16)
        return unused

    lax.fori_loop(0, tiles, memory_tile, 0)
    put_memory = fetch(at.kv_v.at[:, pl.ds(model, model)], at.memory_grad)

    taken = 0
    for group in ([sums.sibling], [sums.first], [sums.second], sums.along_z):
        copies = [
            remote(
                at.small,
                at.small_in.at[taken + k],
                at.small_send,
                at.small_recv,
                taken + k,
                device,
            )
            for k, device in enumerate(group)
        ]
        for copy in copies:
            copy.start()
        sums.pump()
        for copy in copies:
            copy.wait()
        total = at.small[...]
        for k in range(len(group)):
            total = total + at.small_in[taken + k]
        at.small[...] = total
        taken += len(group)
    sums.finish()
    every_other(me, owners, lambda step, other: slot_copy(step, other).wait())
    put_memory.wait()


def backward_with_sums(inputs, head_size, slot_rows):
    length, model = inputs.queries.shape
    memory_len = inputs.memory.shape[0]
    owners = 32
    rows = model // owners
    pairs = model // (2 * head_size)
    both = 2 * length
    ffn = inputs.w_gate.shape[1]
    out3_rows = ffn // owners
    flat = lambda count, columns: jax.ShapeDtypeStruct((count * columns // 128, 128), f32)
    outs = BackwardOut(
        qkv=flat(rows, 3 * model),
        out1=flat(rows, model),
        q2=flat(rows, model),
        kv2=flat(rows, 2 * model),
        out2=flat(rows, model),
        ffn=flat(rows, 2 * ffn),
        out3=flat(out3_rows, model),
        hidden=jax.ShapeDtypeStruct((length, model), f32),
        small=jax.ShapeDtypeStruct((40, 128), f32),
        returned=jax.ShapeDtypeStruct((owners, slot_rows, model), bf16),
        memory_grad=jax.ShapeDtypeStruct((memory_len, model), bf16),
    )
    by_owner = lambda count, columns: pltpu.VMEM((4, 2, 2, 2, count, columns), bf16)
    own = [
        pltpu.VMEM((memory_len, 2 * model), bf16),
        pltpu.VMEM((memory_len, 2 * model), bf16),
        pltpu.VMEM((2, memory_len, both), bf16),
        pltpu.VMEM((model, model), bf16),
        pltpu.VMEM((model, model), bf16),
        pltpu.VMEM((model, 3 * model), bf16),
        pltpu.VMEM((model, memory_len), bf16),
        pltpu.VMEM((memory_len, both), bf16),
        pltpu.VMEM((length, model), bf16),
        pltpu.VMEM((length, 3 * model), bf16),
        pltpu.VMEM((length, model), bf16),
        pltpu.VMEM((length, model), bf16),
        pltpu.VMEM((length, model), f32),
        pltpu.VMEM((owners, slot_rows, model), bf16),
        by_owner(rows, 2 * model),
        by_owner(rows, 2 * model),
        by_owner(rows, 3 * model),
        by_owner(out3_rows, model),
        by_owner(rows, model),
        pltpu.VMEM((length, ffn), f32),
        pltpu.VMEM((length, ffn), f32),
        pltpu.VMEM((length, ffn), bf16),
        pltpu.VMEM((length, max(2 * ffn, 5 * model)), bf16),
        pltpu.VMEM((pairs, length, both), bf16),
        pltpu.VMEM((40, 128), f32),
        pltpu.VMEM((6, 40, 128), f32),
    ]
    chunks = 15
    dma = pltpu.SemaphoreType.DMA
    sems = [
        dma((10 * chunks,)),
        dma((10 * chunks,)),
        pltpu.SemaphoreType.REGULAR((5,)),
        dma((40,)),
        dma((6,)),
        dma((6,)),
        dma((owners - 1,)),
        dma((owners - 1,)),
    ]
    shapes = (
        [(out3_rows, model // 2)] * 2 + [(rows, ffn // 2)] * 4 + [(rows, model)] * 4
    )
    rooms = []
    for shape in shapes:
        for lead in ((4, 4), (2, 4), (4,), (3,)):
            rooms.append(pltpu.VMEM(lead + shape, bf16))
    far = pl.BlockSpec(memory_space=pl.ANY)
    near = pl.BlockSpec(memory_space=pltpu.VMEM)
    results = pl.pallas_call(
        functools.partial(backward_kernel, head_size, 3),
        out_shape=list(outs),
        in_specs=[far] * backward_far + [near] * (len(inputs) - backward_far),
        out_specs=[near] * (len(outs) - 1) + [far],
        scratch_shapes=own + sems + rooms,
        compiler_params=pltpu.CompilerParams(
            collective_id=2, has_side_effects=True, vmem_limit_bytes=63 * 1024 * 1024
        ),
    )(*inputs)
    return BackwardOut(*results)


def table_kernel(copies, ids_ref, rows_ref, *refs):
    if copies:
        small_ref, buckets_ref, refs = refs[0], refs[1], refs[2:]
    sources, out_ref, targets = refs[:copies], refs[copies], refs[copies + 1:2 * copies + 1]
    refs = refs[2 * copies + 1:]
    if copies:
        gains_ref, bias_ref, refs = refs[0], refs[1], refs[2:]
    rooms, sems = refs[:copies], refs[copies:]
    step = pl.program_id(0)

    def moves(inward):
        return [
            pltpu.make_async_copy(source, room, sems[0].at[k])
            if inward
            else pltpu.make_async_copy(room, target, sems[0].at[k])
            for k, (source, room, target) in enumerate(zip(sources, rooms, targets))
        ]

    if copies:

        @pl.when(step == 0)
        def enter():
            for copy in moves(True):
                copy.start()
            parts = gains_ref.shape[1] // 128
            for part in range(3 * parts):
                lanes = slice(part % parts * 128, (part % parts + 1) * 128)
                gains_ref[part // parts:part // parts + 1, lanes] = small_ref[part:part + 1, :]
            length = buckets_ref.shape[1]
            heads, count = bias_ref.shape
            hits = lax.broadcasted_iota(jnp.int32, (count, length), 0) == buckets_ref[...]
            diagonal = lax.broadcasted_iota(
                jnp.int32, (count, count), 0
            ) == lax.broadcasted_iota(jnp.int32, (count, count), 1)
            for head in range(heads):
                first = 3 * parts + head // 2 * 3
                pair = jnp.concatenate(
                    [small_ref[first + k:first + k + 1, :] for k in range(3)], axis=1
                )
                row = pair[:, head % 2 * length:(head % 2 + 1) * length]
                column = jnp.sum(jnp.where(hits, row, 0.0), axis=1, keepdims=True)
                bias_ref[head:head + 1, :] = jnp.sum(
                    jnp.where(diagonal, column, 0.0), axis=0, keepdims=True
                )

        @pl.when(step == 1)
        def turn():
            for copy in moves(True):
                copy.wait()
            for copy in moves(False):
                copy.start()

        @pl.when(step == pl.num_programs(0) - 1)
        def leave():
            for copy in moves(False):
                copy.wait()

    block = out_ref.shape[0]
    row = lax.broadcasted_iota(jnp.int32, (block, ids_ref.shape[1]), 0)
    wanted = ids_ref[0:1, :].astype(jnp.int32) - step * block
    hits = jnp.where(row == wanted, 1.0, 0.0).astype(bf16)
    out_ref[...] = matmul(hits, rows_ref[...])


def table_and_copies(requests, returned, shard_rows, copies, small=(), small_outs=()):
    slots, model = returned.shape
    block = min(2048, -(-shard_rows // 16) * 8)
    whole = lambda value: pl.BlockSpec(value.shape, lambda i: (0,) * value.ndim)
    far = pl.BlockSpec(memory_space=pltpu.HBM)
    results = pl.pallas_call(
        functools.partial(table_kernel, len(copies)),
        grid=(-(-shard_rows // block),),
        out_shape=[jax.ShapeDtypeStruct((shard_rows, model), f32)]
        + [jax.ShapeDtypeStruct(value.shape, value.dtype) for value in copies]
        + list(small_outs),
        in_specs=[whole(value) for value in (requests, returned, *small)] + [far] * len(copies),
        out_specs=[pl.BlockSpec((block, model), lambda i: (i, 0))]
        + [far] * len(copies)
        + [whole(value) for value in small_outs],
        scratch_shapes=[pltpu.VMEM(value.shape, value.dtype) for value in copies]
        + [pltpu.SemaphoreType.DMA((len(copies),))] * bool(copies),
        compiler_params=pltpu.CompilerParams(vmem_limit_bytes=63 * 1024 * 1024),
        cost_estimate=pl.CostEstimate(
            flops=2 * shard_rows * slots * model,
            bytes_accessed=4 * shard_rows * model,
            transcendentals=0,
        ),
    )(requests, returned, *small, *copies)
    return results[0], results[1:]


def body(
    target_ids,
    target_lengths,
    bucket_table,
    memory,
    table,
    self_qkv,
    self_out,
    cross_q,
    cross_kv,
    cross_out,
    ffn_in,
    ffn_out,
    gains,
    relative_bias,
    cotangent,
):
    pair_count, seq_len = target_ids.shape
    model_width = table.shape[1]
    bucket_count, head_count = relative_bias.shape
    head_size = model_width // head_count
    memory_len = memory.shape[1]
    wide_count = lax.axis_size("wide")
    narrow_count = lax.axis_size("narrow")
    owner_count = wide_count * narrow_count
    special = wide_count == 8 and narrow_count == 4
    ffn_width = ffn_out.shape[0] * owner_count // model_width
    token_count = pair_count * seq_len
    shard_rows = table.shape[0]
    capacity = max(2, (2 * token_count + owner_count - 1) // owner_count)
    room = -(-capacity // 16) * 16 if special else capacity
    slots = owner_count * room

    positions = jnp.arange(seq_len, dtype=jnp.int32)
    valid_flat = (positions[:, None] < target_lengths[0]).astype(f32)
    bucket_hits = (
        bucket_table[:, None] == jnp.arange(bucket_count, dtype=jnp.int32)[None, :]
    ).astype(f32)
    memory_rows = memory.reshape(memory_len, model_width)
    if special:
        main_rows = shard_rows // 16 * 16
        row_count = model_width // owner_count
        widths = (2 * model_width, 3 * model_width) + (model_width,) * 3 + (ffn_width,) * 2
        shapes = [(row_count, columns) for columns in widths]
        shapes.append((ffn_width // owner_count, model_width))
        weights, done = forward_with_gather(
            ForwardIn(
                flat_kv2=cross_kv.reshape(-1, 128),
                flat_qkv=self_qkv.reshape(-1, 128),
                flat_out1=self_out.reshape(-1, 128),
                flat_q2=cross_q.reshape(-1, 128),
                flat_out2=cross_out.reshape(-1, 128),
                flat_in=ffn_in.reshape(-1, 128),
                flat_out3=ffn_out.reshape(-1, 128),
                ids_row=target_ids.reshape(1, token_count),
                keep=valid_flat,
                buckets=bucket_table.reshape(1, seq_len),
                relative=relative_bias.T,
                gains=gains,
                tail=table[main_rows:],
                table=table,
                memory=memory_rows,
            ),
            shapes,
            room,
            head_size,
        )
        requests, slot_pick = done.wanted, done.pick
        w_kv2, w_qkv, w_out1, w_q2, w_out2, w_gate, w_upper, w_out3 = weights
        key_values, cross_probs = done.key_values, done.cross_probs
        embedded, self_normalized = done.embedded, done.normed1
        merged, self_probs, self_mixed = done.merged, done.self_probs, done.mixed1
        after_self, normed_cross = done.after_self, done.normed2
        cross_queries, cross_mixed = done.queries, done.mixed2
        after_cross, normed_ffn = done.after_cross, done.normed3
    else:
        flat_ids = target_ids.reshape(token_count)
        owner_index = flat_ids // shard_rows
        owner_hits = (owner_index[:, None] == jnp.arange(owner_count, dtype=jnp.int32)[None, :]).astype(
            jnp.int32
        )
        rank_within = jnp.sum(jnp.cumsum(owner_hits, axis=0) * owner_hits, axis=1) - 1
        slot_index = owner_index * room + rank_within
        slot_hits = slot_index[:, None] == jnp.arange(slots, dtype=jnp.int32)[None, :]
        outgoing = (
            jnp.sum(
                jnp.where(slot_hits, (flat_ids - owner_index * shard_rows + 1)[:, None], 0), axis=0
            )
            - 1
        )
        slot_pick = (slot_hits & (valid_flat > 0.0)).astype(bf16)
        shards = [
            cross_kv.reshape(-1, 2 * model_width),
            self_qkv.reshape(-1, 3 * model_width),
            self_out.reshape(-1, model_width),
            cross_q.reshape(-1, model_width),
            cross_out.reshape(-1, model_width),
            *jnp.split(ffn_in.reshape(-1, 2 * ffn_width), 2, axis=1),
            ffn_out.reshape(-1, model_width),
        ]
        w_kv2, w_qkv, w_out1, w_q2, w_out2, w_gate, w_upper, w_out3 = [
            lax.all_gather(shard, axes, axis=0, tiled=True) for shard in shards
        ]
        requests = lax.all_to_all(
            lax.all_to_all(
                outgoing.reshape(wide_count, narrow_count, room),
                "wide",
                split_axis=0,
                concat_axis=0,
                tiled=True,
            ),
            "narrow",
            split_axis=1,
            concat_axis=1,
            tiled=True,
        )
        found = table[jnp.maximum(requests, 0)]
        arrived = lax.all_to_all(
            lax.all_to_all(found, "wide", split_axis=0, concat_axis=0, tiled=True),
            "narrow",
            split_axis=1,
            concat_axis=1,
            tiled=True,
        ).reshape(slots, model_width)
        embedded = matmul(slot_pick, arrived)
        key_values = matmul(memory_rows, w_kv2).astype(bf16)
        self_normalized = rms_scaled(embedded, gains[0]).astype(bf16)
        merged = matmul(self_normalized, w_qkv).astype(bf16)
        bias_rows = jnp.dot(relative_bias.T, bucket_hits.T, precision=top_precision).reshape(
            head_count // 2, 1, 2 * seq_len
        )
        self_mixed, self_probs = self_forward(merged, bias_rows, valid_flat, head_size)
        after_self = embedded + matmul(self_mixed, w_out1)
        normed_cross = rms_scaled(after_self, gains[1]).astype(bf16)
        cross_queries = matmul(normed_cross, w_q2).astype(bf16)
        cross_mixed, cross_probs = cross_forward(cross_queries, key_values, head_size)
        after_cross = after_self + matmul(cross_mixed, w_out2)
        normed_ffn = rms_scaled(after_cross, gains[2]).astype(bf16)
    if special:
        sums = backward_with_sums(
            BackwardIn(
                key_values=key_values,
                cross_probs=cross_probs,
                memory=memory_rows,
                w_q2=w_q2,
                w_out1=w_out1,
                w_qkv=w_qkv,
                w_kv2=w_kv2,
                w_gate=w_gate,
                w_upper=w_upper,
                w_out3=w_out3,
                w_out2=w_out2,
                after_self=after_self,
                embedded=embedded,
                merged=merged,
                self_probs=self_probs,
                normed1=self_normalized,
                normed2=normed_cross,
                mixed1=self_mixed,
                queries=cross_queries,
                mixed2=cross_mixed,
                normed3=normed_ffn,
                after_cross=after_cross,
                cotangent=cotangent.reshape(token_count, model_width),
                keep=valid_flat,
                gains=gains,
                pick=slot_pick,
            ),
            head_size,
            room,
        )
        table_grad, copied = table_and_copies(
            requests,
            sums.returned.reshape(slots, model_width),
            shard_rows,
            [*sums[:8], sums.memory_grad],
            (sums.small, bucket_table.reshape(1, seq_len)),
            (
                jax.ShapeDtypeStruct((3, model_width), f32),
                jax.ShapeDtypeStruct((head_count, bucket_count), f32),
            ),
        )
        weight_sums = [value.reshape(-1) for value in copied[:7]]
        hidden, memory_grad, gain_sums, bias_sums = copied[7:]
        bias_sums = bias_sums.T
    else:
        gate, upper = matmul(normed_ffn, w_gate), matmul(normed_ffn, w_upper)
        activated = gated(gate, upper).astype(bf16)
        hidden = (after_cross + matmul(activated, w_out3)) * valid_flat

        upstream = cotangent.reshape(token_count, model_width) * valid_flat
        grad_branch3 = upstream.astype(bf16)
        share_out3 = outer_sum(activated, grad_branch3).astype(bf16)
        grad_act = back_product(grad_branch3, w_out3)
        unused, gate_pull = jax.vjp(gated, gate, upper)
        grad_gate, grad_upper = [part.astype(bf16) for part in gate_pull(grad_act)]
        share_gate = outer_sum(normed_ffn, grad_gate).astype(bf16)
        share_upper = outer_sum(normed_ffn, grad_upper).astype(bf16)
        grad_normed3 = back_product(grad_gate, w_gate) + back_product(grad_upper, w_upper)
        grad_cross_state, grad_gain3 = norm_backward(after_cross, gains[2], grad_normed3)
        grad_cross_state = grad_cross_state + upstream

        grad_branch2 = grad_cross_state.astype(bf16)
        share_out2 = outer_sum(cross_mixed, grad_branch2).astype(bf16)
        grad_cross_mixed = back_product(grad_branch2, w_out2).astype(bf16)
        grad_cross_q, grad_kv = cross_backward(
            cross_queries, key_values, cross_probs, grad_cross_mixed, head_size
        )
        grad_normed2 = back_product(grad_cross_q, w_q2)
        grad_self_state, grad_gain2 = norm_backward(after_self, gains[1], grad_normed2)
        grad_self_state = grad_self_state + grad_cross_state
        grad_branch1 = grad_self_state.astype(bf16)
        grad_self_mixed = back_product(grad_branch1, w_out1).astype(bf16)
        grad_joined, grad_distance = self_backward(merged, self_probs, grad_self_mixed, head_size)
        grad_first_normalized = back_product(grad_joined, w_qkv)
        grad_embedded, grad_gain1 = norm_backward(embedded, gains[0], grad_first_normalized)
        row_grads = (grad_embedded + grad_self_state).astype(bf16)
        slot_grads = outer_sum(slot_pick, row_grads).astype(bf16)
        returned = lax.all_to_all(
            lax.all_to_all(
                slot_grads.reshape(wide_count, narrow_count, room, model_width),
                "wide",
                split_axis=0,
                concat_axis=0,
                tiled=True,
            ),
            "narrow",
            split_axis=1,
            concat_axis=1,
            tiled=True,
        ).reshape(slots, model_width)
        table_grad, unused = table_and_copies(
            requests.reshape(1, slots), returned, shard_rows, []
        )
        memory_grad = back_product(grad_kv, w_kv2).astype(bf16)
        shares = (
            outer_sum(self_normalized, grad_joined).astype(bf16),
            outer_sum(self_mixed, grad_branch1).astype(bf16),
            outer_sum(normed_cross, grad_cross_q).astype(bf16),
            outer_sum(memory_rows, grad_kv).astype(bf16),
            share_out2,
            jnp.concatenate([share_gate, share_upper], axis=1),
            share_out3,
        )
        weight_sums = [
            lax.psum_scatter(share, axes, scatter_dimension=0, tiled=True)
            .astype(f32)
            .reshape(-1)
            for share in shares
        ]
        gain_sums, distance_sums = lax.psum(
            (jnp.stack([grad_gain1, grad_gain2, grad_gain3]), grad_distance.reshape(-1)), axes
        )
        bias_sums = jnp.dot(
            bucket_hits.T, distance_sums.reshape(head_count, seq_len).T, precision=top_precision
        )
    return (
        hidden.reshape(pair_count, seq_len, model_width),
        memory_grad.reshape(pair_count, memory_len, model_width),
        table_grad,
        *weight_sums,
        gain_sums,
        bias_sums,
    )


def solution(mesh):
    split = P(axes)
    return jax.shard_map(
        body,
        mesh=mesh,
        in_specs=(
            P(axes, None),
            split,
            P(),
            P(axes, None, None),
            P(axes, None),
            split,
            split,
            split,
            split,
            split,
            split,
            split,
            P(),
            P(),
            P(axes, None, None),
        ),
        out_specs=(
            P(axes, None, None),
            P(axes, None, None),
            P(axes, None),
            split,
            split,
            split,
            split,
            split,
            split,
            split,
            P(),
            P(),
        ),
        check_vma=False,
    )
```
